32 devices in a mesh: row: 16 (over z, x, core), seq: 2 (over y).
Axes of the slice: x: 2, y: 2, z: 4, core: 2. Of those that a mesh axis runs over, the one named last changes fastest.
Arguments:
- tokens: bfloat16 [32, 2048, 768], P('row', 'seq'), may hold values from -6 to 6
- segments: int32 [32, 2048], P('row'), may hold values from 0 to 3, as said below
- w_qkv: float32 [768, 2304], P(('row', 'seq')), may hold values from -0.21875 to 0.21875
- w_out: float32 [768, 768], P(('row', 'seq')), may hold values from -3.5 to 3.5
- w_up: float32 [768, 3072], P(('row', 'seq')), may hold values from -0.21875 to 0.21875
- w_down: float32 [3072, 768], P(('row', 'seq')), may hold values from -0.109375 to 0.109375
- gain_attn: float32 [768], P(('row', 'seq')), may hold values from 0.25 to 1.75
- gain_mlp: float32 [768], P(('row', 'seq')), may hold values from 0.25 to 1.75
- cotangent: bfloat16 [32, 2048, 768], P('row', 'seq'), may hold values from -6 to 6
Outputs:
- output: bfloat16 [32, 2048, 768], P('row', 'seq')
- d_tokens: float32 [32, 2048, 768], P('row', 'seq')
- grad_qkv: float32 [768, 2304], P(('row', 'seq'))
- grad_out: float32 [768, 768], P(('row', 'seq'))
- grad_up: float32 [768, 3072], P(('row', 'seq'))
- grad_down: float32 [3072, 768], P(('row', 'seq'))
- grad_gain_attn: float32 [768], P(('row', 'seq'))
- grad_gain_mlp: float32 [768], P(('row', 'seq'))
The draws below stay inside these ranges and needn't reach their ends.
Inputs may be any that keep to these rules, and one draw needn't show every extreme that they name: `segments`: segment ids never fall along a row. Among the 2 rows at each index of row, at least one is a single segment.
All inputs are finite; a program needn't handle non-finite values.
Results may differ from the reference program's by a relative error of at most 0.017.
Values may be sent and summed in bfloat16 or wider, within the bound.
No kernel may reach another device: no remote copies, remote signals or barrier semaphores. Data moves between devices by JAX's collectives and lax.ppermute only.
A program may use at most 1 GiB of HBM per device.

```python
import math
import jax
import jax.numpy as jnp
from jax import lax

D = 768
H = 12
HD = 64
FF = 3072
ROW_LEN = 2048
ROWS_DEV = 2
ROWS = 32


def draw_segments(key, part):
    cut_key = jax.random.fold_in(key, 101)
    split_key = jax.random.fold_in(key, 202)
    whole_key = jax.random.fold_in(key, 303)
    cut_points = jax.random.randint(cut_key, (ROWS, 3), 1, ROW_LEN)
    is_split = jax.random.randint(split_key, (ROWS,), 0, 2)
    whole_row = jax.random.randint(whole_key, (ROWS // ROWS_DEV,), 0, ROWS_DEV)
    row_slot = jnp.arange(ROWS, dtype=jnp.int32) % ROWS_DEV
    chosen_slot = jnp.repeat(whole_row, ROWS_DEV, total_repeat_length=ROWS)
    is_split = jnp.where(row_slot == (chosen_slot + 1) % ROWS_DEV, 1, is_split)
    is_split = jnp.where(row_slot == chosen_slot, 0, is_split)
    positions = jnp.arange(ROW_LEN, dtype=jnp.int32)
    passed_cuts = (cut_points[:, :, None] <= positions[None, None, :]).astype(jnp.int32)
    segment_ids = jnp.sum(passed_cuts, axis=1) * is_split[:, None]
    return segment_ids.astype(jnp.int32)


def spiked(result, stream_key, source, target, blocks, factor):
    def block_of(dim):
        return (jnp.arange(result.shape[dim]) // (result.shape[dim] // blocks)).reshape((-1,) + (1,) * (result.ndim - 1 - dim))

    one_side = jax.random.permutation(stream_key, blocks)[block_of(target)]
    second = (block_of(target) + blocks // 2) % blocks
    return jnp.where((block_of(source) == one_side) | (block_of(source) == second), factor * result, result)


def shard_levels(own_key, shape, split, low, high):
    level = 1.0
    for dim, parts in split:
        draws = jax.random.uniform(jax.random.fold_in(jax.random.fold_in(own_key, 6), dim), (parts,), jnp.float32, low / len(split), high / len(split))
        level = level * jnp.repeat(jnp.exp(draws), shape[dim] // parts).reshape((-1,) + (1,) * (len(shape) - 1 - dim))
    return level


def scatter_about(rng, extent, scale, reach, split=(), kind=jnp.bfloat16):
    entries = scale * jax.random.normal(rng, extent, jnp.float32)
    if split:
        entries = entries * shard_levels(rng, extent, split, -0.22, 0.18)
    return jnp.clip(entries, -reach, reach).astype(kind)


def noise_with(stream_key, shape, scale, most, shards, heavy, kind=jnp.bfloat16):
    drawn = scale * jax.random.normal(stream_key, shape, jnp.float32)
    if shards:
        drawn = drawn * shard_levels(stream_key, shape, shards, -0.22, 0.18)
    return jnp.clip(spiked(drawn, jax.random.fold_in(stream_key, 3), *heavy), -most, most).astype(kind)


def setup_inputs(seed: int = 0) -> dict:
    key_list = jax.random.split(jax.random.key(seed), 10)
    tokens = noise_with(key_list[0], (ROWS, ROW_LEN, D), 1.0, 6.0, ((0, 16), (1, 2)), (0, 2, 16, 2.0))
    segments = draw_segments(jax.random.fold_in(key_list[9], 71), 0)
    w_qkv = scatter_about(key_list[2], (D, 3 * D), D ** -0.5, 0.21875, ((0, 32),), jnp.float32)
    w_out = scatter_about(key_list[3], (D, D), (max(2, D // 256)) ** -0.5, 3.5, ((0, 32),), jnp.float32)
    w_up = scatter_about(key_list[4], (D, FF), D ** -0.5, 0.21875, ((0, 32),), jnp.float32)
    w_down = scatter_about(key_list[5], (FF, D), FF ** -0.5, 0.109375, ((0, 32),), jnp.float32)
    gain_attn = jnp.clip(1.0 + 0.15 * jax.random.normal(key_list[6], (D,), jnp.float32), 0.25, 1.75)
    gain_mlp = jnp.clip(1.0 + 0.15 * jax.random.normal(key_list[7], (D,), jnp.float32), 0.25, 1.75)
    cotangent = scatter_about(key_list[8], (ROWS, ROW_LEN, D), 1.0, 6.0, ((0, 16), (1, 2)))
    return dict(tokens=tokens, segments=segments, w_qkv=w_qkv, w_out=w_out, w_up=w_up, w_down=w_down, gain_attn=gain_attn, gain_mlp=gain_mlp, cotangent=cotangent)


EPSILON = 1e-05
MASKED = -1e+30
HIGHEST = lax.Precision.HIGHEST

@jax.custom_vjp
def low(v):
    return lax.optimization_barrier(v.astype(jnp.bfloat16)).astype(jnp.float32)

@jax.custom_vjp
def low_back(v):
    return v

def low_keep(v):
    return (low(v), None)

def low_pass(kept, grad):
    return (grad,)

def back_keep(v):
    return (v, None)

def back_low(kept, grad):
    return (low(grad),)
low.defvjp(low_keep, low_pass)
low_back.defvjp(back_keep, back_low)

def layer_norm(values, scaling):
    mean_value = lax.optimization_barrier(jnp.mean(values, axis=-1, keepdims=True))
    shifted = values - mean_value
    spread = lax.optimization_barrier(jnp.mean(shifted * shifted, axis=-1, keepdims=True))
    return shifted * lax.rsqrt(spread + EPSILON) * scaling

def product(left, right):
    return jnp.dot(left, right, precision=HIGHEST)

def attend(packed, row_segments):
    row_tokens = packed.shape[0]
    queries = packed[:, :D].reshape(row_tokens, H, HD)
    key_heads = packed[:, D:2 * D].reshape(row_tokens, H, HD)
    value_heads = packed[:, 2 * D:].reshape(row_tokens, H, HD)
    scores = jnp.einsum('qhd,khd->hqk', queries, key_heads, precision=HIGHEST) * (1.0 / math.sqrt(HD))
    scores = low_back(scores)
    positions = jnp.arange(row_tokens, dtype=jnp.int32)
    same_doc = row_segments[:, None] == row_segments[None, :]
    attend_mask = same_doc & (positions[None, :] <= positions[:, None])
    select_mask = same_doc & (positions[None, :] < positions[:, None])
    offset = math.log(ROW_LEN / 2.0) + 0.5
    chosen = jnp.where(select_mask, jax.nn.softplus(scores[0] - offset), 0.0)
    penalty = jnp.cumsum(chosen, axis=0) - chosen
    logits = jnp.where(attend_mask[None], scores - penalty[None], MASKED)
    row_max = lax.optimization_barrier(jnp.max(logits, axis=-1, keepdims=True))
    log_norm = row_max + jnp.log(lax.optimization_barrier(jnp.sum(jnp.exp(logits - row_max), axis=-1, keepdims=True)))
    attention = jnp.exp(logits - log_norm)
    mixed = jnp.einsum('hqk,khd->qhd', low(attention), value_heads, precision=HIGHEST)
    return mixed.reshape(row_tokens, D)

def row_layer(row_input, row_segments, weights):
    w_attn, w_proj, w_expand, w_reduce, scale_attn, scale_mlp = weights
    normed = low(layer_norm(row_input, scale_attn))
    packed = low_back(low(product(normed, w_attn)))
    mixed = low_back(low(attend(packed, row_segments)))
    branch = low_back(product(mixed, w_proj))
    middle = row_input + branch
    normed_mlp = low(layer_norm(middle, scale_mlp))
    hidden = low_back(product(normed_mlp, w_expand))
    active = low(jax.nn.gelu(hidden, approximate=False))
    return middle + product(active, w_reduce)

def reference(tokens, segments, w_qkv, w_out, w_up, w_down, gain_attn, gain_mlp, cotangent):

    def forward(inputs, weight_qkv, weight_out, weight_up, weight_down, scale_attn, scale_mlp):
        rounded = (low(weight_qkv), low(weight_out), low(weight_up), low(weight_down), low(scale_attn), low(scale_mlp))

        def one_row(row_item):
            return row_layer(row_item[0], row_item[1], rounded)
        return lax.map(jax.checkpoint(one_row), (inputs, segments))
    output, pullback = jax.vjp(forward, tokens.astype(jnp.float32), w_qkv, w_out, w_up, w_down, gain_attn, gain_mlp)
    gradients = pullback(cotangent.astype(jnp.float32))
    return (output.astype(jnp.bfloat16), gradients[0], gradients[1], gradients[2], gradients[3], gradients[4], gradients[5], gradients[6])
```

```python
from functools import partial
import math

import jax
import jax.numpy as jnp
from jax import lax
from jax.experimental import pallas as pl
from jax.experimental.pallas import tpu as pltpu
from jax.sharding import PartitionSpec as P

H = 12
HD = 64
ROW_LEN = 2048
EPSILON = 1e-05
MASKED = -1e30
BIG = 1e30
LOG2E = 1.4426950408889634
OFFSET = math.log(ROW_LEN / 2.0) + 0.5
SAFE = 64.0
B = 256
BT = 512
MIB = 2**20
F32 = jnp.float32
BF = jnp.bfloat16


def dot(a, b):
    return jnp.dot(a, b, preferred_element_type=F32)


def dot_nt(a, b):
    return lax.dot_general(a, b, (((1,), (1,)), ((), ())), preferred_element_type=F32)


def dot_tn(a, b):
    return lax.dot_general(a, b, (((0,), (0,)), ((), ())), preferred_element_type=F32)


def iota(shape, dim):
    return lax.broadcasted_iota(jnp.int32, shape, dim)


def half_lanes(rows):
    return iota((rows, 128), 1) < HD


def pick_columns(c):
    return (iota((512, 128), 0) == 4 * iota((512, 128), 1) + c).astype(F32).astype(BF)


def pick_rows(piece, c):
    return (iota((piece, 4 * piece), 1) == 4 * iota((piece, 4 * piece), 0) + c).astype(F32).astype(BF)


def pack_kernel(qkv_ref, out_ref, up_ref, down_ref, ga_ref, gm_ref, o_ref):
    piece, features = out_ref.shape
    lane = iota((piece, 128), 1)
    col = 3 * features
    o_ref[:, :col] = qkv_ref[...].astype(BF)
    o_ref[:, col : col + features] = out_ref[...].astype(BF)
    col += features
    for c in range(4):
        pick = pick_columns(c)
        for tile in range(features // 128):
            part = up_ref[:, 512 * tile : 512 * tile + 512].astype(BF)
            o_ref[:, col + 128 * tile : col + 128 * tile + 128] = dot(part, pick).astype(BF)
        col += features
    for c in range(4):
        o_ref[:, col : col + features] = dot(pick_rows(piece, c), down_ref[...].astype(BF)).astype(BF)
        col += features
    gains = jnp.where(lane == 0, ga_ref[...], jnp.where(lane == 1, gm_ref[...], 0.0))
    o_ref[:, col : col + 128] = gains.astype(BF)


def pack(w_qkv, w_out, w_up, w_down, gain_attn, gain_mlp):
    piece, features = w_out.shape
    return pl.pallas_call(
        pack_kernel,
        out_shape=jax.ShapeDtypeStruct((piece, 12 * features + 128), BF),
        name="pack_weights",
    )(w_qkv, w_out, w_up, w_down, gain_attn[:, None], gain_mlp[:, None])


def unpack_kernel(b_ref, out_ref, up_ref, down_ref):
    piece, features = out_ref.shape
    out_ref[...] = b_ref[:, :features].astype(F32)
    for tile in range(features // 128):
        total = None
        for c in range(4):
            col = features * (1 + c) + 128 * tile
            part = dot_nt(b_ref[:, col : col + 128], pick_columns(c))
            total = part if total is None else total + part
        up_ref[:, 512 * tile : 512 * tile + 512] = total
    total = None
    for c in range(4):
        col = features * (5 + c)
        part = dot_tn(pick_rows(piece, c), b_ref[:, col : col + features])
        total = part if total is None else total + part
    down_ref[...] = total


def unpack(buffer):
    piece = buffer.shape[0]
    features = (buffer.shape[1] - 128) // 9
    return pl.pallas_call(
        unpack_kernel,
        out_shape=(
            jax.ShapeDtypeStruct((piece, features), F32),
            jax.ShapeDtypeStruct((piece, 4 * features), F32),
            jax.ShapeDtypeStruct((4 * piece, features), F32),
        ),
        name="unpack_gradients",
    )(buffer)


def moments(values):
    mean_value = jnp.mean(values, axis=-1, keepdims=True)
    shifted = values - mean_value
    spread = jnp.mean(shifted * shifted, axis=-1, keepdims=True)
    return shifted, lax.rsqrt(spread + EPSILON)


def qkv_kernel(x_ref, gain_ref, wq_ref, wk_ref, wv_ref, q_ref, k_ref, v_ref, qt_ref, rows_ref, size_ref):
    features = x_ref.shape[1]

    @pl.when(pl.program_id(0) == 0)
    def _():
        rows_ref[...] = gain_ref[...].astype(F32).T[:8]
        size_ref[...] = jnp.zeros_like(size_ref)

    shifted, scale = moments(x_ref[...].astype(F32))
    normed = (shifted * scale * rows_ref[0:1, :]).astype(BF)
    low = half_lanes(x_ref.shape[0])
    heads = (iota((features, 128), 0) // HD == iota((features, 128), 1)).astype(F32).astype(BF)

    def spread(ref, packed, other):
        for p in range(H // 2):
            pair = packed[:, 128 * p : 128 * p + 128]
            ref[:, 256 * p : 256 * p + 128] = jnp.where(low, pair, other).astype(BF)
            ref[:, 256 * p + 128 : 256 * p + 256] = jnp.where(low, other, pair).astype(BF)

    q = dot(normed, wq_ref[...]) * (LOG2E / math.sqrt(HD))
    qt_ref[...] = q.astype(BF).T
    spread(q_ref, q, 0.0)
    size_ref[0:1] = jnp.maximum(size_ref[0:1], jnp.max(dot((q * q).astype(BF), heads), axis=0, keepdims=True))
    k = dot(normed, wk_ref[...])
    spread(k_ref, k, 1.0)
    size_ref[1:2] = jnp.maximum(size_ref[1:2], jnp.max(dot((k * k).astype(BF), heads), axis=0, keepdims=True))
    spread(v_ref, dot(normed, wv_ref[...]), 1.0)


def project_qkv(x, weights):
    tokens, features = x.shape
    last = weights.shape[1] // 128 - 1

    def column(i):
        return pl.BlockSpec((features, features), lambda t: (0, i))

    def tall(cols):
        return pl.BlockSpec((BT, cols), lambda t: (t, 0))

    return pl.pallas_call(
        qkv_kernel,
        grid=(tokens // BT,),
        in_specs=[
            tall(features),
            pl.BlockSpec((features, 128), lambda t: (0, last)),
            column(0),
            column(1),
            column(2),
        ],
        out_specs=[
            tall(2 * features),
            tall(2 * features),
            tall(2 * features),
            pl.BlockSpec((features, BT), lambda t: (0, t)),
            pl.BlockSpec((8, features), lambda t: (0, 0)),
            pl.BlockSpec((8, 128), lambda t: (0, 0)),
        ],
        out_shape=[
            jax.ShapeDtypeStruct((tokens, 2 * features), BF),
            jax.ShapeDtypeStruct((tokens, 2 * features), BF),
            jax.ShapeDtypeStruct((tokens, 2 * features), BF),
            jax.ShapeDtypeStruct((features, tokens), BF),
            jax.ShapeDtypeStruct((8, features), F32),
            jax.ShapeDtypeStruct((8, 128), F32),
        ],
        compiler_params=pltpu.CompilerParams(vmem_limit_bytes=48 * MIB),
        name="project_qkv",
    )(x, weights, weights, weights, weights)


def selection(scores, segq, segk, ib, jb):
    rows = iota((B, B), 0) + ib * B
    cols = iota((B, B), 1) + jb * B
    same = segq == segk
    x = scores - OFFSET * LOG2E
    soft = jnp.maximum(x, 0.0) + jnp.log2(1.0 + jnp.exp2(-jnp.abs(x)))
    return jnp.where(same & (cols < rows), soft, 0.0), same & (cols <= rows)


def two_part(tri, values):
    high = values.astype(BF)
    rest = (values - high.astype(F32)).astype(BF)
    return dot(tri, high) + dot(tri, rest)


def forward_kernel(tab, q_ref, k_ref, v_ref, segq_ref, segk_ref, k_any, seg_any, o_ref, li_ref, e_ref,
                   acc, carry, tri, qx, kbuf, segbuf, sem):
    t = pl.program_id(0)
    ib, jb = tab[3, t], tab[4, t]

    @pl.when(t == 0)
    def _():
        carry[...] = jnp.zeros_like(carry)
        tri[...] = (iota((B, B), 1) < iota((B, B), 0)).astype(F32).astype(BF)

    @pl.when(jb == 0)
    def _():
        acc[...] = jnp.zeros_like(acc)
        qx[...] = q_ref[...]

        @pl.when(tab[6, t] != 0)
        def _():
            lane = iota((B, 128), 1)

            def step(other, top):
                base = tab[1, t + other]
                copies = (
                    pltpu.make_async_copy(k_any.at[pl.ds(pl.multiple_of(base * B, B), B), :], kbuf, sem.at[0]),
                    pltpu.make_async_copy(seg_any.at[base], segbuf, sem.at[1]),
                )
                for copy in copies:
                    copy.start()
                for copy in copies:
                    copy.wait()
                first = dot_nt(q_ref[:, 0:128], kbuf[:, 0:128])
                chosen, kept = selection(first, segq_ref[...], segbuf[0:1, :], ib, other)
                penalty = jnp.where(kept, two_part(tri[...], chosen) + carry[other, 0:1, :], BIG)
                for h in range(H):
                    w = slice(128 * h, 128 * h + 128)
                    z = dot_nt(q_ref[:, w], kbuf[:, w]) - penalty
                    top = jnp.where(lane == h, jnp.maximum(top, jnp.max(z, axis=1, keepdims=True)), top)
                return top

            top = lax.fori_loop(0, ib + 1, step, jnp.full((B, 128), -BIG, F32))
            for h in range(H):
                shift = -jnp.sum(jnp.where(lane == h, top, 0.0), axis=1, keepdims=True)
                one = shift.astype(BF).astype(F32)
                two = (shift - one).astype(BF).astype(F32)
                three = shift - one - two
                at = lane - (HD if h % 2 == 0 else 0)
                extra = jnp.where(at == 0, one, jnp.where(at == 1, two, jnp.where(at == 2, three, 0.0)))
                w = slice(128 * h, 128 * h + 128)
                keep = (lane < HD) if h % 2 == 0 else (lane >= HD)
                qx[:, w] = jnp.where(keep, q_ref[:, w].astype(F32), extra).astype(BF)

    @pl.when(tab[2, t] != 0)
    def _():
        first = dot_nt(q_ref[:, 0:128], k_ref[:, 0:128])
        chosen, kept = selection(first, segq_ref[...], segk_ref[0, 0:1, :], ib, jb)
        penalty = jnp.where(kept, two_part(tri[...], chosen) + carry[jb, 0:1, :], BIG)
        carry[jb, 0:1, :] = carry[jb, 0:1, :] + jnp.sum(chosen, axis=0, keepdims=True)
        for h in range(H):
            w = slice(128 * h, 128 * h + 128)
            e = jnp.exp2(dot_nt(qx[:, w], k_ref[:, w]) - penalty).astype(BF)
            e_ref[0, h] = e
            acc[:, w] += dot(e, v_ref[:, w])

    @pl.when(jb == ib)
    def _():
        low = half_lanes(B)
        for p in range(H // 2):
            one = acc[:, 256 * p : 256 * p + 128]
            two = acc[:, 256 * p + 128 : 256 * p + 256]
            inverse = 1.0 / pltpu.roll(jnp.where(low, two, one), HD, 1)
            o_ref[:, 128 * p : 128 * p + 128] = (jnp.where(low, one, two) * inverse).astype(BF)
            li_ref[:, 128 * p : 128 * p + 128] = inverse


def attention_forward(table, q, k, v, seg_col, seg_row):
    tokens = q.shape[0]
    blocks = tokens // B
    tiles = table.shape[1]
    wide = 128 * H
    narrow = HD * H
    return pl.pallas_call(
        forward_kernel,
        grid_spec=pltpu.PrefetchScalarGridSpec(
            num_scalar_prefetch=1,
            grid=(tiles,),
            in_specs=[
                pl.BlockSpec((B, wide), lambda t, tab: (tab[0, t], 0)),
                pl.BlockSpec((B, wide), lambda t, tab: (tab[1, t], 0)),
                pl.BlockSpec((B, wide), lambda t, tab: (tab[1, t], 0)),
                pl.BlockSpec((B, 1), lambda t, tab: (tab[0, t], 0)),
                pl.BlockSpec((1, 8, B), lambda t, tab: (tab[1, t], 0, 0)),
                pl.BlockSpec(memory_space=pl.ANY),
                pl.BlockSpec(memory_space=pl.ANY),
            ],
            out_specs=[
                pl.BlockSpec((B, narrow), lambda t, tab: (tab[0, t], 0)),
                pl.BlockSpec((B, narrow), lambda t, tab: (tab[0, t], 0)),
                pl.BlockSpec((1, H, B, B), lambda t, tab: (tab[5, t], 0, 0, 0)),
            ],
            scratch_shapes=[
                pltpu.VMEM((B, wide), F32),
                pltpu.VMEM((blocks, 8, B), F32),
                pltpu.VMEM((B, B), BF),
                pltpu.VMEM((B, wide), BF),
                pltpu.VMEM((B, wide), BF),
                pltpu.VMEM((8, B), jnp.int32),
                pltpu.SemaphoreType.DMA((2,)),
            ],
        ),
        out_shape=[
            jax.ShapeDtypeStruct((tokens, narrow), BF),
            jax.ShapeDtypeStruct((tokens, narrow), F32),
            jax.ShapeDtypeStruct((tiles, H, B, B), BF),
        ],
        compiler_params=pltpu.CompilerParams(vmem_limit_bytes=56 * MIB),
        name="attention_forward",
    )(table, q, k, v, seg_col, seg_row, k, seg_row)


def backward_kernel(tab, e_ref, q_ref, k_ref, v_ref, d_ref, qt_ref, dt_ref, segq_ref, segk_ref, o_ref,
                    dq, dkt, dvt, carry, tri):
    t = pl.program_id(0)
    ib, jb = tab[3, t], tab[4, t]
    narrow = HD * H

    @pl.when(t == 0)
    def _():
        carry[...] = jnp.zeros_like(carry)
        tri[...] = (iota((B, B), 1) > iota((B, B), 0)).astype(F32).astype(BF)
        dkt[...] = jnp.zeros_like(dkt)
        dvt[...] = jnp.zeros_like(dvt)

    @pl.when(jb == 0)
    def _():
        dq[...] = jnp.zeros_like(dq)

    @pl.when(tab[2, t] != 0)
    def _():
        low = half_lanes(B)
        cols = pl.ds(pl.multiple_of(jb * B, B), B)
        total = None
        parts = {}
        for h in list(range(1, H)) + [0]:
            w = slice(128 * h, 128 * h + 128)
            own = slice(HD * h, HD * h + HD)
            e = e_ref[0, h]
            dz = e.astype(F32) * dot_nt(d_ref[:, w], v_ref[:, w])
            total = dz if total is None else total + dz
            dvt[own, cols] += dot(dt_ref[own, :], e)
            if h == 0:
                gate = jax.nn.sigmoid(dot_nt(q_ref[:, w], k_ref[:, w]) * (1.0 / LOG2E) - OFFSET)
                rows = iota((B, B), 0) + ib * B
                keys = iota((B, B), 1) + jb * B
                kept = (segq_ref[...] == segk_ref[0, 0:1, :]) & (keys < rows)
                later = carry[jb, 0:1, :] + two_part(tri[...], total)
                carry[jb, 0:1, :] = carry[jb, 0:1, :] + jnp.sum(total, axis=0, keepdims=True)
                dz = dz - jnp.where(kept, later * gate, 0.0)
            ds = dz.astype(BF)
            dkt[own, cols] += dot(qt_ref[own, :], ds)
            parts[h] = dot(ds, k_ref[:, w])
            if h ^ 1 in parts:
                p = h // 2
                dq[:, 128 * p : 128 * p + 128] += jnp.where(low, parts[2 * p], parts[2 * p + 1])

    @pl.when(jb == ib)
    def _():
        cols = pl.ds(pl.multiple_of(ib * B, B), B)
        o_ref[:, :narrow] = (dq[...] * (1.0 / math.sqrt(HD))).astype(BF)
        o_ref[:, narrow : 2 * narrow] = (dkt[:, cols] * (1.0 / LOG2E)).astype(BF).T
        o_ref[:, 2 * narrow :] = dvt[:, cols].astype(BF).T


def attention_backward(table, e, q, k, v, d, qt, dt, seg_col, seg_row):
    tokens = q.shape[0]
    blocks = tokens // B
    tiles = table.shape[1]
    wide = 128 * H
    narrow = HD * H
    return pl.pallas_call(
        backward_kernel,
        grid_spec=pltpu.PrefetchScalarGridSpec(
            num_scalar_prefetch=1,
            grid=(tiles,),
            in_specs=[
                pl.BlockSpec((1, H, B, B), lambda t, tab: (tab[5, t], 0, 0, 0)),
                pl.BlockSpec((B, wide), lambda t, tab: (tab[0, t], 0)),
                pl.BlockSpec((B, wide), lambda t, tab: (tab[1, t], 0)),
                pl.BlockSpec((B, wide), lambda t, tab: (tab[1, t], 0)),
                pl.BlockSpec((B, wide), lambda t, tab: (tab[0, t], 0)),
                pl.BlockSpec((narrow, B), lambda t, tab: (0, tab[0, t])),
                pl.BlockSpec((narrow, B), lambda t, tab: (0, tab[0, t])),
                pl.BlockSpec((B, 1), lambda t, tab: (tab[0, t], 0)),
                pl.BlockSpec((1, 8, B), lambda t, tab: (tab[1, t], 0, 0)),
            ],
            out_specs=pl.BlockSpec((B, 3 * narrow), lambda t, tab: (tab[0, t], 0)),
            scratch_shapes=[
                pltpu.VMEM((B, narrow), F32),
                pltpu.VMEM((narrow, tokens), F32),
                pltpu.VMEM((narrow, tokens), F32),
                pltpu.VMEM((blocks, 8, B), F32),
                pltpu.VMEM((B, B), BF),
            ],
        ),
        out_shape=jax.ShapeDtypeStruct((tokens, 3 * narrow), BF),
        compiler_params=pltpu.CompilerParams(vmem_limit_bytes=60 * MIB),
        name="attention_backward",
    )(table, e, q, k, v, d, qt, dt, seg_col, seg_row)


def tile_tables(segments, first, slow):
    blocks = segments.shape[0] // B
    ib = jnp.array([i for i in range(blocks) for j in range(i + 1)], jnp.int32)
    jb = jnp.array([j for i in range(blocks) for j in range(i + 1)], jnp.int32)
    back_ib = jnp.array([i for i in reversed(range(blocks)) for j in range(i + 1)], jnp.int32)
    back_jb = jnp.array([j for i in reversed(range(blocks)) for j in range(i + 1)], jnp.int32)
    heads = segments[::B]
    tails = segments[B - 1 :: B]
    touch = (heads[:, None] <= tails[None, :]).astype(jnp.int32)
    shift = first * (blocks // 2)

    def table(rows, keys):
        active = touch[rows, keys]
        return jnp.stack(
            [
                (rows + shift) % blocks,
                (keys + shift) % blocks,
                active,
                rows,
                keys,
                rows * (rows + 1) // 2 + keys,
                jnp.broadcast_to(slow, rows.shape),
            ]
        )

    return table(ib, jb), table(back_ib, back_jb)


def mlp_kernel(x_ref, ob_ref, dy_ref, li_ref, gain_ref, wo_ref, wu_ref, wd_ref, out_ref, dx_ref, d_ref, dt_ref, g_any,
               xh, scales, y, dn, n2, gup, gdown, gout, gsum, stage, sem):
    c, t = pl.program_id(0), pl.program_id(1)
    chunks, steps = pl.num_programs(0), pl.num_programs(1)
    rows = pl.ds(pl.multiple_of(t * BT, BT), BT)
    features = x_ref.shape[1]

    def send(slot, column):
        start = pl.multiple_of(column, 128)
        return pltpu.make_async_copy(stage.at[slot], g_any.at[:, pl.ds(start, features)], sem.at[slot])

    @pl.when(c == 0)
    def _():
        middle = x_ref[...].astype(F32) + dot(ob_ref[...], wo_ref[...])
        shifted, scale = moments(middle)
        xh[rows, :] = (shifted * scale).astype(BF)
        scales[rows, :] = jnp.broadcast_to(scale, (BT, 128))
        y[rows, :] = middle
        dn[rows, :] = jnp.zeros_like(middle)
        n2[rows, :] = (shifted * scale * gain_ref[1:2, :]).astype(BF)

    @pl.when(t == 0)
    def _():
        gup[...] = jnp.zeros_like(gup)
        gdown[...] = jnp.zeros_like(gdown)

    @pl.when((c == 0) & (t == 0))
    def _():
        gout[...] = jnp.zeros_like(gout)
        gsum[...] = jnp.zeros_like(gsum)

    n2_low = n2[rows, :]
    dy_low = dy_ref[...]
    u = dot(n2_low, wu_ref[...])
    da = dot_nt(dy_low, wd_ref[...])
    cdf = 0.5 * (1.0 + lax.erf(u * math.sqrt(0.5)))
    density = jnp.exp(-0.5 * u * u) * (1.0 / math.sqrt(2.0 * math.pi))
    active = (u * cdf).astype(BF)
    du = ((cdf + u * density) * da).astype(BF)
    y[rows, :] += dot(active, wd_ref[...])
    gdown[...] += dot_tn(active, dy_low)
    gup[...] += dot_tn(n2_low, du)
    dn[rows, :] += dot_nt(du, wu_ref[...])

    @pl.when(t == steps - 1)
    def _():
        @pl.when(c > 0)
        def _():
            send(0, c * features).wait()
            send(1, (c + chunks) * features).wait()

        stage[0] = gup[...].astype(BF)
        stage[1] = gdown[...].astype(BF)
        send(0, (1 + c) * features).start()
        send(1, (1 + c + chunks) * features).start()

    @pl.when(c == chunks - 1)
    def _():
        out_ref[...] = y[rows, :].astype(BF)
        d_normed = dn[rows, :]
        scale = scales[rows, 0:1]
        unit = xh[rows, :].astype(F32)
        product = d_normed * unit
        gsum[...] += jnp.sum(product.reshape(BT // 8, 8, features), axis=0)
        inner = d_normed * gain_ref[1:2, :]
        dx = dy_low.astype(F32) + scale * (
            inner - jnp.mean(inner, axis=-1, keepdims=True) - unit * jnp.mean(inner * unit, axis=-1, keepdims=True)
        )
        dx_ref[...] = dx
        db = dx.astype(BF)
        gout[...] += dot_tn(ob_ref[...], db)
        scaled = dot_nt(db, wo_ref[...]) * li_ref[...]
        dt_ref[...] = scaled.astype(BF).T
        low = half_lanes(BT)
        lane = iota((BT, 128), 1)
        swap_row, swap_col = iota((128, 128), 0), iota((128, 128), 1)
        swap = ((swap_row // HD != swap_col // HD) & (swap_col % HD < 2)).astype(F32).astype(BF)
        for p in range(H // 2):
            w = slice(128 * p, 128 * p + 128)
            pair = scaled[:, w]
            both = pair * ob_ref[:, w].astype(F32)
            high = both.astype(BF)
            delta = dot(high, swap) + dot((both - high.astype(F32)).astype(BF), swap)
            top = delta.astype(BF).astype(F32)
            extra = jnp.where((lane == 0) | (lane == HD), -top, top - delta)
            d_ref[:, 256 * p : 256 * p + 128] = jnp.where(low, pair, extra).astype(BF)
            d_ref[:, 256 * p + 128 : 256 * p + 256] = jnp.where(low, extra, pair).astype(BF)

    @pl.when((c == chunks - 1) & (t == steps - 1))
    def _():
        stage[2] = gout[...].astype(BF)
        column = jnp.broadcast_to(jnp.sum(gsum[...], axis=0, keepdims=True), (128, features))
        stage[3, :, :128] = column.T.astype(BF)
        last = pltpu.make_async_copy(
            stage.at[3, :, pl.ds(0, 128)], g_any.at[:, pl.ds((1 + 2 * 4) * features, 128)], sem.at[3]
        )
        send(2, 0).start()
        last.start()
        send(0, chunks * features).wait()
        send(1, 2 * chunks * features).wait()
        send(2, 0).wait()
        last.wait()


def feed_forward(x, ob, dy, li, gains, weights):
    tokens, features = x.shape
    steps = tokens // BT
    chunks = 4

    def ends(c, t):
        return (jnp.where((c == 0) | (c == chunks - 1), t, steps - 1), 0)

    def at_first(c, t):
        return (jnp.where(c == 0, t, steps - 1), 0)

    def at_last(c, t):
        return (jnp.where(c == chunks - 1, t, 0), 0)

    block = (BT, features)
    once = pl.Buffered(1)
    return pl.pallas_call(
        mlp_kernel,
        grid=(chunks, steps),
        in_specs=[
            pl.BlockSpec(block, at_first, pipeline_mode=once),
            pl.BlockSpec(block, ends),
            pl.BlockSpec(block, lambda c, t: (t, 0)),
            pl.BlockSpec(block, at_last, pipeline_mode=once),
            pl.BlockSpec((8, features), lambda c, t: (0, 0)),
            pl.BlockSpec((features, features), lambda c, t: (0, 3), pipeline_mode=once),
            pl.BlockSpec((features, features), lambda c, t: (0, 4 + c)),
            pl.BlockSpec((features, features), lambda c, t: (0, 8 + c)),
        ],
        out_specs=[
            pl.BlockSpec(block, at_last),
            pl.BlockSpec(block, at_last),
            pl.BlockSpec((BT, 2 * features), at_last),
            pl.BlockSpec((features, BT), lambda c, t: (0, at_last(c, t)[0])),
            pl.BlockSpec(memory_space=pl.ANY),
        ],
        out_shape=[
            jax.ShapeDtypeStruct((tokens, features), BF),
            jax.ShapeDtypeStruct((tokens, features), F32),
            jax.ShapeDtypeStruct((tokens, 2 * features), BF),
            jax.ShapeDtypeStruct((features, tokens), BF),
            jax.ShapeDtypeStruct((features, 9 * features + 128), BF),
        ],
        scratch_shapes=[
            pltpu.VMEM((tokens, features), BF),
            pltpu.VMEM((tokens, 128), F32),
            pltpu.VMEM((tokens, features), F32),
            pltpu.VMEM((tokens, features), F32),
            pltpu.VMEM((tokens, features), BF),
            pltpu.VMEM((features, features), F32),
            pltpu.VMEM((features, features), F32),
            pltpu.VMEM((features, features), F32),
            pltpu.VMEM((8, features), F32),
            pltpu.VMEM((4, features, features), BF),
            pltpu.SemaphoreType.DMA((4,)),
        ],
        compiler_params=pltpu.CompilerParams(vmem_limit_bytes=63 * MIB),
        name="feed_forward",
    )(x, ob, dy, li, gains, weights, weights, weights)


def first_kernel(x_ref, dqkv_ref, dx_ref, gain_ref, wq_ref, wk_ref, wv_ref, out_ref, low_ref, g_ref, acc, gsum):
    t = pl.program_id(0)
    features = x_ref.shape[1]

    @pl.when(t == 0)
    def _():
        acc[...] = jnp.zeros_like(acc)
        gsum[...] = jnp.zeros_like(gsum)

    shifted, scale = moments(x_ref[...].astype(F32))
    xh = shifted * scale
    gain = gain_ref[0:1, :]
    normed = (xh * gain).astype(BF)
    acc[...] += dot_tn(normed, dqkv_ref[...])
    d_normed = (
        dot_nt(dqkv_ref[:, :features], wq_ref[...])
        + dot_nt(dqkv_ref[:, features : 2 * features], wk_ref[...])
        + dot_nt(dqkv_ref[:, 2 * features :], wv_ref[...])
    )
    gsum[...] += jnp.sum((d_normed * xh).reshape(BT // 8, 8, features), axis=0)
    inner = d_normed * gain
    dx = dx_ref[...] + scale * (
        inner - jnp.mean(inner, axis=-1, keepdims=True) - xh * jnp.mean(inner * xh, axis=-1, keepdims=True)
    )
    out_ref[...] = dx
    low_ref[...] = dx.astype(BF)

    @pl.when(t == pl.num_programs(0) - 1)
    def _():
        g_ref[:, : 3 * features] = acc[...].astype(BF)
        column = jnp.broadcast_to(jnp.sum(gsum[...], axis=0, keepdims=True), (128, features))
        g_ref[:, 3 * features :] = column.T.astype(BF)


def first_gradients(x, dqkv, dx, gains, weights):
    tokens, features = x.shape

    def tall(cols):
        return pl.BlockSpec((BT, cols), lambda t: (t, 0))

    def column(i):
        return pl.BlockSpec((features, features), lambda t: (0, i))

    return pl.pallas_call(
        first_kernel,
        grid=(tokens // BT,),
        in_specs=[
            tall(features),
            tall(3 * features),
            tall(features),
            pl.BlockSpec((8, features), lambda t: (0, 0)),
            column(0),
            column(1),
            column(2),
        ],
        out_specs=[
            tall(features),
            tall(features),
            pl.BlockSpec((features, 3 * features + 128), lambda t: (0, 0)),
        ],
        out_shape=[
            jax.ShapeDtypeStruct((tokens, features), F32),
            jax.ShapeDtypeStruct((tokens, features), BF),
            jax.ShapeDtypeStruct((features, 3 * features + 128), BF),
        ],
        scratch_shapes=[pltpu.VMEM((features, 3 * features), F32), pltpu.VMEM((8, features), F32)],
        compiler_params=pltpu.CompilerParams(vmem_limit_bytes=60 * MIB),
        name="first_gradients",
    )(x, dqkv, dx, gains, weights, weights, weights)


def swap(value):
    return lax.ppermute(value, "seq", [(0, 1), (1, 0)])


def own_and_other(pair, position):
    return (
        lax.dynamic_index_in_dim(pair, position, 0, keepdims=False),
        lax.dynamic_index_in_dim(pair, 1 - position, 0, keepdims=False),
    )


def in_order(own, other, position):
    return jnp.where(position == 0, jnp.stack([own, other]), jnp.stack([other, own]))


def row_body(tokens, segments, w_qkv, w_out, w_up, w_down, gain_attn, gain_mlp, cotangent):
    both = ("row", "seq")
    position = lax.axis_index("seq")
    _, half, features = tokens.shape
    own, other = own_and_other(tokens, position)
    x = jnp.concatenate([own, swap(other)])
    packed = pack(w_qkv, w_out, w_up, w_down, gain_attn, gain_mlp)
    weights = lax.all_gather(packed, both, axis=0, tiled=True)
    own, other = own_and_other(cotangent, position)
    dy = jnp.concatenate([own, swap(other)])
    row_segments = lax.dynamic_index_in_dim(segments, position, 0, keepdims=False)
    stored = jnp.roll(row_segments, position * half)
    seg_col = stored[:, None]
    seg_row = jnp.broadcast_to(stored.reshape(-1, 1, B), (stored.shape[0] // B, 8, B))
    q, k, v, qt, gains, sizes = project_qkv(x, weights)
    slow = jnp.any(sizes[0] * sizes[1] * 1.05 > SAFE * SAFE).astype(jnp.int32)
    table, back_table = tile_tables(row_segments, position, slow)
    ob, li, e = attention_forward(table, q, k, v, seg_col, seg_row)
    output, dx, d, dt, g_later = feed_forward(x, ob, dy, li, gains, weights)
    r_later = lax.psum_scatter(g_later, both, scatter_dimension=0, tiled=True)
    output = in_order(output[:half], swap(output[half:]), position)
    dqkv = attention_backward(back_table, e, q, k, v, d, qt, dt, seg_col, seg_row)
    d_tokens, d_low, g_first = first_gradients(x, dqkv, dx, gains, weights)
    g_first, r_later = lax.optimization_barrier((g_first, r_later))
    r_first = lax.psum_scatter(g_first, both, scatter_dimension=0, tiled=True)
    d_tokens = in_order(d_tokens[:half], swap(d_low[half:]).astype(F32), position)
    g_out, g_up, g_down = unpack(r_later)
    return (
        output,
        d_tokens,
        r_first[:, : 3 * features].astype(F32),
        g_out,
        g_up,
        g_down,
        r_first[:, 3 * features].astype(F32),
        r_later[:, 9 * features].astype(F32),
    )


def from_behind(value, axis, steps):
    count = lax.axis_size(axis)
    first, last = (max(0, -steps), min(count, count - steps))
    return lax.ppermute(value, axis, [(source, source + steps) for source in range(first, last)])


def layer_norm(values, scaling):
    mean_value = jnp.mean(values, axis=-1, keepdims=True)
    shifted = values - mean_value
    spread = jnp.mean(shifted * shifted, axis=-1, keepdims=True)
    return shifted * lax.rsqrt(spread + EPSILON) * scaling


def running_sums(values):
    places = jnp.arange(values.shape[1], dtype=jnp.int32)
    upto = (places[None, :] <= places[:, None]).astype(jnp.float32)
    return jnp.einsum("im,rmj->rij", upto, values, precision=lax.Precision.HIGHEST)


def block_masks(segments, position, source, block_len):
    offsets = jnp.arange(block_len, dtype=jnp.int32)
    query_pos = position * block_len + offsets
    key_pos = source * block_len + offsets
    query_start = position * block_len
    key_start = jnp.maximum(source, 0) * block_len
    query_seg = lax.dynamic_slice_in_dim(segments, query_start, block_len, 1)
    key_seg = lax.dynamic_slice_in_dim(segments, key_start, block_len, 1)
    same_doc = (query_seg[:, :, None] == key_seg[:, None, :]) & (source >= 0)
    earlier = key_pos[None, :] < query_pos[:, None]
    reached = key_pos[None, :] <= query_pos[:, None]
    return (same_doc & reached[None], same_doc & earlier[None])


def block_logits(queries, key_heads, carried, segments, position, source, offset):
    block_len = queries.shape[1]
    scores = jnp.einsum(
        "rqhd,rkhd->rhqk", queries, key_heads, preferred_element_type=jnp.float32
    ) * (1.0 / math.sqrt(HD))
    attend_mask, select_mask = block_masks(segments, position, source, block_len)
    chosen = jnp.where(select_mask, jax.nn.softplus(scores[:, 0] - offset), 0.0)
    running = running_sums(chosen)
    penalty = carried[:, None, :] + running - chosen
    logits = jnp.where(attend_mask[:, None], scores - penalty[:, None], MASKED)
    return (scores, logits, attend_mask, select_mask, carried + running[:, -1])


def ring_body(tokens, segments, w_qkv, w_out, w_up, w_down, gain_attn, gain_mlp, cotangent):
    low_pieces = (
        w_qkv.astype(jnp.bfloat16),
        w_out.astype(jnp.bfloat16),
        w_up.astype(jnp.bfloat16),
        w_down.astype(jnp.bfloat16),
        gain_attn.astype(jnp.bfloat16),
        gain_mlp.astype(jnp.bfloat16),
    )
    gathered = (
        lax.all_gather(low_pieces[0], ("row", "seq"), axis=0, tiled=True),
        lax.all_gather(low_pieces[1], ("row", "seq"), axis=0, tiled=True),
        lax.all_gather(low_pieces[2], ("row", "seq"), axis=0, tiled=True),
        lax.all_gather(low_pieces[3], ("row", "seq"), axis=0, tiled=True),
        lax.all_gather(low_pieces[4], ("row", "seq"), axis=0, tiled=True),
        lax.all_gather(low_pieces[5], ("row", "seq"), axis=0, tiled=True),
    )
    qkv_full, out_full, up_full, down_full, attn_scale, mlp_scale = gathered
    row_count, block_len, features = tokens.shape
    token_count = row_count * block_len
    position = lax.axis_index("seq")
    sections = lax.axis_size("seq")
    offset = math.log(ROW_LEN / 2.0) + 0.5
    inputs = tokens.astype(jnp.float32).reshape(token_count, features)
    normed, attn_norm_back = jax.vjp(layer_norm, inputs, attn_scale.astype(jnp.float32))
    normed_low = normed.astype(jnp.bfloat16)
    packed = jnp.dot(normed_low, qkv_full, preferred_element_type=jnp.float32).astype(jnp.bfloat16)
    packed = packed.reshape(row_count, block_len, 3 * features)
    queries = packed[:, :, :features].reshape(row_count, block_len, H, HD)
    key_value = packed[:, :, features:]
    carried = jnp.zeros((row_count, block_len), jnp.float32)
    running_max = jnp.full((row_count, H, block_len), MASKED, jnp.float32)
    running_sum = jnp.zeros((row_count, H, block_len), jnp.float32)
    accumulated = jnp.zeros((row_count, block_len, H, HD), jnp.float32)
    kept_pairs = []
    kept_sums = []
    for section in range(sections):
        source = position - section
        key_heads = key_value[:, :, :features].reshape(row_count, block_len, H, HD)
        value_heads = key_value[:, :, features:].reshape(row_count, block_len, H, HD)
        scores, logits, attend_mask, select_mask, passed = block_logits(
            queries, key_heads, carried, segments, position, source, offset
        )
        kept_pairs.append(key_value)
        kept_sums.append(carried)
        new_max = jnp.maximum(running_max, jnp.max(logits, axis=-1))
        rescale = jnp.exp(running_max - new_max)
        exp_scores = jnp.where(attend_mask[:, None], jnp.exp(logits - new_max[..., None]), 0.0)
        running_sum = running_sum * rescale + jnp.sum(exp_scores, axis=-1)
        accumulated = accumulated * jnp.transpose(rescale, (0, 2, 1))[..., None] + jnp.einsum(
            "rhqk,rkhd->rqhd",
            exp_scores.astype(jnp.bfloat16),
            value_heads,
            preferred_element_type=jnp.float32,
        )
        running_max = new_max
        if section + 1 < sections:
            key_value = from_behind(key_value, "seq", 1)
            carried = from_behind(passed, "seq", 1)
    log_norm = running_max + jnp.log(running_sum)
    attn_heads = accumulated / jnp.transpose(running_sum, (0, 2, 1))[..., None]
    mixed_low = attn_heads.reshape(token_count, features).astype(jnp.bfloat16)
    branch = jnp.dot(mixed_low, out_full, preferred_element_type=jnp.float32)
    middle = inputs + branch
    normed_mlp, mlp_norm_back = jax.vjp(layer_norm, middle, mlp_scale.astype(jnp.float32))
    normed_mlp_low = normed_mlp.astype(jnp.bfloat16)
    hidden = jnp.dot(normed_mlp_low, up_full, preferred_element_type=jnp.float32)
    active, gelu_back = jax.vjp(partial(jax.nn.gelu, approximate=False), hidden)
    active_low = active.astype(jnp.bfloat16)
    output = (middle + jnp.dot(active_low, down_full, preferred_element_type=jnp.float32)).astype(
        jnp.bfloat16
    )
    output = output.reshape(row_count, block_len, features)
    upstream = cotangent.reshape(token_count, features)
    grad_down = jnp.dot(active_low.T, upstream, preferred_element_type=jnp.float32)
    d_active = jnp.dot(upstream, down_full.T, preferred_element_type=jnp.float32)
    d_hidden = gelu_back(d_active)[0].astype(jnp.bfloat16)
    grad_up = jnp.dot(normed_mlp_low.T, d_hidden, preferred_element_type=jnp.float32)
    d_normed_mlp = jnp.dot(d_hidden, up_full.T, preferred_element_type=jnp.float32)
    d_middle_part, grad_mlp_gain = mlp_norm_back(d_normed_mlp)
    d_middle = upstream.astype(jnp.float32) + d_middle_part
    d_branch = d_middle.astype(jnp.bfloat16)
    grad_out = jnp.dot(mixed_low.T, d_branch, preferred_element_type=jnp.float32)
    d_mixed = jnp.dot(d_branch, out_full.T, preferred_element_type=jnp.float32).astype(jnp.bfloat16)
    d_mixed = d_mixed.reshape(row_count, block_len, H, HD)
    correction = jnp.transpose(
        jnp.sum(d_mixed.astype(jnp.float32) * attn_heads, axis=-1), (0, 2, 1)
    )
    score_scale = 1.0 / math.sqrt(HD)
    grads_pair = jnp.zeros((row_count, block_len, 2 * features), jnp.float32)
    grads_column = jnp.zeros((row_count, block_len), jnp.float32)
    grad_query = jnp.zeros((row_count, block_len, H, HD), jnp.float32)
    for section in reversed(range(sections)):
        source = position - section
        key_value = kept_pairs[section]
        key_heads = key_value[:, :, :features].reshape(row_count, block_len, H, HD)
        value_heads = key_value[:, :, features:].reshape(row_count, block_len, H, HD)
        scores, logits, attend_mask, select_mask, unused = block_logits(
            queries, key_heads, kept_sums[section], segments, position, source, offset
        )
        attention = jnp.where(attend_mask[:, None], jnp.exp(logits - log_norm[..., None]), 0.0)
        attention_low = attention.astype(jnp.bfloat16)
        grad_values = jnp.einsum(
            "rhqk,rqhd->rkhd", attention_low, d_mixed, preferred_element_type=jnp.float32
        )
        grad_attention = jnp.einsum(
            "rqhd,rkhd->rhqk", d_mixed, value_heads, preferred_element_type=jnp.float32
        )
        grad_logits = attention * (grad_attention - correction[..., None])
        summed = jnp.sum(grad_logits, axis=1)
        column = jnp.sum(summed, axis=1)
        running = running_sums(summed)
        grad_chosen = jnp.where(
            select_mask, running - column[:, None, :] - grads_column[:, None, :], 0.0
        )
        grad_scores = grad_logits.at[:, 0].add(grad_chosen * jax.nn.sigmoid(scores[:, 0] - offset))
        grad_scores = grad_scores.astype(jnp.bfloat16)
        grad_query = (
            grad_query
            + jnp.einsum(
                "rhqk,rkhd->rqhd", grad_scores, key_heads, preferred_element_type=jnp.float32
            )
            * score_scale
        )
        grad_keys = (
            jnp.einsum("rhqk,rqhd->rkhd", grad_scores, queries, preferred_element_type=jnp.float32)
            * score_scale
        )
        grads_pair = grads_pair + jnp.concatenate(
            [
                grad_keys.reshape(row_count, block_len, features),
                grad_values.reshape(row_count, block_len, features),
            ],
            axis=-1,
        )
        grads_column = grads_column + column
        if section > 0:
            grads_pair, grads_column = (
                from_behind(grads_pair.astype(jnp.bfloat16), "seq", -1).astype(grads_pair.dtype),
                from_behind(grads_column.astype(jnp.bfloat16), "seq", -1).astype(
                    grads_column.dtype
                ),
            )
    d_packed = jnp.concatenate(
        [grad_query.reshape(token_count, features), grads_pair.reshape(token_count, 2 * features)],
        axis=-1,
    )
    d_packed = d_packed.astype(jnp.bfloat16)
    grad_qkv = jnp.dot(normed_low.T, d_packed, preferred_element_type=jnp.float32)
    d_normed = jnp.dot(d_packed, qkv_full.T, preferred_element_type=jnp.float32)
    d_inputs_part, grad_attn_gain = attn_norm_back(d_normed)
    d_tokens = (d_middle + d_inputs_part).reshape(row_count, block_len, features)
    gradients = (grad_qkv, grad_out, grad_up, grad_down, grad_attn_gain, grad_mlp_gain)
    reduced = (
        lax.psum_scatter(gradients[0], ("row", "seq"), scatter_dimension=0, tiled=True),
        lax.psum_scatter(gradients[1], ("row", "seq"), scatter_dimension=0, tiled=True),
        lax.psum_scatter(gradients[2], ("row", "seq"), scatter_dimension=0, tiled=True),
        lax.psum_scatter(gradients[3], ("row", "seq"), scatter_dimension=0, tiled=True),
        lax.psum_scatter(gradients[4], ("row", "seq"), scatter_dimension=0, tiled=True),
        lax.psum_scatter(gradients[5], ("row", "seq"), scatter_dimension=0, tiled=True),
    )
    return (
        output,
        d_tokens,
        reduced[0],
        reduced[1],
        reduced[2],
        reduced[3],
        reduced[4],
        reduced[5],
    )


def body(tokens, *rest):
    if lax.axis_size("seq") == 2 and tokens.shape[0] == 2:
        return row_body(tokens, *rest)
    return ring_body(tokens, *rest)


def solution(mesh):
    placed = (
        P("row", "seq", None),
        P("row", None),
        P(("row", "seq"), None),
        P(("row", "seq"), None),
        P(("row", "seq"), None),
        P(("row", "seq"), None),
        P(("row", "seq")),
        P(("row", "seq")),
        P("row", "seq", None),
    )
    return jax.shard_map(
        body,
        mesh=mesh,
        in_specs=placed,
        out_specs=(
            P("row", "seq", None),
            P("row", "seq", None),
            P(("row", "seq"), None),
            P(("row", "seq"), None),
            P(("row", "seq"), None),
            P(("row", "seq"), None),
            P(("row", "seq")),
            P(("row", "seq")),
        ),
        check_vma=False,
    )
```

```python
from functools import partial
import math

import jax
import jax.numpy as jnp
from jax import lax
from jax.experimental import pallas as pl
from jax.experimental.pallas import tpu as pltpu
from jax.sharding import PartitionSpec as P

H = 12
HD = 64
ROW_LEN = 2048
EPSILON = 1e-05
MASKED = -1e30
BIG = 1e30
LOG2E = 1.4426950408889634
OFFSET = math.log(ROW_LEN / 2.0) + 0.5
SAFE = 64.0
B = 256
BT = 512
MIB = 2**20
F32 = jnp.float32
BF = jnp.bfloat16


def dot(a, b):
    return jnp.dot(a, b, preferred_element_type=F32)


def dot_nt(a, b):
    return lax.dot_general(a, b, (((1,), (1,)), ((), ())), preferred_element_type=F32)


def dot_tn(a, b):
    return lax.dot_general(a, b, (((0,), (0,)), ((), ())), preferred_element_type=F32)


def iota(shape, dim):
    return lax.broadcasted_iota(jnp.int32, shape, dim)


def half_lanes(rows):
    return iota((rows, 128), 1) < HD


def pick_columns(c):
    return (iota((512, 128), 0) == 4 * iota((512, 128), 1) + c).astype(F32).astype(BF)


def pick_rows(piece, c):
    return (iota((piece, 4 * piece), 1) == 4 * iota((piece, 4 * piece), 0) + c).astype(F32).astype(BF)


def pack_kernel(qkv_ref, out_ref, up_ref, down_ref, ga_ref, gm_ref, a_ref, b_ref, l_ref):
    piece, features = out_ref.shape
    lane = iota((piece, 128), 1)
    a_ref[...] = qkv_ref[:, : 2 * features].astype(BF)
    b_ref[:, :features] = qkv_ref[:, 2 * features :].astype(BF)
    gains = jnp.where(lane == 0, ga_ref[...], jnp.where(lane == 1, gm_ref[...], 0.0))
    b_ref[:, features:] = gains.astype(BF)
    l_ref[:, :features] = out_ref[...].astype(BF)
    for c in range(4):
        pick = pick_columns(c)
        col = features * (1 + c)
        for tile in range(features // 128):
            part = up_ref[:, 512 * tile : 512 * tile + 512].astype(BF)
            l_ref[:, col + 128 * tile : col + 128 * tile + 128] = dot(part, pick).astype(BF)
        col = features * (5 + c)
        l_ref[:, col : col + features] = dot(pick_rows(piece, c), down_ref[...].astype(BF)).astype(BF)


def pack(w_qkv, w_out, w_up, w_down, gain_attn, gain_mlp):
    piece, features = w_out.shape
    return pl.pallas_call(
        pack_kernel,
        out_shape=[
            jax.ShapeDtypeStruct((piece, cols), BF) for cols in (2 * features, features + 128, 9 * features)
        ],
        name="pack_weights",
    )(w_qkv, w_out, w_up, w_down, gain_attn[:, None], gain_mlp[:, None])


def unpack_kernel(b_ref, out_ref, up_ref, down_ref):
    piece, features = out_ref.shape
    out_ref[...] = b_ref[:, :features].astype(F32)
    for tile in range(features // 128):
        total = None
        for c in range(4):
            col = features * (1 + c) + 128 * tile
            part = dot_nt(b_ref[:, col : col + 128], pick_columns(c))
            total = part if total is None else total + part
        up_ref[:, 512 * tile : 512 * tile + 512] = total
    total = None
    for c in range(4):
        col = features * (5 + c)
        part = dot_tn(pick_rows(piece, c), b_ref[:, col : col + features])
        total = part if total is None else total + part
    down_ref[...] = total


def unpack(buffer):
    piece = buffer.shape[0]
    features = (buffer.shape[1] - 128) // 9
    return pl.pallas_call(
        unpack_kernel,
        out_shape=(
            jax.ShapeDtypeStruct((piece, features), F32),
            jax.ShapeDtypeStruct((piece, 4 * features), F32),
            jax.ShapeDtypeStruct((4 * piece, features), F32),
        ),
        name="unpack_gradients",
    )(buffer)


def moments(values):
    mean_value = jnp.mean(values, axis=-1, keepdims=True)
    shifted = values - mean_value
    spread = jnp.mean(shifted * shifted, axis=-1, keepdims=True)
    return shifted, lax.rsqrt(spread + EPSILON)


def pick_half(own_ref, other_ref, step, steps):
    return jnp.where(step < steps // 2, own_ref[...], other_ref[...])


def halves(cols, steps):
    return (
        pl.BlockSpec((BT, cols), lambda t: (jnp.minimum(t, steps // 2 - 1), 0)),
        pl.BlockSpec((BT, cols), lambda t: (jnp.maximum(t - steps // 2, 0), 0)),
    )


def qkv_kernel(x_ref, other_ref, w_ref, v_w_ref, q_ref, k_ref, v_ref, rows_ref, size_ref):
    features = x_ref.shape[1]

    @pl.when(pl.program_id(0) == 0)
    def _():
        rows_ref[...] = v_w_ref[:, features:].astype(F32).T[:8]
        size_ref[...] = jnp.zeros_like(size_ref)

    shifted, scale = moments(pick_half(x_ref, other_ref, pl.program_id(0), pl.num_programs(0)).astype(F32))
    normed = (shifted * scale * rows_ref[0:1, :]).astype(BF)
    low = half_lanes(x_ref.shape[0])
    heads = (iota((features, 128), 0) // HD == iota((features, 128), 1)).astype(F32).astype(BF)

    def spread(ref, packed, other):
        for p in range(H // 2):
            pair = packed[:, 128 * p : 128 * p + 128]
            ref[:, 256 * p : 256 * p + 128] = jnp.where(low, pair, other).astype(BF)
            ref[:, 256 * p + 128 : 256 * p + 256] = jnp.where(low, other, pair).astype(BF)

    def measure(row, value):
        most = jnp.max(dot((value * value).astype(BF), heads), axis=0, keepdims=True)
        size_ref[row : row + 1] = jnp.maximum(size_ref[row : row + 1], most)

    q = dot(normed, w_ref[:, :features]) * (LOG2E / math.sqrt(HD))
    spread(q_ref, q, 0.0)
    measure(0, q)
    k = dot(normed, w_ref[:, features:])
    spread(k_ref, k, 1.0)
    measure(1, k)
    spread(v_ref, dot(normed, v_w_ref[:, :features]), 1.0)


def project_qkv(own, other, w_qk, w_v):
    tokens, features = 2 * own.shape[0], own.shape[1]
    steps = tokens // BT

    def tall(cols):
        return pl.BlockSpec((BT, cols), lambda t: (t, 0))

    def whole(array):
        return pl.BlockSpec(array.shape, lambda t: (0, 0))

    return pl.pallas_call(
        qkv_kernel,
        grid=(steps,),
        in_specs=[*halves(features, steps), whole(w_qk), whole(w_v)],
        out_specs=[
            tall(2 * features),
            tall(2 * features),
            tall(2 * features),
            pl.BlockSpec((8, features), lambda t: (0, 0)),
            pl.BlockSpec((8, 128), lambda t: (0, 0)),
        ],
        out_shape=[
            jax.ShapeDtypeStruct((tokens, 2 * features), BF),
            jax.ShapeDtypeStruct((tokens, 2 * features), BF),
            jax.ShapeDtypeStruct((tokens, 2 * features), BF),
            jax.ShapeDtypeStruct((8, features), F32),
            jax.ShapeDtypeStruct((8, 128), F32),
        ],
        compiler_params=pltpu.CompilerParams(vmem_limit_bytes=48 * MIB),
        name="project_qkv",
    )(own, other, w_qk, w_v)


def pick(h):
    return slice(128 * h, 128 * h + 128)


def block_rows(index):
    return pl.ds(pl.multiple_of(index * B, B), B)


def two_part(tri, values):
    high = values.astype(BF)
    rest = (values - high.astype(F32)).astype(BF)
    return dot(tri, high) + dot(tri, rest)


def selection(scores, segq, segk, rows, cols):
    earlier = (segq == segk) & (cols < rows)
    x = scores - OFFSET * LOG2E
    grown = jnp.exp2(jnp.minimum(x, 100.0))
    more = 1.0 + grown
    return jnp.where(earlier, jnp.maximum(x, jnp.log2(more)), 0.0), jnp.where(earlier, grown / more, 0.0)


def mixed(first, second):
    done = 0
    for n, step in enumerate(first):
        step()
        upto = (n + 1) * len(second) // len(first)
        for other in second[done:upto]:
            other()
        done = upto


STRIP = 64


def key_copies(block, stored, k_any, v_any, kx, vx, sem):
    rows = block_rows(stored)
    return (
        pltpu.make_async_copy(k_any.at[rows, :], kx.at[block], sem.at[0, block]),
        pltpu.make_async_copy(v_any.at[rows, :], vx.at[block], sem.at[1, block]),
    )


def forward_kernel(tab, slow, q_ref, q0_ref, k0_ref, segq_ref, segk_ref, k_any, v_any, o_ref, li_ref, e_ref,
                   acc, carry, tri, qx, penalty, gate, work, high, kx, vx, sem):
    t = pl.program_id(0)
    ib, jb = tab[2, t], tab[3, t]

    @pl.when(t == 0)
    def _():
        for block in range(kx.shape[0]):
            for copy in key_copies(block, tab[1, block * (block + 3) // 2], k_any, v_any, kx, vx, sem):
                copy.start()

    def prepare(step, slot):
        keys = block_rows(tab[1, step])
        at = tab[3, step]
        ahead = (tab[2, step] - at) * B
        segk = segk_ref[tab[1, step], 0:1, :]
        sums = []

        def scores():
            work[...] = dot_nt(q0_ref[block_rows(tab[0, step]), :], k0_ref[keys, :])

        def strip(n):
            part = slice(STRIP * n, STRIP * n + STRIP)
            segq = segq_ref[pl.ds(pl.multiple_of(tab[0, step] * B + STRIP * n, STRIP), STRIP), :]
            return part, segq, iota((STRIP, B), 0) + (ahead + STRIP * n), iota((STRIP, B), 1)

        def choose(n):
            part, segq, rows, cols = strip(n)
            chosen, opened = selection(work[part, :], segq, segk, rows, cols)
            gate[slot, part, :] = opened.astype(BF)
            high[part, :] = chosen.astype(BF)
            sums.append(jnp.sum(chosen, axis=0, keepdims=True))

        def add():
            before = carry[at, 0:1, :]
            work[...] = dot(tri[...], high[...]) + before
            carry[at, 0:1, :] = before + sum(sums[1:], sums[0])

        def close(n):
            part, segq, rows, cols = strip(n)
            penalty[slot, part, :] = jnp.where((segq == segk) & (cols <= rows), work[part, :], BIG)

        count = range(B // STRIP)
        return [scores] + [partial(choose, n) for n in count] + [add] + [partial(close, n) for n in count]

    @pl.when(t == 0)
    def _():
        carry[...] = jnp.zeros_like(carry)
        tri[...] = (iota((B, B), 1) < iota((B, B), 0)).astype(F32).astype(BF)
        for step in prepare(0, 0):
            step()

    @pl.when(jb == 0)
    def _():
        acc[...] = jnp.zeros_like(acc)
        qx[...] = q_ref[...]
        for copy in key_copies(ib, tab[0, t], k_any, v_any, kx, vx, sem):
            copy.wait()

        @pl.when(slow[0] != 0)
        def _():
            lane = iota((B, 128), 1)
            segq = segq_ref[block_rows(tab[0, t]), :]
            cols = iota((B, B), 1)

            def chosen(other):
                rows = iota((B, B), 0) + (ib - other) * B
                base = tab[1, t + other]
                first = dot_nt(q_ref[:, 0:128], k0_ref[block_rows(base), :])
                return selection(first, segq, segk_ref[base, 0:1, :], rows, cols)[0]

            own = jnp.sum(chosen(0), axis=0, keepdims=True)

            def step(other, top):
                base = tab[1, t + other]
                before = carry[other, 0:1, :] - jnp.where(other == 0, own, 0.0)
                kept = (segq == segk_ref[base, 0:1, :]) & (cols <= iota((B, B), 0) + (ib - other) * B)
                z_penalty = jnp.where(kept, dot(tri[...], chosen(other).astype(BF)) + before, BIG)
                for h in range(H):
                    z = dot_nt(q_ref[:, pick(h)], kx[other, :, pick(h)]) - z_penalty
                    top = jnp.where(lane == h, jnp.maximum(top, jnp.max(z, axis=1, keepdims=True)), top)
                return top

            top = lax.fori_loop(0, ib + 1, step, jnp.full((B, 128), -BIG, F32))
            for h in range(H):
                shift = -jnp.sum(jnp.where(lane == h, top, 0.0), axis=1, keepdims=True)
                one = shift.astype(BF).astype(F32)
                two = (shift - one).astype(BF).astype(F32)
                three = shift - one - two
                at = lane - (HD if h % 2 == 0 else 0)
                extra = jnp.where(at == 0, one, jnp.where(at == 1, two, jnp.where(at == 2, three, 0.0)))
                keep = (lane < HD) if h % 2 == 0 else (lane >= HD)
                qx[:, pick(h)] = jnp.where(keep, q_ref[:, pick(h)].astype(F32), extra).astype(BF)

    slot = t % 2

    def head(h):
        e = jnp.exp2(dot_nt(qx[:, pick(h)], kx[jb, :, pick(h)]) - penalty[slot]).astype(BF)
        e_ref[0, h] = e
        acc[:, pick(h)] += dot(e, vx[jb, :, pick(h)])

    e_ref[0, H] = gate[slot]
    mixed([partial(head, h) for h in range(H)], prepare(t + 1, 1 - slot))

    @pl.when(jb == ib)
    def _():
        low = half_lanes(B)
        for p in range(H // 2):
            one = acc[:, pick(2 * p)]
            two = acc[:, pick(2 * p + 1)]
            inverse = 1.0 / pltpu.roll(jnp.where(low, two, one), HD, 1)
            o_ref[:, pick(p)] = (jnp.where(low, one, two) * inverse).astype(BF)
            li_ref[:, pick(p)] = inverse


def attention_forward(table, slow, q, k, v, seg_col, seg_row):
    tokens = q.shape[0]
    blocks = tokens // B
    tiles = table.shape[1] - 1
    wide = 128 * H
    narrow = HD * H
    once = pl.Buffered(1)
    return pl.pallas_call(
        forward_kernel,
        grid_spec=pltpu.PrefetchScalarGridSpec(
            num_scalar_prefetch=2,
            grid=(tiles,),
            in_specs=[
                pl.BlockSpec((B, wide), lambda t, tab, slow: (tab[0, t], 0)),
                pl.BlockSpec((tokens, 128), lambda t, tab, slow: (0, 0), pipeline_mode=once),
                pl.BlockSpec((tokens, 128), lambda t, tab, slow: (0, 0), pipeline_mode=once),
                pl.BlockSpec((tokens, 1), lambda t, tab, slow: (0, 0), pipeline_mode=once),
                pl.BlockSpec((blocks, 8, B), lambda t, tab, slow: (0, 0, 0), pipeline_mode=once),
                pl.BlockSpec(memory_space=pl.ANY),
                pl.BlockSpec(memory_space=pl.ANY),
            ],
            out_specs=[
                pl.BlockSpec((B, narrow), lambda t, tab, slow: (tab[0, t], 0)),
                pl.BlockSpec((B, narrow), lambda t, tab, slow: (tab[0, t], 0)),
                pl.BlockSpec((1, H + 1, B, B), lambda t, tab, slow: (tab[4, t], 0, 0, 0)),
            ],
            scratch_shapes=[
                pltpu.VMEM((B, wide), F32),
                pltpu.VMEM((blocks, 8, B), F32),
                pltpu.VMEM((B, B), BF),
                pltpu.VMEM((B, wide), BF),
                pltpu.VMEM((2, B, B), F32),
                pltpu.VMEM((2, B, B), BF),
                pltpu.VMEM((B, B), F32),
                pltpu.VMEM((B, B), BF),
                pltpu.VMEM((blocks, B, wide), BF),
                pltpu.VMEM((blocks, B, wide), BF),
                pltpu.SemaphoreType.DMA((2, blocks)),
            ],
        ),
        out_shape=[
            jax.ShapeDtypeStruct((tokens, narrow), BF),
            jax.ShapeDtypeStruct((tokens, narrow), F32),
            jax.ShapeDtypeStruct((tiles, H + 1, B, B), BF),
        ],
        compiler_params=pltpu.CompilerParams(vmem_limit_bytes=48 * MIB),
        name="attention_forward",
    )(table, slow, q, q, k, seg_col, seg_row, k, v)


def backward_kernel(tab, e_ref, q_ref, d_ref, q0_ref, k0_ref, k_any, v_any, o_ref,
                    dq, dkt, dvt, carry, tri, sums, first, gate, work, kx, vx, sem):
    t = pl.program_id(0)
    last = pl.num_programs(0) - 1
    before = jnp.maximum(t - 1, 0)
    narrow = HD * H
    low = half_lanes(B)
    slot = t % 2

    @pl.when(t == 0)
    def _():
        for block in range(kx.shape[0]):
            for copy in key_copies(block, tab[1, block], k_any, v_any, kx, vx, sem):
                copy.start()
        carry[...] = jnp.zeros_like(carry)
        tri[...] = (iota((B, B), 1) > iota((B, B), 0)).astype(F32).astype(BF)
        dkt[...] = jnp.zeros_like(dkt)
        dvt[...] = jnp.zeros_like(dvt)
        dq[...] = jnp.zeros_like(dq)
        sums[...] = jnp.zeros_like(sums)
        first[...] = jnp.zeros_like(first)
        gate[...] = jnp.zeros_like(gate)

    @pl.when((tab[3, t] == 0) & (t < last))
    def _():
        dq[tab[2, t] % 2] = jnp.zeros(dq.shape[1:], F32)

    @pl.when(t < kx.shape[0])
    def _():
        for copy in key_copies(t, tab[1, t], k_any, v_any, kx, vx, sem):
            copy.wait()

    def finish():
        at = tab[3, before]

        def add():
            total = sums[1 - slot]
            later = carry[at, 0:1, :] + two_part(tri[...], total)
            carry[at, 0:1, :] = carry[at, 0:1, :] + jnp.sum(total, axis=0, keepdims=True)
            work[...] = (first[1 - slot] - later * gate[1 - slot].astype(F32)).astype(BF)

        def keys():
            dkt[:HD, block_rows(at)] += dot_tn(q0_ref[block_rows(tab[0, before]), :], work[...])[:HD]

        def queries():
            more = dot(work[...], k0_ref[block_rows(tab[1, before]), :])
            dq[tab[2, before] % 2, :, :128] += jnp.where(low, more, 0.0)

        return [add, keys, queries]

    @pl.when(t == last)
    def _():
        for step in finish():
            step()

    @pl.when(t < last)
    def _():
        cols = block_rows(tab[3, t])
        turn = tab[2, t] % 2
        kept = {}
        parts = {}

        def score(h):
            e = e_ref[0, h]
            dz = e.astype(F32) * dot_nt(d_ref[:, pick(h)], vx[tab[3, t], :, pick(h)])
            if h == 0:
                first[slot] = dz
                sums[slot] = dz
            else:
                sums[slot] += dz
                kept[h] = dz.astype(BF)

        def products(h):
            own = slice(HD * h, HD * h + HD)
            data = slice(HD * (h % 2), HD * (h % 2) + HD)
            dvt[own, cols] += dot_tn(d_ref[:, pick(h)], e_ref[0, h])[data]
            if h == 0:
                parts[0] = 0.0
                return
            ds = kept.pop(h)
            dkt[own, cols] += dot_tn(q_ref[:, pick(h)], ds)[data]
            parts[h] = dot(ds, kx[tab[3, t], :, pick(h)])
            if h % 2:
                dq[turn, :, pick(h // 2)] += jnp.where(low, parts.pop(h - 1), parts.pop(h))

        gate[slot] = e_ref[0, H]
        steps = [partial(score, 0)]
        for h in range(H):
            if h + 1 < H:
                steps.append(partial(score, h + 1))
            steps.append(partial(products, h))
        mixed(steps, finish())

    @pl.when((t > 0) & (tab[3, before] == tab[2, before]))
    def _():
        cols = block_rows(tab[2, before])
        o_ref[:, :narrow] = (dq[tab[2, before] % 2] * (1.0 / math.sqrt(HD))).astype(BF)
        o_ref[:, narrow : 2 * narrow] = (dkt[:, cols] * (1.0 / LOG2E)).astype(BF).T
        o_ref[:, 2 * narrow :] = dvt[:, cols].astype(BF).T


def attention_backward(table, e, q, k, v, d):
    tokens = q.shape[0]
    blocks = tokens // B
    tiles = table.shape[1] - 1
    wide = 128 * H
    narrow = HD * H
    once = pl.Buffered(1)
    return pl.pallas_call(
        backward_kernel,
        grid_spec=pltpu.PrefetchScalarGridSpec(
            num_scalar_prefetch=1,
            grid=(tiles + 1,),
            in_specs=[
                pl.BlockSpec((1, H + 1, B, B), lambda t, tab: (tab[4, t], 0, 0, 0)),
                pl.BlockSpec((B, wide), lambda t, tab: (tab[0, t], 0)),
                pl.BlockSpec((B, wide), lambda t, tab: (tab[0, t], 0)),
                pl.BlockSpec((tokens, 128), lambda t, tab: (0, 0), pipeline_mode=once),
                pl.BlockSpec((tokens, 128), lambda t, tab: (0, 0), pipeline_mode=once),
                pl.BlockSpec(memory_space=pl.ANY),
                pl.BlockSpec(memory_space=pl.ANY),
            ],
            out_specs=pl.BlockSpec((B, 3 * narrow), lambda t, tab: (tab[0, jnp.maximum(t - 1, 0)], 0)),
            scratch_shapes=[
                pltpu.VMEM((2, B, narrow), F32),
                pltpu.VMEM((narrow, tokens), F32),
                pltpu.VMEM((narrow, tokens), F32),
                pltpu.VMEM((blocks, 8, B), F32),
                pltpu.VMEM((B, B), BF),
                pltpu.VMEM((2, B, B), F32),
                pltpu.VMEM((2, B, B), F32),
                pltpu.VMEM((2, B, B), BF),
                pltpu.VMEM((B, B), BF),
                pltpu.VMEM((blocks, B, wide), BF),
                pltpu.VMEM((blocks, B, wide), BF),
                pltpu.SemaphoreType.DMA((2, blocks)),
            ],
        ),
        out_shape=jax.ShapeDtypeStruct((tokens, 3 * narrow), BF),
        compiler_params=pltpu.CompilerParams(vmem_limit_bytes=56 * MIB),
        cost_estimate=pl.CostEstimate(flops=tiles * H * B * B * 1024, bytes_accessed=tiles * B * B, transcendentals=0),
        name="attention_backward",
    )(table, e, q, d, q, k, k, v)


def tile_tables(blocks, position):
    pairs = [(i, j) for i in range(blocks) for j in range(i + 1)]
    back = [(i, j) for i in reversed(range(blocks)) for j in range(i + 1)]
    shift = position * (blocks // 2)

    def table(order):
        order = order + order[-1:]
        rows = jnp.array([i for i, _ in order], jnp.int32)
        keys = jnp.array([j for _, j in order], jnp.int32)
        return jnp.stack(
            [(rows + shift) % blocks, (keys + shift) % blocks, rows, keys, rows * (rows + 1) // 2 + keys]
        )

    return table(pairs), table(back)


PART = 256
ROWS = 64


def mlp_kernel(x_ref, x2_ref, ob_ref, dy1_ref, dy2_ref, li_ref, gain_ref, wo_ref, wu_ref, wd_ref, out_ref, dx_ref, d_ref, g_any,
               xh, scales, y, dn, n2, gup, gdown, gout, gsum, stage, us, das, actives, dus, sem):
    c, t = pl.program_id(0), pl.program_id(1)
    chunks, steps = pl.num_programs(0), pl.num_programs(1)
    rows = pl.ds(pl.multiple_of(t * BT, BT), BT)
    features = x_ref.shape[1]

    def send(slot, column):
        start = pl.multiple_of(column, 128)
        return pltpu.make_async_copy(stage.at[slot], g_any.at[:, pl.ds(start, features)], sem.at[slot])

    @pl.when(c == 0)
    def _():
        middle = pick_half(x_ref, x2_ref, t, steps).astype(F32) + dot(ob_ref[...], wo_ref[...])
        shifted, scale = moments(middle)
        xh[rows, :] = (shifted * scale).astype(BF)
        scales[rows, :] = jnp.broadcast_to(scale, (BT, 128))
        y[rows, :] = middle
        dn[rows, :] = jnp.zeros_like(middle)
        n2[rows, :] = (shifted * scale * gain_ref[1:2, :]).astype(BF)

    @pl.when(t == 0)
    def _():
        gup[...] = jnp.zeros_like(gup)
        gdown[...] = jnp.zeros_like(gdown)

    @pl.when((c == 0) & (t == 0))
    def _():
        gout[...] = jnp.zeros_like(gout)
        gsum[...] = jnp.zeros_like(gsum)

    n2_low = n2[rows, :]
    dy_low = pick_half(dy1_ref, dy2_ref, t, steps)

    def enter(p):
        units = slice(PART * p, PART * p + PART)

        def up():
            us[p % 2] = dot(n2_low, wu_ref[:, units])

        def down():
            das[p % 2] = dot_nt(dy_low, wd_ref[units, :])

        return [up, down]

    def bend(p, n):
        part = slice(ROWS * n, ROWS * n + ROWS)
        u = us[p % 2, part, :]
        cdf = 0.5 * (1.0 + lax.erf(u * math.sqrt(0.5)))
        density = jnp.exp(-0.5 * u * u) * (1.0 / math.sqrt(2.0 * math.pi))
        units = slice(PART * p, PART * p + PART)
        actives[part, units] = (u * cdf).astype(BF)
        dus[part, units] = ((cdf + u * density) * das[p % 2, part, :]).astype(BF)

    def leave(p):
        units = slice(PART * p, PART * p + PART)

        def down():
            y[rows, :] += dot(actives[:, units], wd_ref[units, :])

        def up():
            dn[rows, :] += dot_nt(dus[:, units], wu_ref[:, units])

        return [down, up]

    parts = features // PART
    for step in enter(0):
        step()
    for p in range(parts):
        products = (leave(p - 1) if p else []) + (enter(p + 1) if p + 1 < parts else [])
        mixed(products, [partial(bend, p, n) for n in range(BT // ROWS)])
    for step in leave(parts - 1):
        step()
    gdown[...] += dot_tn(actives[...], dy_low)
    gup[...] += dot_tn(n2_low, dus[...])

    @pl.when(t == steps - 1)
    def _():
        @pl.when(c > 0)
        def _():
            send(0, c * features).wait()
            send(1, (c + chunks) * features).wait()

        stage[0] = gup[...].astype(BF)
        stage[1] = gdown[...].astype(BF)
        send(0, (1 + c) * features).start()
        send(1, (1 + c + chunks) * features).start()

    @pl.when(c == chunks - 1)
    def _():
        out_ref[...] = y[rows, :].astype(BF)
        d_normed = dn[rows, :]
        scale = scales[rows, 0:1]
        unit = xh[rows, :].astype(F32)
        product = d_normed * unit
        gsum[...] += jnp.sum(product.reshape(BT // 8, 8, features), axis=0)
        inner = d_normed * gain_ref[1:2, :]
        dx = dy_low.astype(F32) + scale * (
            inner - jnp.mean(inner, axis=-1, keepdims=True) - unit * jnp.mean(inner * unit, axis=-1, keepdims=True)
        )
        dx_ref[...] = dx.astype(BF)
        db = dx.astype(BF)
        gout[...] += dot_tn(ob_ref[...], db)
        scaled = dot_nt(db, wo_ref[...]) * li_ref[...]
        low = half_lanes(BT)
        lane = iota((BT, 128), 1)
        swap_row, swap_col = iota((128, 128), 0), iota((128, 128), 1)
        swap = ((swap_row // HD != swap_col // HD) & (swap_col % HD < 2)).astype(F32).astype(BF)
        for p in range(H // 2):
            w = slice(128 * p, 128 * p + 128)
            pair = scaled[:, w]
            both = pair * ob_ref[:, w].astype(F32)
            high = both.astype(BF)
            delta = dot(high, swap) + dot((both - high.astype(F32)).astype(BF), swap)
            top = delta.astype(BF).astype(F32)
            extra = jnp.where((lane == 0) | (lane == HD), -top, top - delta)
            d_ref[:, 256 * p : 256 * p + 128] = jnp.where(low, pair, extra).astype(BF)
            d_ref[:, 256 * p + 128 : 256 * p + 256] = jnp.where(low, extra, pair).astype(BF)

    @pl.when((c == chunks - 1) & (t == steps - 1))
    def _():
        stage[2] = gout[...].astype(BF)
        column = jnp.broadcast_to(jnp.sum(gsum[...], axis=0, keepdims=True), (128, features))
        stage[3, :, :128] = column.T.astype(BF)
        last = pltpu.make_async_copy(
            stage.at[3, :, pl.ds(0, 128)], g_any.at[:, pl.ds((1 + 2 * 4) * features, 128)], sem.at[3]
        )
        send(2, 0).start()
        last.start()
        send(0, chunks * features).wait()
        send(1, 2 * chunks * features).wait()
        send(2, 0).wait()
        last.wait()


def feed_forward(x, x_other, ob, dy, dy_other, li, gains, weights):
    tokens, features = ob.shape
    steps = tokens // BT
    chunks = 4

    def ends(c, t):
        return (jnp.where((c == 0) | (c == chunks - 1), t, steps - 1), 0)

    def own(t):
        return jnp.minimum(t, steps // 2 - 1)

    def other(t):
        return jnp.maximum(t - steps // 2, 0)

    def at_last(c, t):
        return (jnp.where(c == chunks - 1, t, 0), 0)

    block = (BT, features)
    once = pl.Buffered(1)
    return pl.pallas_call(
        mlp_kernel,
        grid=(chunks, steps),
        in_specs=[
            pl.BlockSpec(block, lambda c, t: (own(jnp.where(c == 0, t, steps - 1)), 0), pipeline_mode=once),
            pl.BlockSpec(block, lambda c, t: (other(jnp.where(c == 0, t, steps - 1)), 0), pipeline_mode=once),
            pl.BlockSpec(block, ends),
            pl.BlockSpec(block, lambda c, t: (own(t), 0)),
            pl.BlockSpec(block, lambda c, t: (other(t), 0)),
            pl.BlockSpec(block, at_last, pipeline_mode=once),
            pl.BlockSpec((8, features), lambda c, t: (0, 0)),
            pl.BlockSpec((features, features), lambda c, t: (0, 0), pipeline_mode=once),
            pl.BlockSpec((features, features), lambda c, t: (0, 1 + c)),
            pl.BlockSpec((features, features), lambda c, t: (0, 1 + chunks + c)),
        ],
        out_specs=[
            pl.BlockSpec(block, at_last),
            pl.BlockSpec(block, at_last),
            pl.BlockSpec((BT, 2 * features), at_last),
            pl.BlockSpec(memory_space=pl.ANY),
        ],
        out_shape=[
            jax.ShapeDtypeStruct((tokens, features), BF),
            jax.ShapeDtypeStruct((tokens, features), BF),
            jax.ShapeDtypeStruct((tokens, 2 * features), BF),
            jax.ShapeDtypeStruct((features, 9 * features + 128), BF),
        ],
        scratch_shapes=[
            pltpu.VMEM((tokens, features), BF),
            pltpu.VMEM((tokens, 128), F32),
            pltpu.VMEM((tokens, features), F32),
            pltpu.VMEM((tokens, features), F32),
            pltpu.VMEM((tokens, features), BF),
            pltpu.VMEM((features, features), F32),
            pltpu.VMEM((features, features), F32),
            pltpu.VMEM((features, features), F32),
            pltpu.VMEM((8, features), F32),
            pltpu.VMEM((4, features, features), BF),
            pltpu.VMEM((2, BT, PART), F32),
            pltpu.VMEM((2, BT, PART), F32),
            pltpu.VMEM((BT, features), BF),
            pltpu.VMEM((BT, features), BF),
            pltpu.SemaphoreType.DMA((4,)),
        ],
        compiler_params=pltpu.CompilerParams(vmem_limit_bytes=63 * MIB),
        name="feed_forward",
    )(x, x_other, ob, dy, dy_other, li, gains, weights, weights, weights)


def weight_order(bits, dims):
    return [
        sum(((place >> (bits - 1 - n)) & 1) << dim for n, dim in enumerate(dims)) for place in range(2**bits)
    ]


def weight_kernel(x_ref, other_ref, dqkv_ref, gain_ref, a_ref, b_ref, acc, *, orders):
    t = pl.program_id(0)

    @pl.when(t == 0)
    def _():
        acc[...] = jnp.zeros_like(acc)

    shifted, scale = moments(pick_half(x_ref, other_ref, t, pl.num_programs(0)).astype(F32))
    normed = (shifted * scale * gain_ref[0:1, :]).astype(BF)
    acc[...] += dot_tn(normed, dqkv_ref[...])

    @pl.when(t == pl.num_programs(0) - 1)
    def _():
        _, piece, split = a_ref.shape
        for place, block in enumerate(orders[0]):
            a_ref[place] = acc[piece * block : piece * block + piece, :split].astype(BF)
        for place, block in enumerate(orders[1]):
            b_ref[place] = acc[piece * block : piece * block + piece, split:].astype(BF)


def first_weight_gradient(x, x_other, dqkv, gains, orders):
    tokens, features = dqkv.shape[0], x.shape[1]
    steps = tokens // BT
    blocks = len(orders[0])
    shapes = [(blocks, features // blocks, cols) for cols in (2 * features, features)]
    return pl.pallas_call(
        partial(weight_kernel, orders=orders),
        grid=(steps,),
        in_specs=[
            *halves(features, steps),
            pl.BlockSpec((BT, 3 * features), lambda t: (t, 0)),
            pl.BlockSpec(gains.shape, lambda t: (0, 0)),
        ],
        out_specs=[pl.BlockSpec(shape, lambda t: (0, 0, 0)) for shape in shapes],
        out_shape=[jax.ShapeDtypeStruct(shape, BF) for shape in shapes],
        scratch_shapes=[pltpu.VMEM((features, 3 * features), F32)],
        compiler_params=pltpu.CompilerParams(vmem_limit_bytes=48 * MIB),
        cost_estimate=pl.CostEstimate(
            flops=12 * tokens * features * features, bytes_accessed=16 * tokens * features, transcendentals=0
        ),
        name="first_weight_gradient",
    )(x, x_other, dqkv, gains)


def tokens_kernel(x_ref, dqkv_ref, dx_ref, gain_ref, w_ref, v_w_ref, out_ref, gsum_ref):
    features = x_ref.shape[1]

    @pl.when(pl.program_id(0) == 0)
    def _():
        gsum_ref[...] = jnp.zeros_like(gsum_ref)

    shifted, scale = moments(x_ref[...].astype(F32))
    xh = shifted * scale
    d_normed = dot_nt(dqkv_ref[:, : 2 * features], w_ref[...])
    d_normed += dot_nt(dqkv_ref[:, 2 * features :], v_w_ref[:, :features])
    gsum_ref[...] += jnp.sum((d_normed * xh).reshape(BT // 8, 8, features), axis=0)
    inner = d_normed * gain_ref[0:1, :]
    dx = dx_ref[...].astype(F32) + scale * (
        inner - jnp.mean(inner, axis=-1, keepdims=True) - xh * jnp.mean(inner * xh, axis=-1, keepdims=True)
    )
    out_ref[...] = dx.astype(out_ref.dtype)


def first_token_gradient(x, dqkv, dx, gains, w_qk, w_v, half, dtype):
    tokens, features = x.shape
    steps = tokens // BT

    def tall(cols):
        return pl.BlockSpec((BT, cols), lambda t: (t + half * steps, 0))

    def whole(array):
        return pl.BlockSpec(array.shape, lambda t: (0, 0))

    own = pl.BlockSpec((BT, features), lambda t: (t, 0))
    return pl.pallas_call(
        tokens_kernel,
        grid=(steps,),
        in_specs=[own, tall(3 * features), tall(features), whole(gains), whole(w_qk), whole(w_v)],
        out_specs=[own, pl.BlockSpec((8, features), lambda t: (0, 0))],
        out_shape=[jax.ShapeDtypeStruct((tokens, features), dtype), jax.ShapeDtypeStruct((8, features), F32)],
        compiler_params=pltpu.CompilerParams(vmem_limit_bytes=48 * MIB),
        cost_estimate=pl.CostEstimate(
            flops=12 * tokens * features * features, bytes_accessed=16 * tokens * features, transcendentals=0
        ),
        name="first_token_gradient",
    )(x, dqkv, dx, gains, w_qk, w_v)


def swap(value):
    return lax.ppermute(value, "seq", [(0, 1), (1, 0)])


def own_and_other(pair, position):
    return (
        lax.dynamic_index_in_dim(pair, position, 0, keepdims=False),
        lax.dynamic_index_in_dim(pair, 1 - position, 0, keepdims=False),
    )


def in_order(own, other, position):
    return jnp.where(position == 0, jnp.stack([own, other]), jnp.stack([other, own]))


def exchange(value, dim):
    axis = "seq" if dim == 0 else "row"
    step = 1 if dim == 0 else 1 << (dim - 1)
    return lax.ppermute(value, axis, [(i, i ^ step) for i in range(lax.axis_size(axis))])


def bit(dim):
    return lax.axis_index("seq") if dim == 0 else (lax.axis_index("row") >> (dim - 1)) & 1


def doubled(array, shape, held, dim):
    other = exchange(array, dim)
    outer = sum(1 for d in held if d > dim)
    own = array.reshape(2**outer, -1, *shape)
    other = other.reshape(own.shape)
    both = jnp.where(bit(dim) == 0, jnp.stack([own, other], 1), jnp.stack([other, own], 1))
    return both.reshape(-1, *shape)


def halved(value, dim):
    half = value.shape[0] // 2
    mine = bit(dim)
    keep = lax.dynamic_slice_in_dim(value, mine * half, half, 0)
    send = lax.dynamic_slice_in_dim(value, (1 - mine) * half, half, 0)
    return keep + exchange(send, dim)


def cut(value, shares):
    rows = value.shape[0] // sum(shares)
    ends = [rows * sum(shares[: n + 1]) for n in range(len(shares))]
    return [value[end - rows * share : end] for share, end in zip(shares, ends) if share]


def after(value, *others):
    return lax.optimization_barrier((value, *others))[0]


def row_body(tokens, segments, w_qkv, w_out, w_up, w_down, gain_attn, gain_mlp, cotangent):
    both = ("row", "seq")
    position = lax.axis_index("seq")
    devices = 2 * lax.axis_size("row")
    bits = devices.bit_length() - 1
    far = tuple(range(3, bits))
    _, half, features = tokens.shape
    *pieces, later_piece = pack(w_qkv, w_out, w_up, w_down, gain_attn, gain_mlp)
    x, other = own_and_other(tokens, position)
    paths = ((0, *reversed(far), 2, 1), (0, 2, *reversed(far), 1))
    gathered = [piece[None] for piece in pieces]
    parts = cut(other, [0] * (bits - 4) + [2, 2, 3, 1])
    x_parts = []
    for stage in range(bits):
        *gathered, x_parts, parts = lax.optimization_barrier((*gathered, x_parts, parts))
        if stage == bits - 2:
            later_piece = after(later_piece, *gathered)
        for n, path in enumerate(paths):
            gathered[n] = doubled(gathered[n], pieces[n].shape, path[:stage], path[stage])
        if stage and parts:
            x_parts = x_parts + [swap(parts[0])]
            parts = parts[1:]
    x_other = jnp.concatenate(x_parts)
    w_qk, w_v = [array.reshape(-1, array.shape[-1]) for array in gathered]
    w_later = lax.all_gather(later_piece, both, axis=0, tiled=True)
    dy, other = own_and_other(cotangent, position)
    dy_other = swap(after(other, w_qk, x_other))
    row_segments = lax.dynamic_index_in_dim(segments, position, 0, keepdims=False)
    stored = jnp.roll(row_segments, position * half)
    seg_col = stored[:, None]
    seg_row = jnp.broadcast_to(stored.reshape(-1, 1, B), (stored.shape[0] // B, 8, B))
    q, k, v, gains, sizes = project_qkv(x, x_other, w_qk, w_v)
    slow = jnp.any(sizes[0] * sizes[1] * 1.05 > SAFE * SAFE).astype(jnp.int32)[None]
    table, back_table = tile_tables(2 * half // B, position)
    ob, li, e = attention_forward(table, slow, q, k, v, seg_col, seg_row)
    output, dx, d, g_later = feed_forward(x, x_other, ob, dy, dy_other, li, gains, w_later)
    r_later = lax.psum_scatter(g_later, both, scatter_dimension=0, tiled=True)
    output_other = swap(output[half:])
    dqkv = attention_backward(back_table, e, q, k, v, d)
    dqkv, output_other = lax.optimization_barrier((dqkv, output_other))
    paths = ((1, 2, *far, 0), (1, *far, 2, 0))
    d_other, sum_other = first_token_gradient(x_other, dqkv, dx, gains, w_qk, w_v, 1, BF)
    parts = cut(d_other, [1, 1, 1, 1])
    d_parts = []
    orders = [weight_order(bits, path) for path in paths]
    summed = list(first_weight_gradient(x, x_other, after(dqkv, d_other), gains, orders))
    d_own, sum_own = first_token_gradient(x, after(dqkv, *summed), dx, gains, w_qk, w_v, 0, F32)
    sums = jnp.sum(sum_other + sum_own, axis=0)
    g_gain = jnp.transpose(sums.reshape(*[2] * bits, -1), [bits - 1 - dim for dim in paths[0]] + [bits])
    g_gain = g_gain.reshape(devices, 1, -1)
    for stage in range(bits):
        if stage == bits - 1:
            summed[0], r_later = lax.optimization_barrier((summed[0], r_later))
        *summed, d_parts, parts = lax.optimization_barrier((*summed, d_parts, parts))
        for n, path in enumerate(paths):
            summed[n] = halved(summed[n], path[stage])
        if parts:
            d_parts = d_parts + [swap(parts[0])]
            parts = parts[1:]
        g_gain = halved(g_gain, paths[0][stage])
    output = in_order(output[:half], output_other, position)
    d_tokens = in_order(d_own, jnp.concatenate(d_parts).astype(F32), position)
    g_out, g_up, g_down = unpack(r_later)
    return (
        output,
        d_tokens,
        jnp.concatenate([summed[0][0], summed[1][0]], axis=1).astype(F32),
        g_out,
        g_up,
        g_down,
        g_gain[0, 0],
        r_later[:, 9 * features].astype(F32),
    )


def from_behind(value, axis, steps):
    count = lax.axis_size(axis)
    first, last = (max(0, -steps), min(count, count - steps))
    return lax.ppermute(value, axis, [(source, source + steps) for source in range(first, last)])


def layer_norm(values, scaling):
    mean_value = jnp.mean(values, axis=-1, keepdims=True)
    shifted = values - mean_value
    spread = jnp.mean(shifted * shifted, axis=-1, keepdims=True)
    return shifted * lax.rsqrt(spread + EPSILON) * scaling


def running_sums(values):
    places = jnp.arange(values.shape[1], dtype=jnp.int32)
    upto = (places[None, :] <= places[:, None]).astype(jnp.float32)
    return jnp.einsum("im,rmj->rij", upto, values, precision=lax.Precision.HIGHEST)


def block_masks(segments, position, source, block_len):
    offsets = jnp.arange(block_len, dtype=jnp.int32)
    query_pos = position * block_len + offsets
    key_pos = source * block_len + offsets
    query_start = position * block_len
    key_start = jnp.maximum(source, 0) * block_len
    query_seg = lax.dynamic_slice_in_dim(segments, query_start, block_len, 1)
    key_seg = lax.dynamic_slice_in_dim(segments, key_start, block_len, 1)
    same_doc = (query_seg[:, :, None] == key_seg[:, None, :]) & (source >= 0)
    earlier = key_pos[None, :] < query_pos[:, None]
    reached = key_pos[None, :] <= query_pos[:, None]
    return (same_doc & reached[None], same_doc & earlier[None])


def block_logits(queries, key_heads, carried, segments, position, source, offset):
    block_len = queries.shape[1]
    scores = jnp.einsum(
        "rqhd,rkhd->rhqk", queries, key_heads, preferred_element_type=jnp.float32
    ) * (1.0 / math.sqrt(HD))
    attend_mask, select_mask = block_masks(segments, position, source, block_len)
    chosen = jnp.where(select_mask, jax.nn.softplus(scores[:, 0] - offset), 0.0)
    running = running_sums(chosen)
    penalty = carried[:, None, :] + running - chosen
    logits = jnp.where(attend_mask[:, None], scores - penalty[:, None], MASKED)
    return (scores, logits, attend_mask, select_mask, carried + running[:, -1])


def ring_body(tokens, segments, w_qkv, w_out, w_up, w_down, gain_attn, gain_mlp, cotangent):
    low_pieces = (
        w_qkv.astype(jnp.bfloat16),
        w_out.astype(jnp.bfloat16),
        w_up.astype(jnp.bfloat16),
        w_down.astype(jnp.bfloat16),
        gain_attn.astype(jnp.bfloat16),
        gain_mlp.astype(jnp.bfloat16),
    )
    gathered = (
        lax.all_gather(low_pieces[0], ("row", "seq"), axis=0, tiled=True),
        lax.all_gather(low_pieces[1], ("row", "seq"), axis=0, tiled=True),
        lax.all_gather(low_pieces[2], ("row", "seq"), axis=0, tiled=True),
        lax.all_gather(low_pieces[3], ("row", "seq"), axis=0, tiled=True),
        lax.all_gather(low_pieces[4], ("row", "seq"), axis=0, tiled=True),
        lax.all_gather(low_pieces[5], ("row", "seq"), axis=0, tiled=True),
    )
    qkv_full, out_full, up_full, down_full, attn_scale, mlp_scale = gathered
    row_count, block_len, features = tokens.shape
    token_count = row_count * block_len
    position = lax.axis_index("seq")
    sections = lax.axis_size("seq")
    offset = math.log(ROW_LEN / 2.0) + 0.5
    inputs = tokens.astype(jnp.float32).reshape(token_count, features)
    normed, attn_norm_back = jax.vjp(layer_norm, inputs, attn_scale.astype(jnp.float32))
    normed_low = normed.astype(jnp.bfloat16)
    packed = jnp.dot(normed_low, qkv_full, preferred_element_type=jnp.float32).astype(jnp.bfloat16)
    packed = packed.reshape(row_count, block_len, 3 * features)
    queries = packed[:, :, :features].reshape(row_count, block_len, H, HD)
    key_value = packed[:, :, features:]
    carried = jnp.zeros((row_count, block_len), jnp.float32)
    running_max = jnp.full((row_count, H, block_len), MASKED, jnp.float32)
    running_sum = jnp.zeros((row_count, H, block_len), jnp.float32)
    accumulated = jnp.zeros((row_count, block_len, H, HD), jnp.float32)
    kept_pairs = []
    kept_sums = []
    for section in range(sections):
        source = position - section
        key_heads = key_value[:, :, :features].reshape(row_count, block_len, H, HD)
        value_heads = key_value[:, :, features:].reshape(row_count, block_len, H, HD)
        scores, logits, attend_mask, select_mask, passed = block_logits(
            queries, key_heads, carried, segments, position, source, offset
        )
        kept_pairs.append(key_value)
        kept_sums.append(carried)
        new_max = jnp.maximum(running_max, jnp.max(logits, axis=-1))
        rescale = jnp.exp(running_max - new_max)
        exp_scores = jnp.where(attend_mask[:, None], jnp.exp(logits - new_max[..., None]), 0.0)
        running_sum = running_sum * rescale + jnp.sum(exp_scores, axis=-1)
        accumulated = accumulated * jnp.transpose(rescale, (0, 2, 1))[..., None] + jnp.einsum(
            "rhqk,rkhd->rqhd",
            exp_scores.astype(jnp.bfloat16),
            value_heads,
            preferred_element_type=jnp.float32,
        )
        running_max = new_max
        if section + 1 < sections:
            key_value = from_behind(key_value, "seq", 1)
            carried = from_behind(passed, "seq", 1)
    log_norm = running_max + jnp.log(running_sum)
    attn_heads = accumulated / jnp.transpose(running_sum, (0, 2, 1))[..., None]
    mixed_low = attn_heads.reshape(token_count, features).astype(jnp.bfloat16)
    branch = jnp.dot(mixed_low, out_full, preferred_element_type=jnp.float32)
    middle = inputs + branch
    normed_mlp, mlp_norm_back = jax.vjp(layer_norm, middle, mlp_scale.astype(jnp.float32))
    normed_mlp_low = normed_mlp.astype(jnp.bfloat16)
    hidden = jnp.dot(normed_mlp_low, up_full, preferred_element_type=jnp.float32)
    active, gelu_back = jax.vjp(partial(jax.nn.gelu, approximate=False), hidden)
    active_low = active.astype(jnp.bfloat16)
    output = (middle + jnp.dot(active_low, down_full, preferred_element_type=jnp.float32)).astype(
        jnp.bfloat16
    )
    output = output.reshape(row_count, block_len, features)
    upstream = cotangent.reshape(token_count, features)
    grad_down = jnp.dot(active_low.T, upstream, preferred_element_type=jnp.float32)
    d_active = jnp.dot(upstream, down_full.T, preferred_element_type=jnp.float32)
    d_hidden = gelu_back(d_active)[0].astype(jnp.bfloat16)
    grad_up = jnp.dot(normed_mlp_low.T, d_hidden, preferred_element_type=jnp.float32)
    d_normed_mlp = jnp.dot(d_hidden, up_full.T, preferred_element_type=jnp.float32)
    d_middle_part, grad_mlp_gain = mlp_norm_back(d_normed_mlp)
    d_middle = upstream.astype(jnp.float32) + d_middle_part
    d_branch = d_middle.astype(jnp.bfloat16)
    grad_out = jnp.dot(mixed_low.T, d_branch, preferred_element_type=jnp.float32)
    d_mixed = jnp.dot(d_branch, out_full.T, preferred_element_type=jnp.float32).astype(jnp.bfloat16)
    d_mixed = d_mixed.reshape(row_count, block_len, H, HD)
    correction = jnp.transpose(
        jnp.sum(d_mixed.astype(jnp.float32) * attn_heads, axis=-1), (0, 2, 1)
    )
    score_scale = 1.0 / math.sqrt(HD)
    grads_pair = jnp.zeros((row_count, block_len, 2 * features), jnp.float32)
    grads_column = jnp.zeros((row_count, block_len), jnp.float32)
    grad_query = jnp.zeros((row_count, block_len, H, HD), jnp.float32)
    for section in reversed(range(sections)):
        source = position - section
        key_value = kept_pairs[section]
        key_heads = key_value[:, :, :features].reshape(row_count, block_len, H, HD)
        value_heads = key_value[:, :, features:].reshape(row_count, block_len, H, HD)
        scores, logits, attend_mask, select_mask, unused = block_logits(
            queries, key_heads, kept_sums[section], segments, position, source, offset
        )
        attention = jnp.where(attend_mask[:, None], jnp.exp(logits - log_norm[..., None]), 0.0)
        attention_low = attention.astype(jnp.bfloat16)
        grad_values = jnp.einsum(
            "rhqk,rqhd->rkhd", attention_low, d_mixed, preferred_element_type=jnp.float32
        )
        grad_attention = jnp.einsum(
            "rqhd,rkhd->rhqk", d_mixed, value_heads, preferred_element_type=jnp.float32
        )
        grad_logits = attention * (grad_attention - correction[..., None])
        summed = jnp.sum(grad_logits, axis=1)
        column = jnp.sum(summed, axis=1)
        running = running_sums(summed)
        grad_chosen = jnp.where(
            select_mask, running - column[:, None, :] - grads_column[:, None, :], 0.0
        )
        grad_scores = grad_logits.at[:, 0].add(grad_chosen * jax.nn.sigmoid(scores[:, 0] - offset))
        grad_scores = grad_scores.astype(jnp.bfloat16)
        grad_query = (
            grad_query
            + jnp.einsum(
                "rhqk,rkhd->rqhd", grad_scores, key_heads, preferred_element_type=jnp.float32
            )
            * score_scale
        )
        grad_keys = (
            jnp.einsum("rhqk,rqhd->rkhd", grad_scores, queries, preferred_element_type=jnp.float32)
            * score_scale
        )
        grads_pair = grads_pair + jnp.concatenate(
            [
                grad_keys.reshape(row_count, block_len, features),
                grad_values.reshape(row_count, block_len, features),
            ],
            axis=-1,
        )
        grads_column = grads_column + column
        if section > 0:
            grads_pair, grads_column = (
                from_behind(grads_pair.astype(jnp.bfloat16), "seq", -1).astype(grads_pair.dtype),
                from_behind(grads_column.astype(jnp.bfloat16), "seq", -1).astype(
                    grads_column.dtype
                ),
            )
    d_packed = jnp.concatenate(
        [grad_query.reshape(token_count, features), grads_pair.reshape(token_count, 2 * features)],
        axis=-1,
    )
    d_packed = d_packed.astype(jnp.bfloat16)
    grad_qkv = jnp.dot(normed_low.T, d_packed, preferred_element_type=jnp.float32)
    d_normed = jnp.dot(d_packed, qkv_full.T, preferred_element_type=jnp.float32)
    d_inputs_part, grad_attn_gain = attn_norm_back(d_normed)
    d_tokens = (d_middle + d_inputs_part).reshape(row_count, block_len, features)
    gradients = (grad_qkv, grad_out, grad_up, grad_down, grad_attn_gain, grad_mlp_gain)
    reduced = (
        lax.psum_scatter(gradients[0], ("row", "seq"), scatter_dimension=0, tiled=True),
        lax.psum_scatter(gradients[1], ("row", "seq"), scatter_dimension=0, tiled=True),
        lax.psum_scatter(gradients[2], ("row", "seq"), scatter_dimension=0, tiled=True),
        lax.psum_scatter(gradients[3], ("row", "seq"), scatter_dimension=0, tiled=True),
        lax.psum_scatter(gradients[4], ("row", "seq"), scatter_dimension=0, tiled=True),
        lax.psum_scatter(gradients[5], ("row", "seq"), scatter_dimension=0, tiled=True),
    )
    return (
        output,
        d_tokens,
        reduced[0],
        reduced[1],
        reduced[2],
        reduced[3],
        reduced[4],
        reduced[5],
    )


def body(tokens, *rest):
    rows = lax.axis_size("row")
    if lax.axis_size("seq") == 2 and tokens.shape[0] == 2 and rows >= 4 and rows & (rows - 1) == 0:
        return row_body(tokens, *rest)
    return ring_body(tokens, *rest)


def solution(mesh):
    placed = (
        P("row", "seq", None),
        P("row", None),
        P(("row", "seq"), None),
        P(("row", "seq"), None),
        P(("row", "seq"), None),
        P(("row", "seq"), None),
        P(("row", "seq")),
        P(("row", "seq")),
        P("row", "seq", None),
    )
    return jax.shard_map(
        body,
        mesh=mesh,
        in_specs=placed,
        out_specs=(
            P("row", "seq", None),
            P("row", "seq", None),
            P(("row", "seq"), None),
            P(("row", "seq"), None),
            P(("row", "seq"), None),
            P(("row", "seq"), None),
            P(("row", "seq")),
            P(("row", "seq")),
        ),
        check_vma=False,
    )
```

```python
from functools import partial
import math

import jax
import jax.numpy as jnp
from jax import lax
from jax.experimental import pallas as pl
from jax.experimental.pallas import tpu as pltpu
from jax.sharding import PartitionSpec as P

H = 12
HD = 64
ROW_LEN = 2048
EPSILON = 1e-05
MASKED = -1e30
BIG = 1e30
LOG2E = 1.4426950408889634
OFFSET = math.log(ROW_LEN / 2.0) + 0.5
SAFE = 64.0
B = 256
BT = 512
MIB = 2**20
F32 = jnp.float32
BF = jnp.bfloat16


def dot(a, b):
    return jnp.dot(a, b, preferred_element_type=F32)


def dot_nt(a, b):
    return lax.dot_general(a, b, (((1,), (1,)), ((), ())), preferred_element_type=F32)


def dot_tn(a, b):
    return lax.dot_general(a, b, (((0,), (0,)), ((), ())), preferred_element_type=F32)


def iota(shape, dim):
    return lax.broadcasted_iota(jnp.int32, shape, dim)


def half_lanes(rows):
    return iota((rows, 128), 1) < HD


def pick_columns(c):
    return (iota((512, 128), 0) == 4 * iota((512, 128), 1) + c).astype(F32).astype(BF)


def pick_rows(piece, c):
    return (iota((piece, 4 * piece), 1) == 4 * iota((piece, 4 * piece), 0) + c).astype(F32).astype(BF)


def pack_kernel(qkv_ref, out_ref, up_ref, down_ref, ga_ref, gm_ref, a_ref, b_ref, l_ref):
    piece, features = out_ref.shape
    lane = iota((piece, 128), 1)
    a_ref[...] = qkv_ref[:, : 2 * features].astype(BF)
    b_ref[:, :features] = qkv_ref[:, 2 * features :].astype(BF)
    gains = jnp.where(lane == 0, ga_ref[...], jnp.where(lane == 1, gm_ref[...], 0.0))
    b_ref[:, features:] = gains.astype(BF)
    l_ref[:, :features] = out_ref[...].astype(BF)
    for c in range(4):
        pick = pick_columns(c)
        col = features * (1 + c)
        for tile in range(features // 128):
            part = up_ref[:, 512 * tile : 512 * tile + 512].astype(BF)
            l_ref[:, col + 128 * tile : col + 128 * tile + 128] = dot(part, pick).astype(BF)
        col = features * (5 + c)
        l_ref[:, col : col + features] = dot(pick_rows(piece, c), down_ref[...].astype(BF)).astype(BF)


def pack(w_qkv, w_out, w_up, w_down, gain_attn, gain_mlp):
    piece, features = w_out.shape
    return pl.pallas_call(
        pack_kernel,
        out_shape=[
            jax.ShapeDtypeStruct((piece, cols), BF) for cols in (2 * features, features + 128, 9 * features)
        ],
        name="pack_weights",
    )(w_qkv, w_out, w_up, w_down, gain_attn[:, None], gain_mlp[:, None])


def unpack_kernel(b_ref, out_ref, up_ref, down_ref):
    piece, features = out_ref.shape
    out_ref[...] = b_ref[:, :features].astype(F32)
    for tile in range(features // 128):
        total = None
        for c in range(4):
            col = features * (1 + c) + 128 * tile
            part = dot_nt(b_ref[:, col : col + 128], pick_columns(c))
            total = part if total is None else total + part
        up_ref[:, 512 * tile : 512 * tile + 512] = total
    total = None
    for c in range(4):
        col = features * (5 + c)
        part = dot_tn(pick_rows(piece, c), b_ref[:, col : col + features])
        total = part if total is None else total + part
    down_ref[...] = total


def unpack(buffer):
    piece = buffer.shape[0]
    features = (buffer.shape[1] - 128) // 9
    return pl.pallas_call(
        unpack_kernel,
        out_shape=(
            jax.ShapeDtypeStruct((piece, features), F32),
            jax.ShapeDtypeStruct((piece, 4 * features), F32),
            jax.ShapeDtypeStruct((4 * piece, features), F32),
        ),
        name="unpack_gradients",
    )(buffer)


def moments(values):
    mean_value = jnp.mean(values, axis=-1, keepdims=True)
    shifted = values - mean_value
    spread = jnp.mean(shifted * shifted, axis=-1, keepdims=True)
    return shifted, lax.rsqrt(spread + EPSILON)


def pick_half(own_ref, other_ref, step, steps):
    return jnp.where(step < steps // 2, own_ref[...], other_ref[...])


def halves(cols, steps):
    return (
        pl.BlockSpec((BT, cols), lambda t: (jnp.minimum(t, steps // 2 - 1), 0)),
        pl.BlockSpec((BT, cols), lambda t: (jnp.maximum(t - steps // 2, 0), 0)),
    )


def qkv_kernel(x_ref, other_ref, w_ref, v_w_ref, q_ref, k_ref, v_ref, rows_ref, size_ref):
    features = x_ref.shape[1]

    @pl.when(pl.program_id(0) == 0)
    def _():
        rows_ref[...] = v_w_ref[:, features:].astype(F32).T[:8]
        size_ref[...] = jnp.zeros_like(size_ref)

    shifted, scale = moments(pick_half(x_ref, other_ref, pl.program_id(0), pl.num_programs(0)).astype(F32))
    normed = (shifted * scale * rows_ref[0:1, :]).astype(BF)
    low = half_lanes(x_ref.shape[0])
    heads = (iota((features, 128), 0) // HD == iota((features, 128), 1)).astype(F32).astype(BF)

    def spread(ref, packed, other):
        for p in range(H // 2):
            pair = packed[:, 128 * p : 128 * p + 128]
            ref[:, 256 * p : 256 * p + 128] = jnp.where(low, pair, other).astype(BF)
            ref[:, 256 * p + 128 : 256 * p + 256] = jnp.where(low, other, pair).astype(BF)

    def measure(row, value):
        most = jnp.max(dot((value * value).astype(BF), heads), axis=0, keepdims=True)
        size_ref[row : row + 1] = jnp.maximum(size_ref[row : row + 1], most)

    q = dot(normed, w_ref[:, :features]) * (LOG2E / math.sqrt(HD))
    spread(q_ref, q, 0.0)
    measure(0, q)
    k = dot(normed, w_ref[:, features:])
    spread(k_ref, k, 1.0)
    measure(1, k)
    spread(v_ref, dot(normed, v_w_ref[:, :features]), 1.0)


def project_qkv(own, other, w_qk, w_v):
    tokens, features = 2 * own.shape[0], own.shape[1]
    steps = tokens // BT

    def tall(cols):
        return pl.BlockSpec((BT, cols), lambda t: (t, 0))

    def whole(array):
        return pl.BlockSpec(array.shape, lambda t: (0, 0))

    return pl.pallas_call(
        qkv_kernel,
        grid=(steps,),
        in_specs=[*halves(features, steps), whole(w_qk), whole(w_v)],
        out_specs=[
            tall(2 * features),
            tall(2 * features),
            tall(2 * features),
            pl.BlockSpec((8, features), lambda t: (0, 0)),
            pl.BlockSpec((8, 128), lambda t: (0, 0)),
        ],
        out_shape=[
            jax.ShapeDtypeStruct((tokens, 2 * features), BF),
            jax.ShapeDtypeStruct((tokens, 2 * features), BF),
            jax.ShapeDtypeStruct((tokens, 2 * features), BF),
            jax.ShapeDtypeStruct((8, features), F32),
            jax.ShapeDtypeStruct((8, 128), F32),
        ],
        compiler_params=pltpu.CompilerParams(vmem_limit_bytes=48 * MIB),
        name="project_qkv",
    )(own, other, w_qk, w_v)


def pick(h):
    return slice(128 * h, 128 * h + 128)


def block_rows(index):
    return pl.ds(pl.multiple_of(index * B, B), B)


def two_part(tri, values):
    high = values.astype(BF)
    rest = (values - high.astype(F32)).astype(BF)
    return dot(tri, high) + dot(tri, rest)


def selection(scores, segq, segk, rows, cols):
    earlier = (segq == segk) & (cols < rows)
    x = scores - OFFSET * LOG2E
    grown = jnp.exp2(jnp.minimum(x, 100.0))
    more = 1.0 + grown
    return jnp.where(earlier, jnp.maximum(x, jnp.log2(more)), 0.0), jnp.where(earlier, grown / more, 0.0)


def mixed(first, second):
    done = 0
    for n, step in enumerate(first):
        step()
        upto = (n + 1) * len(second) // len(first)
        for other in second[done:upto]:
            other()
        done = upto


STRIP = 64
LEAD = 2


def key_copies(block, stored, k_any, v_any, kx, vx, sem):
    rows = block_rows(stored)
    return (
        pltpu.make_async_copy(k_any.at[rows, :], kx.at[block], sem.at[0, block]),
        pltpu.make_async_copy(v_any.at[rows, :], vx.at[block], sem.at[1, block]),
    )


def forward_kernel(tab, slow, q_ref, q0_ref, k0_ref, segq_ref, segk_ref, k_any, v_any, o_ref, li_ref, e_ref,
                   acc, carry, tri, qx, penalty, gate, work, high, kx, vx, sem):
    t = pl.program_id(0)
    ib, jb = tab[2, t], tab[3, t]

    @pl.when(t == 0)
    def _():
        for block in range(kx.shape[0]):
            for copy in key_copies(block, tab[1, block * (block + 3) // 2], k_any, v_any, kx, vx, sem):
                copy.start()

    def prepare(step, slot):
        keys = block_rows(tab[1, step])
        at = tab[3, step]
        ahead = (tab[2, step] - at) * B
        segk = segk_ref[tab[1, step], 0:1, :]
        sums = []

        def scores():
            work[...] = dot_nt(q0_ref[block_rows(tab[0, step]), :], k0_ref[keys, :])

        def strip(n):
            part = slice(STRIP * n, STRIP * n + STRIP)
            segq = segq_ref[pl.ds(pl.multiple_of(tab[0, step] * B + STRIP * n, STRIP), STRIP), :]
            return part, segq, iota((STRIP, B), 0) + (ahead + STRIP * n), iota((STRIP, B), 1)

        def choose(n):
            part, segq, rows, cols = strip(n)
            chosen, opened = selection(work[part, :], segq, segk, rows, cols)
            gate[slot, part, :] = opened.astype(BF)
            high[part, :] = chosen.astype(BF)
            sums.append(jnp.sum(chosen, axis=0, keepdims=True))

        def add():
            before = carry[at, 0:1, :]
            work[...] = dot(tri[...], high[...]) + before
            carry[at, 0:1, :] = before + sum(sums[1:], sums[0])

        def close(n):
            part, segq, rows, cols = strip(n)
            penalty[slot, part, :] = jnp.where((segq == segk) & (cols <= rows), work[part, :], BIG)

        count = range(B // STRIP)
        return [scores] + [partial(choose, n) for n in count] + [add] + [partial(close, n) for n in count]

    @pl.when(t == 0)
    def _():
        carry[...] = jnp.zeros_like(carry)
        tri[...] = (iota((B, B), 1) < iota((B, B), 0)).astype(F32).astype(BF)
        for step in prepare(0, 0):
            step()

    @pl.when(jb == 0)
    def _():
        acc[...] = jnp.zeros_like(acc)
        qx[...] = q_ref[...]
        for copy in key_copies(ib, tab[0, t], k_any, v_any, kx, vx, sem):
            copy.wait()

        @pl.when(slow[0] != 0)
        def _():
            lane = iota((B, 128), 1)
            segq = segq_ref[block_rows(tab[0, t]), :]
            cols = iota((B, B), 1)

            def chosen(other):
                rows = iota((B, B), 0) + (ib - other) * B
                base = tab[1, t + other]
                first = dot_nt(q_ref[:, 0:128], k0_ref[block_rows(base), :])
                return selection(first, segq, segk_ref[base, 0:1, :], rows, cols)[0]

            own = jnp.sum(chosen(0), axis=0, keepdims=True)

            def step(other, top):
                base = tab[1, t + other]
                before = carry[other, 0:1, :] - jnp.where(other == 0, own, 0.0)
                kept = (segq == segk_ref[base, 0:1, :]) & (cols <= iota((B, B), 0) + (ib - other) * B)
                z_penalty = jnp.where(kept, dot(tri[...], chosen(other).astype(BF)) + before, BIG)
                for h in range(H):
                    z = dot_nt(q_ref[:, pick(h)], kx[other, :, pick(h)]) - z_penalty
                    top = jnp.where(lane == h, jnp.maximum(top, jnp.max(z, axis=1, keepdims=True)), top)
                return top

            top = lax.fori_loop(0, ib + 1, step, jnp.full((B, 128), -BIG, F32))
            for h in range(H):
                shift = -jnp.sum(jnp.where(lane == h, top, 0.0), axis=1, keepdims=True)
                one = shift.astype(BF).astype(F32)
                two = (shift - one).astype(BF).astype(F32)
                three = shift - one - two
                at = lane - (HD if h % 2 == 0 else 0)
                extra = jnp.where(at == 0, one, jnp.where(at == 1, two, jnp.where(at == 2, three, 0.0)))
                keep = (lane < HD) if h % 2 == 0 else (lane >= HD)
                qx[:, pick(h)] = jnp.where(keep, q_ref[:, pick(h)].astype(F32), extra).astype(BF)

    slot = t % 2

    def head(h):
        e = jnp.exp2(dot_nt(qx[:, pick(h)], kx[jb, :, pick(h)]) - penalty[slot]).astype(BF)
        e_ref[0, h] = e

    def value(h):
        acc[:, pick(h)] += dot(e_ref[0, h], vx[jb, :, pick(h)])

    e_ref[0, H] = gate[slot]
    steps = [partial(head, h) for h in range(LEAD)]
    for h in range(H):
        if h + LEAD < H:
            steps.append(partial(head, h + LEAD))
        steps.append(partial(value, h))
    mixed(steps, prepare(t + 1, 1 - slot))

    @pl.when(jb == ib)
    def _():
        low = half_lanes(B)
        for p in range(H // 2):
            one = acc[:, pick(2 * p)]
            two = acc[:, pick(2 * p + 1)]
            inverse = 1.0 / pltpu.roll(jnp.where(low, two, one), HD, 1)
            o_ref[:, pick(p)] = (jnp.where(low, one, two) * inverse).astype(BF)
            li_ref[:, pick(p)] = inverse


def attention_forward(table, slow, q, k, v, seg_col, seg_row):
    tokens = q.shape[0]
    blocks = tokens // B
    tiles = table.shape[1] - 1
    wide = 128 * H
    narrow = HD * H
    once = pl.Buffered(1)
    return pl.pallas_call(
        forward_kernel,
        grid_spec=pltpu.PrefetchScalarGridSpec(
            num_scalar_prefetch=2,
            grid=(tiles,),
            in_specs=[
                pl.BlockSpec((B, wide), lambda t, tab, slow: (tab[0, t], 0)),
                pl.BlockSpec((tokens, 128), lambda t, tab, slow: (0, 0), pipeline_mode=once),
                pl.BlockSpec((tokens, 128), lambda t, tab, slow: (0, 0), pipeline_mode=once),
                pl.BlockSpec((tokens, 1), lambda t, tab, slow: (0, 0), pipeline_mode=once),
                pl.BlockSpec((blocks, 8, B), lambda t, tab, slow: (0, 0, 0), pipeline_mode=once),
                pl.BlockSpec(memory_space=pl.ANY),
                pl.BlockSpec(memory_space=pl.ANY),
            ],
            out_specs=[
                pl.BlockSpec((B, narrow), lambda t, tab, slow: (tab[0, t], 0)),
                pl.BlockSpec((B, narrow), lambda t, tab, slow: (tab[0, t], 0)),
                pl.BlockSpec((1, H + 1, B, B), lambda t, tab, slow: (tab[4, t], 0, 0, 0)),
            ],
            scratch_shapes=[
                pltpu.VMEM((B, wide), F32),
                pltpu.VMEM((blocks, 8, B), F32),
                pltpu.VMEM((B, B), BF),
                pltpu.VMEM((B, wide), BF),
                pltpu.VMEM((2, B, B), F32),
                pltpu.VMEM((2, B, B), BF),
                pltpu.VMEM((B, B), F32),
                pltpu.VMEM((B, B), BF),
                pltpu.VMEM((blocks, B, wide), BF),
                pltpu.VMEM((blocks, B, wide), BF),
                pltpu.SemaphoreType.DMA((2, blocks)),
            ],
        ),
        out_shape=[
            jax.ShapeDtypeStruct((tokens, narrow), BF),
            jax.ShapeDtypeStruct((tokens, narrow), F32),
            jax.ShapeDtypeStruct((tiles, H + 1, B, B), BF),
        ],
        compiler_params=pltpu.CompilerParams(vmem_limit_bytes=48 * MIB),
        name="attention_forward",
    )(table, slow, q, q, k, seg_col, seg_row, k, v)


def backward_kernel(tab, e_ref, q_ref, d_ref, q0_ref, k0_ref, k_any, v_any, o_ref,
                    dq, dkt, dvt, carry, tri, sums, first, gate, work, kx, vx, sem):
    t = pl.program_id(0)
    last = pl.num_programs(0) - 1
    before = jnp.maximum(t - 1, 0)
    narrow = HD * H
    low = half_lanes(B)
    slot = t % 2

    @pl.when(t == 0)
    def _():
        for block in range(kx.shape[0]):
            for copy in key_copies(block, tab[1, block], k_any, v_any, kx, vx, sem):
                copy.start()
        carry[...] = jnp.zeros_like(carry)
        tri[...] = (iota((B, B), 1) > iota((B, B), 0)).astype(F32).astype(BF)
        dkt[...] = jnp.zeros_like(dkt)
        dvt[...] = jnp.zeros_like(dvt)
        dq[...] = jnp.zeros_like(dq)
        sums[...] = jnp.zeros_like(sums)
        first[...] = jnp.zeros_like(first)
        gate[...] = jnp.zeros_like(gate)

    @pl.when((tab[3, t] == 0) & (t < last))
    def _():
        dq[tab[2, t] % 2] = jnp.zeros(dq.shape[1:], F32)

    @pl.when(t < kx.shape[0])
    def _():
        for copy in key_copies(t, tab[1, t], k_any, v_any, kx, vx, sem):
            copy.wait()

    def finish():
        at = tab[3, before]

        def add():
            total = sums[1 - slot]
            later = carry[at, 0:1, :] + two_part(tri[...], total)
            carry[at, 0:1, :] = carry[at, 0:1, :] + jnp.sum(total, axis=0, keepdims=True)
            work[...] = (first[1 - slot] - later * gate[1 - slot].astype(F32)).astype(BF)

        def keys():
            dkt[:HD, block_rows(at)] += dot_tn(q0_ref[block_rows(tab[0, before]), :], work[...])[:HD]

        def queries():
            more = dot(work[...], k0_ref[block_rows(tab[1, before]), :])
            dq[tab[2, before] % 2, :, :128] += jnp.where(low, more, 0.0)

        return [add, keys, queries]

    @pl.when(t == last)
    def _():
        for step in finish():
            step()

    @pl.when(t < last)
    def _():
        cols = block_rows(tab[3, t])
        turn = tab[2, t] % 2
        kept = {}
        parts = {}

        def score(h):
            e = e_ref[0, h]
            dz = e.astype(F32) * dot_nt(d_ref[:, pick(h)], vx[tab[3, t], :, pick(h)])
            if h == 0:
                first[slot] = dz
                sums[slot] = dz
            else:
                sums[slot] += dz
                kept[h] = dz.astype(BF)

        def products(h):
            own = slice(HD * h, HD * h + HD)
            data = slice(HD * (h % 2), HD * (h % 2) + HD)
            dvt[own, cols] += dot_tn(d_ref[:, pick(h)], e_ref[0, h])[data]
            if h == 0:
                parts[0] = 0.0
                return
            ds = kept.pop(h)
            dkt[own, cols] += dot_tn(q_ref[:, pick(h)], ds)[data]
            parts[h] = dot(ds, kx[tab[3, t], :, pick(h)])
            if h % 2:
                dq[turn, :, pick(h // 2)] += jnp.where(low, parts.pop(h - 1), parts.pop(h))

        gate[slot] = e_ref[0, H]
        steps = [partial(score, h) for h in range(LEAD)]
        for h in range(H):
            if h + LEAD < H:
                steps.append(partial(score, h + LEAD))
            steps.append(partial(products, h))
        mixed(steps, finish())

    @pl.when((t > 0) & (tab[3, before] == tab[2, before]))
    def _():
        cols = block_rows(tab[2, before])
        o_ref[:, :narrow] = (dq[tab[2, before] % 2] * (1.0 / math.sqrt(HD))).astype(BF)
        o_ref[:, narrow : 2 * narrow] = (dkt[:, cols] * (1.0 / LOG2E)).astype(BF).T
        o_ref[:, 2 * narrow :] = dvt[:, cols].astype(BF).T


def attention_backward(table, e, q, k, v, d):
    tokens = q.shape[0]
    blocks = tokens // B
    tiles = table.shape[1] - 1
    wide = 128 * H
    narrow = HD * H
    once = pl.Buffered(1)
    return pl.pallas_call(
        backward_kernel,
        grid_spec=pltpu.PrefetchScalarGridSpec(
            num_scalar_prefetch=1,
            grid=(tiles + 1,),
            in_specs=[
                pl.BlockSpec((1, H + 1, B, B), lambda t, tab: (tab[4, t], 0, 0, 0)),
                pl.BlockSpec((B, wide), lambda t, tab: (tab[0, t], 0)),
                pl.BlockSpec((B, wide), lambda t, tab: (tab[0, t], 0)),
                pl.BlockSpec((tokens, 128), lambda t, tab: (0, 0), pipeline_mode=once),
                pl.BlockSpec((tokens, 128), lambda t, tab: (0, 0), pipeline_mode=once),
                pl.BlockSpec(memory_space=pl.ANY),
                pl.BlockSpec(memory_space=pl.ANY),
            ],
            out_specs=pl.BlockSpec((B, 3 * narrow), lambda t, tab: (tab[0, jnp.maximum(t - 1, 0)], 0)),
            scratch_shapes=[
                pltpu.VMEM((2, B, narrow), F32),
                pltpu.VMEM((narrow, tokens), F32),
                pltpu.VMEM((narrow, tokens), F32),
                pltpu.VMEM((blocks, 8, B), F32),
                pltpu.VMEM((B, B), BF),
                pltpu.VMEM((2, B, B), F32),
                pltpu.VMEM((2, B, B), F32),
                pltpu.VMEM((2, B, B), BF),
                pltpu.VMEM((B, B), BF),
                pltpu.VMEM((blocks, B, wide), BF),
                pltpu.VMEM((blocks, B, wide), BF),
                pltpu.SemaphoreType.DMA((2, blocks)),
            ],
        ),
        out_shape=jax.ShapeDtypeStruct((tokens, 3 * narrow), BF),
        compiler_params=pltpu.CompilerParams(vmem_limit_bytes=56 * MIB),
        cost_estimate=pl.CostEstimate(flops=tiles * H * B * B * 1024, bytes_accessed=tiles * B * B, transcendentals=0),
        name="attention_backward",
    )(table, e, q, d, q, k, k, v)


def tile_tables(blocks, position):
    pairs = [(i, j) for i in range(blocks) for j in range(i + 1)]
    back = [(i, j) for i in reversed(range(blocks)) for j in range(i + 1)]
    shift = position * (blocks // 2)

    def table(order):
        order = order + order[-1:]
        rows = jnp.array([i for i, _ in order], jnp.int32)
        keys = jnp.array([j for _, j in order], jnp.int32)
        return jnp.stack(
            [(rows + shift) % blocks, (keys + shift) % blocks, rows, keys, rows * (rows + 1) // 2 + keys]
        )

    return table(pairs), table(back)


PART = 256
ROWS = 64


def mlp_kernel(x_ref, x2_ref, ob_ref, dy1_ref, dy2_ref, li_ref, gain_ref, wo_ref, wu_ref, wd_ref, out_ref, dx_ref, d_ref, g_any,
               xh, scales, y, dn, n2, gup, gdown, gout, gsum, stage, us, das, actives, dus, sem):
    c, t = pl.program_id(0), pl.program_id(1)
    chunks, steps = pl.num_programs(0), pl.num_programs(1)
    rows = pl.ds(pl.multiple_of(t * BT, BT), BT)
    features = x_ref.shape[1]

    def send(slot, column):
        start = pl.multiple_of(column, 128)
        return pltpu.make_async_copy(stage.at[slot], g_any.at[:, pl.ds(start, features)], sem.at[slot])

    @pl.when(c == 0)
    def _():
        middle = pick_half(x_ref, x2_ref, t, steps).astype(F32) + dot(ob_ref[...], wo_ref[...])
        shifted, scale = moments(middle)
        xh[rows, :] = (shifted * scale).astype(BF)
        scales[rows, :] = jnp.broadcast_to(scale, (BT, 128))
        y[rows, :] = middle
        dn[rows, :] = jnp.zeros_like(middle)
        n2[rows, :] = (shifted * scale * gain_ref[1:2, :]).astype(BF)

    @pl.when(t == 0)
    def _():
        gup[...] = jnp.zeros_like(gup)
        gdown[...] = jnp.zeros_like(gdown)

    @pl.when((c == 0) & (t == 0))
    def _():
        gout[...] = jnp.zeros_like(gout)
        gsum[...] = jnp.zeros_like(gsum)

    n2_low = n2[rows, :]
    dy_low = pick_half(dy1_ref, dy2_ref, t, steps)

    def enter(p):
        units = slice(PART * p, PART * p + PART)

        def up():
            us[p % 2] = dot(n2_low, wu_ref[:, units])

        def down():
            das[p % 2] = dot_nt(dy_low, wd_ref[units, :])

        return [up, down]

    def bend(p, n):
        part = slice(ROWS * n, ROWS * n + ROWS)
        u = us[p % 2, part, :]
        cdf = 0.5 * (1.0 + lax.erf(u * math.sqrt(0.5)))
        density = jnp.exp(-0.5 * u * u) * (1.0 / math.sqrt(2.0 * math.pi))
        units = slice(PART * p, PART * p + PART)
        actives[part, units] = (u * cdf).astype(BF)
        dus[part, units] = ((cdf + u * density) * das[p % 2, part, :]).astype(BF)

    def leave(p):
        units = slice(PART * p, PART * p + PART)

        def down():
            y[rows, :] += dot(actives[:, units], wd_ref[units, :])

        def up():
            dn[rows, :] += dot_nt(dus[:, units], wu_ref[:, units])

        return [down, up]

    parts = features // PART
    for step in enter(0):
        step()
    for p in range(parts):
        products = (leave(p - 1) if p else []) + (enter(p + 1) if p + 1 < parts else [])
        mixed(products, [partial(bend, p, n) for n in range(BT // ROWS)])
    for step in leave(parts - 1):
        step()
    gdown[...] += dot_tn(actives[...], dy_low)
    gup[...] += dot_tn(n2_low, dus[...])

    @pl.when(t == steps - 1)
    def _():
        @pl.when(c > 0)
        def _():
            send(0, c * features).wait()
            send(1, (c + chunks) * features).wait()

        stage[0] = gup[...].astype(BF)
        stage[1] = gdown[...].astype(BF)
        send(0, (1 + c) * features).start()
        send(1, (1 + c + chunks) * features).start()

    @pl.when(c == chunks - 1)
    def _():
        out_ref[...] = y[rows, :].astype(BF)
        d_normed = dn[rows, :]
        scale = scales[rows, 0:1]
        unit = xh[rows, :].astype(F32)
        product = d_normed * unit
        gsum[...] += jnp.sum(product.reshape(BT // 8, 8, features), axis=0)
        inner = d_normed * gain_ref[1:2, :]
        dx = dy_low.astype(F32) + scale * (
            inner - jnp.mean(inner, axis=-1, keepdims=True) - unit * jnp.mean(inner * unit, axis=-1, keepdims=True)
        )
        dx_ref[...] = dx.astype(BF)
        db = dx.astype(BF)
        gout[...] += dot_tn(ob_ref[...], db)
        scaled = dot_nt(db, wo_ref[...]) * li_ref[...]
        low = half_lanes(BT)
        lane = iota((BT, 128), 1)
        swap_row, swap_col = iota((128, 128), 0), iota((128, 128), 1)
        swap = ((swap_row // HD != swap_col // HD) & (swap_col % HD < 2)).astype(F32).astype(BF)
        for p in range(H // 2):
            w = slice(128 * p, 128 * p + 128)
            pair = scaled[:, w]
            both = pair * ob_ref[:, w].astype(F32)
            high = both.astype(BF)
            delta = dot(high, swap) + dot((both - high.astype(F32)).astype(BF), swap)
            top = delta.astype(BF).astype(F32)
            extra = jnp.where((lane == 0) | (lane == HD), -top, top - delta)
            d_ref[:, 256 * p : 256 * p + 128] = jnp.where(low, pair, extra).astype(BF)
            d_ref[:, 256 * p + 128 : 256 * p + 256] = jnp.where(low, extra, pair).astype(BF)

    @pl.when((c == chunks - 1) & (t == steps - 1))
    def _():
        stage[2] = gout[...].astype(BF)
        column = jnp.broadcast_to(jnp.sum(gsum[...], axis=0, keepdims=True), (128, features))
        stage[3, :, :128] = column.T.astype(BF)
        last = pltpu.make_async_copy(
            stage.at[3, :, pl.ds(0, 128)], g_any.at[:, pl.ds((1 + 2 * 4) * features, 128)], sem.at[3]
        )
        send(2, 0).start()
        last.start()
        send(0, chunks * features).wait()
        send(1, 2 * chunks * features).wait()
        send(2, 0).wait()
        last.wait()


def feed_forward(x, x_other, ob, dy, dy_other, li, gains, weights):
    tokens, features = ob.shape
    steps = tokens // BT
    chunks = 4

    def ends(c, t):
        return (jnp.where((c == 0) | (c == chunks - 1), t, steps - 1), 0)

    def own(t):
        return jnp.minimum(t, steps // 2 - 1)

    def other(t):
        return jnp.maximum(t - steps // 2, 0)

    def at_last(c, t):
        return (jnp.where(c == chunks - 1, t, 0), 0)

    block = (BT, features)
    once = pl.Buffered(1)
    return pl.pallas_call(
        mlp_kernel,
        grid=(chunks, steps),
        in_specs=[
            pl.BlockSpec(block, lambda c, t: (own(jnp.where(c == 0, t, steps - 1)), 0), pipeline_mode=once),
            pl.BlockSpec(block, lambda c, t: (other(jnp.where(c == 0, t, steps - 1)), 0), pipeline_mode=once),
            pl.BlockSpec(block, ends),
            pl.BlockSpec(block, lambda c, t: (own(t), 0)),
            pl.BlockSpec(block, lambda c, t: (other(t), 0)),
            pl.BlockSpec(block, at_last, pipeline_mode=once),
            pl.BlockSpec((8, features), lambda c, t: (0, 0)),
            pl.BlockSpec((features, features), lambda c, t: (0, 0), pipeline_mode=once),
            pl.BlockSpec((features, features), lambda c, t: (0, 1 + c)),
            pl.BlockSpec((features, features), lambda c, t: (0, 1 + chunks + c)),
        ],
        out_specs=[
            pl.BlockSpec(block, at_last),
            pl.BlockSpec(block, at_last),
            pl.BlockSpec((BT, 2 * features), at_last),
            pl.BlockSpec(memory_space=pl.ANY),
        ],
        out_shape=[
            jax.ShapeDtypeStruct((tokens, features), BF),
            jax.ShapeDtypeStruct((tokens, features), BF),
            jax.ShapeDtypeStruct((tokens, 2 * features), BF),
            jax.ShapeDtypeStruct((features, 9 * features + 128), BF),
        ],
        scratch_shapes=[
            pltpu.VMEM((tokens, features), BF),
            pltpu.VMEM((tokens, 128), F32),
            pltpu.VMEM((tokens, features), F32),
            pltpu.VMEM((tokens, features), F32),
            pltpu.VMEM((tokens, features), BF),
            pltpu.VMEM((features, features), F32),
            pltpu.VMEM((features, features), F32),
            pltpu.VMEM((features, features), F32),
            pltpu.VMEM((8, features), F32),
            pltpu.VMEM((4, features, features), BF),
            pltpu.VMEM((2, BT, PART), F32),
            pltpu.VMEM((2, BT, PART), F32),
            pltpu.VMEM((BT, features), BF),
            pltpu.VMEM((BT, features), BF),
            pltpu.SemaphoreType.DMA((4,)),
        ],
        compiler_params=pltpu.CompilerParams(vmem_limit_bytes=63 * MIB),
        name="feed_forward",
    )(x, x_other, ob, dy, dy_other, li, gains, weights, weights, weights)


def weight_order(bits, dims):
    return [
        sum(((place >> (bits - 1 - n)) & 1) << dim for n, dim in enumerate(dims)) for place in range(2**bits)
    ]


def weight_kernel(x_ref, other_ref, dqkv_ref, gain_ref, a_ref, b_ref, acc, *, orders):
    t = pl.program_id(0)

    @pl.when(t == 0)
    def _():
        acc[...] = jnp.zeros_like(acc)

    shifted, scale = moments(pick_half(x_ref, other_ref, t, pl.num_programs(0)).astype(F32))
    normed = (shifted * scale * gain_ref[0:1, :]).astype(BF)
    acc[...] += dot_tn(normed, dqkv_ref[...])

    @pl.when(t == pl.num_programs(0) - 1)
    def _():
        _, piece, split = a_ref.shape
        for place, block in enumerate(orders[0]):
            a_ref[place] = acc[piece * block : piece * block + piece, :split].astype(BF)
        for place, block in enumerate(orders[1]):
            b_ref[place] = acc[piece * block : piece * block + piece, split:].astype(BF)


def first_weight_gradient(x, x_other, dqkv, gains, orders):
    tokens, features = dqkv.shape[0], x.shape[1]
    steps = tokens // BT
    blocks = len(orders[0])
    shapes = [(blocks, features // blocks, cols) for cols in (2 * features, features)]
    return pl.pallas_call(
        partial(weight_kernel, orders=orders),
        grid=(steps,),
        in_specs=[
            *halves(features, steps),
            pl.BlockSpec((BT, 3 * features), lambda t: (t, 0)),
            pl.BlockSpec(gains.shape, lambda t: (0, 0)),
        ],
        out_specs=[pl.BlockSpec(shape, lambda t: (0, 0, 0)) for shape in shapes],
        out_shape=[jax.ShapeDtypeStruct(shape, BF) for shape in shapes],
        scratch_shapes=[pltpu.VMEM((features, 3 * features), F32)],
        compiler_params=pltpu.CompilerParams(vmem_limit_bytes=48 * MIB),
        cost_estimate=pl.CostEstimate(
            flops=12 * tokens * features * features, bytes_accessed=16 * tokens * features, transcendentals=0
        ),
        name="first_weight_gradient",
    )(x, x_other, dqkv, gains)


def tokens_kernel(x_ref, dqkv_ref, dx_ref, gain_ref, w_ref, v_w_ref, out_ref, gsum_ref):
    features = x_ref.shape[1]

    @pl.when(pl.program_id(0) == 0)
    def _():
        gsum_ref[...] = jnp.zeros_like(gsum_ref)

    shifted, scale = moments(x_ref[...].astype(F32))
    xh = shifted * scale
    d_normed = dot_nt(dqkv_ref[:, : 2 * features], w_ref[...])
    d_normed += dot_nt(dqkv_ref[:, 2 * features :], v_w_ref[:, :features])
    gsum_ref[...] += jnp.sum((d_normed * xh).reshape(BT // 8, 8, features), axis=0)
    inner = d_normed * gain_ref[0:1, :]
    dx = dx_ref[...].astype(F32) + scale * (
        inner - jnp.mean(inner, axis=-1, keepdims=True) - xh * jnp.mean(inner * xh, axis=-1, keepdims=True)
    )
    out_ref[...] = dx.astype(out_ref.dtype)


def first_token_gradient(x, dqkv, dx, gains, w_qk, w_v, half, dtype):
    tokens, features = x.shape
    steps = tokens // BT

    def tall(cols):
        return pl.BlockSpec((BT, cols), lambda t: (t + half * steps, 0))

    def whole(array):
        return pl.BlockSpec(array.shape, lambda t: (0, 0))

    own = pl.BlockSpec((BT, features), lambda t: (t, 0))
    return pl.pallas_call(
        tokens_kernel,
        grid=(steps,),
        in_specs=[own, tall(3 * features), tall(features), whole(gains), whole(w_qk), whole(w_v)],
        out_specs=[own, pl.BlockSpec((8, features), lambda t: (0, 0))],
        out_shape=[jax.ShapeDtypeStruct((tokens, features), dtype), jax.ShapeDtypeStruct((8, features), F32)],
        compiler_params=pltpu.CompilerParams(vmem_limit_bytes=48 * MIB),
        cost_estimate=pl.CostEstimate(
            flops=12 * tokens * features * features, bytes_accessed=16 * tokens * features, transcendentals=0
        ),
        name="first_token_gradient",
    )(x, dqkv, dx, gains, w_qk, w_v)


def swap(value):
    return lax.ppermute(value, "seq", [(0, 1), (1, 0)])


def own_and_other(pair, position):
    return (
        lax.dynamic_index_in_dim(pair, position, 0, keepdims=False),
        lax.dynamic_index_in_dim(pair, 1 - position, 0, keepdims=False),
    )


def in_order(own, other, position):
    return jnp.where(position == 0, jnp.stack([own, other]), jnp.stack([other, own]))


def exchange(value, dim):
    axis = "seq" if dim == 0 else "row"
    step = 1 if dim == 0 else 1 << (dim - 1)
    return lax.ppermute(value, axis, [(i, i ^ step) for i in range(lax.axis_size(axis))])


def bit(dim):
    return lax.axis_index("seq") if dim == 0 else (lax.axis_index("row") >> (dim - 1)) & 1


def doubled(array, shape, held, dim):
    other = exchange(array, dim)
    outer = sum(1 for d in held if d > dim)
    own = array.reshape(2**outer, -1, *shape)
    other = other.reshape(own.shape)
    both = jnp.where(bit(dim) == 0, jnp.stack([own, other], 1), jnp.stack([other, own], 1))
    return both.reshape(-1, *shape)


def halved(value, dim):
    half = value.shape[0] // 2
    mine = bit(dim)
    keep = lax.dynamic_slice_in_dim(value, mine * half, half, 0)
    send = lax.dynamic_slice_in_dim(value, (1 - mine) * half, half, 0)
    return keep + exchange(send, dim)


def cut(value, shares):
    rows = value.shape[0] // sum(shares)
    ends = [rows * sum(shares[: n + 1]) for n in range(len(shares))]
    return [value[end - rows * share : end] for share, end in zip(shares, ends) if share]


def after(value, *others):
    return lax.optimization_barrier((value, *others))[0]


def row_body(tokens, segments, w_qkv, w_out, w_up, w_down, gain_attn, gain_mlp, cotangent):
    both = ("row", "seq")
    position = lax.axis_index("seq")
    devices = 2 * lax.axis_size("row")
    bits = devices.bit_length() - 1
    far = tuple(range(3, bits))
    _, half, features = tokens.shape
    *pieces, later_piece = pack(w_qkv, w_out, w_up, w_down, gain_attn, gain_mlp)
    x, other = own_and_other(tokens, position)
    paths = ((0, *reversed(far), 2, 1), (0, 2, *reversed(far), 1))
    gathered = [piece[None] for piece in pieces]
    parts = cut(other, [0] * (bits - 4) + [2, 2, 3, 1])
    x_parts = []
    for stage in range(bits):
        if stage:
            *gathered, x_parts, parts = lax.optimization_barrier((*gathered, x_parts, parts))
        if stage == bits - 2:
            later_piece = after(later_piece, *gathered)
        for n, path in enumerate(paths):
            gathered[n] = doubled(gathered[n], pieces[n].shape, path[:stage], path[stage])
        if stage and parts:
            x_parts = x_parts + [swap(parts[0])]
            parts = parts[1:]
    x_other = jnp.concatenate(x_parts)
    w_qk, w_v = [array.reshape(-1, array.shape[-1]) for array in gathered]
    w_later = lax.all_gather(later_piece, both, axis=0, tiled=True)
    dy, other = own_and_other(cotangent, position)
    dy_other = swap(after(other, w_qk, x_other))
    row_segments = lax.dynamic_index_in_dim(segments, position, 0, keepdims=False)
    stored = jnp.roll(row_segments, position * half)
    seg_col = stored[:, None]
    seg_row = jnp.broadcast_to(stored.reshape(-1, 1, B), (stored.shape[0] // B, 8, B))
    q, k, v, gains, sizes = project_qkv(x, x_other, w_qk, w_v)
    slow = jnp.any(sizes[0] * sizes[1] * 1.05 > SAFE * SAFE).astype(jnp.int32)[None]
    table, back_table = tile_tables(2 * half // B, position)
    ob, li, e = attention_forward(table, slow, q, k, v, seg_col, seg_row)
    output, dx, d, g_later = feed_forward(x, x_other, ob, dy, dy_other, li, gains, w_later)
    r_later = lax.psum_scatter(g_later, both, scatter_dimension=0, tiled=True)
    output_other = swap(output[half:])
    dqkv = attention_backward(back_table, e, q, k, v, d)
    dqkv, output_other = lax.optimization_barrier((dqkv, output_other))
    paths = ((1, 2, *far, 0), (1, *far, 2, 0))
    d_other, sum_other = first_token_gradient(x_other, dqkv, dx, gains, w_qk, w_v, 1, BF)
    parts = cut(d_other, [1, 1, 1, 1])
    d_parts = []
    orders = [weight_order(bits, path) for path in paths]
    summed = list(first_weight_gradient(x, x_other, after(dqkv, d_other), gains, orders))
    d_own, sum_own = first_token_gradient(x, after(dqkv, *summed), dx, gains, w_qk, w_v, 0, F32)
    sums = jnp.sum(sum_other + sum_own, axis=0)
    g_gain = jnp.transpose(sums.reshape(*[2] * bits, -1), [bits - 1 - dim for dim in paths[0]] + [bits])
    g_gain = g_gain.reshape(devices, 1, -1)
    for stage in range(bits):
        if stage == bits - 2:
            summed[0], r_later = lax.optimization_barrier((summed[0], r_later))
        *summed, d_parts, parts = lax.optimization_barrier((*summed, d_parts, parts))
        if stage:
            summed[0], g_gain = lax.optimization_barrier((summed[0], g_gain))
        for n, path in enumerate(paths):
            summed[n] = halved(summed[n], path[stage])
        if parts:
            d_parts = d_parts + [swap(parts[0])]
            parts = parts[1:]
        g_gain = halved(g_gain, paths[0][stage])
    output = in_order(output[:half], output_other, position)
    d_tokens = in_order(d_own, jnp.concatenate(d_parts).astype(F32), position)
    g_out, g_up, g_down = unpack(r_later)
    return (
        output,
        d_tokens,
        jnp.concatenate([summed[0][0], summed[1][0]], axis=1).astype(F32),
        g_out,
        g_up,
        g_down,
        g_gain[0, 0],
        r_later[:, 9 * features].astype(F32),
    )


def from_behind(value, axis, steps):
    count = lax.axis_size(axis)
    first, last = (max(0, -steps), min(count, count - steps))
    return lax.ppermute(value, axis, [(source, source + steps) for source in range(first, last)])


def layer_norm(values, scaling):
    mean_value = jnp.mean(values, axis=-1, keepdims=True)
    shifted = values - mean_value
    spread = jnp.mean(shifted * shifted, axis=-1, keepdims=True)
    return shifted * lax.rsqrt(spread + EPSILON) * scaling


def running_sums(values):
    places = jnp.arange(values.shape[1], dtype=jnp.int32)
    upto = (places[None, :] <= places[:, None]).astype(jnp.float32)
    return jnp.einsum("im,rmj->rij", upto, values, precision=lax.Precision.HIGHEST)


def block_masks(segments, position, source, block_len):
    offsets = jnp.arange(block_len, dtype=jnp.int32)
    query_pos = position * block_len + offsets
    key_pos = source * block_len + offsets
    query_start = position * block_len
    key_start = jnp.maximum(source, 0) * block_len
    query_seg = lax.dynamic_slice_in_dim(segments, query_start, block_len, 1)
    key_seg = lax.dynamic_slice_in_dim(segments, key_start, block_len, 1)
    same_doc = (query_seg[:, :, None] == key_seg[:, None, :]) & (source >= 0)
    earlier = key_pos[None, :] < query_pos[:, None]
    reached = key_pos[None, :] <= query_pos[:, None]
    return (same_doc & reached[None], same_doc & earlier[None])


def block_logits(queries, key_heads, carried, segments, position, source, offset):
    block_len = queries.shape[1]
    scores = jnp.einsum(
        "rqhd,rkhd->rhqk", queries, key_heads, preferred_element_type=jnp.float32
    ) * (1.0 / math.sqrt(HD))
    attend_mask, select_mask = block_masks(segments, position, source, block_len)
    chosen = jnp.where(select_mask, jax.nn.softplus(scores[:, 0] - offset), 0.0)
    running = running_sums(chosen)
    penalty = carried[:, None, :] + running - chosen
    logits = jnp.where(attend_mask[:, None], scores - penalty[:, None], MASKED)
    return (scores, logits, attend_mask, select_mask, carried + running[:, -1])


def ring_body(tokens, segments, w_qkv, w_out, w_up, w_down, gain_attn, gain_mlp, cotangent):
    low_pieces = (
        w_qkv.astype(jnp.bfloat16),
        w_out.astype(jnp.bfloat16),
        w_up.astype(jnp.bfloat16),
        w_down.astype(jnp.bfloat16),
        gain_attn.astype(jnp.bfloat16),
        gain_mlp.astype(jnp.bfloat16),
    )
    gathered = (
        lax.all_gather(low_pieces[0], ("row", "seq"), axis=0, tiled=True),
        lax.all_gather(low_pieces[1], ("row", "seq"), axis=0, tiled=True),
        lax.all_gather(low_pieces[2], ("row", "seq"), axis=0, tiled=True),
        lax.all_gather(low_pieces[3], ("row", "seq"), axis=0, tiled=True),
        lax.all_gather(low_pieces[4], ("row", "seq"), axis=0, tiled=True),
        lax.all_gather(low_pieces[5], ("row", "seq"), axis=0, tiled=True),
    )
    qkv_full, out_full, up_full, down_full, attn_scale, mlp_scale = gathered
    row_count, block_len, features = tokens.shape
    token_count = row_count * block_len
    position = lax.axis_index("seq")
    sections = lax.axis_size("seq")
    offset = math.log(ROW_LEN / 2.0) + 0.5
    inputs = tokens.astype(jnp.float32).reshape(token_count, features)
    normed, attn_norm_back = jax.vjp(layer_norm, inputs, attn_scale.astype(jnp.float32))
    normed_low = normed.astype(jnp.bfloat16)
    packed = jnp.dot(normed_low, qkv_full, preferred_element_type=jnp.float32).astype(jnp.bfloat16)
    packed = packed.reshape(row_count, block_len, 3 * features)
    queries = packed[:, :, :features].reshape(row_count, block_len, H, HD)
    key_value = packed[:, :, features:]
    carried = jnp.zeros((row_count, block_len), jnp.float32)
    running_max = jnp.full((row_count, H, block_len), MASKED, jnp.float32)
    running_sum = jnp.zeros((row_count, H, block_len), jnp.float32)
    accumulated = jnp.zeros((row_count, block_len, H, HD), jnp.float32)
    kept_pairs = []
    kept_sums = []
    for section in range(sections):
        source = position - section
        key_heads = key_value[:, :, :features].reshape(row_count, block_len, H, HD)
        value_heads = key_value[:, :, features:].reshape(row_count, block_len, H, HD)
        scores, logits, attend_mask, select_mask, passed = block_logits(
            queries, key_heads, carried, segments, position, source, offset
        )
        kept_pairs.append(key_value)
        kept_sums.append(carried)
        new_max = jnp.maximum(running_max, jnp.max(logits, axis=-1))
        rescale = jnp.exp(running_max - new_max)
        exp_scores = jnp.where(attend_mask[:, None], jnp.exp(logits - new_max[..., None]), 0.0)
        running_sum = running_sum * rescale + jnp.sum(exp_scores, axis=-1)
        accumulated = accumulated * jnp.transpose(rescale, (0, 2, 1))[..., None] + jnp.einsum(
            "rhqk,rkhd->rqhd",
            exp_scores.astype(jnp.bfloat16),
            value_heads,
            preferred_element_type=jnp.float32,
        )
        running_max = new_max
        if section + 1 < sections:
            key_value = from_behind(key_value, "seq", 1)
            carried = from_behind(passed, "seq", 1)
    log_norm = running_max + jnp.log(running_sum)
    attn_heads = accumulated / jnp.transpose(running_sum, (0, 2, 1))[..., None]
    mixed_low = attn_heads.reshape(token_count, features).astype(jnp.bfloat16)
    branch = jnp.dot(mixed_low, out_full, preferred_element_type=jnp.float32)
    middle = inputs + branch
    normed_mlp, mlp_norm_back = jax.vjp(layer_norm, middle, mlp_scale.astype(jnp.float32))
    normed_mlp_low = normed_mlp.astype(jnp.bfloat16)
    hidden = jnp.dot(normed_mlp_low, up_full, preferred_element_type=jnp.float32)
    active, gelu_back = jax.vjp(partial(jax.nn.gelu, approximate=False), hidden)
    active_low = active.astype(jnp.bfloat16)
    output = (middle + jnp.dot(active_low, down_full, preferred_element_type=jnp.float32)).astype(
        jnp.bfloat16
    )
    output = output.reshape(row_count, block_len, features)
    upstream = cotangent.reshape(token_count, features)
    grad_down = jnp.dot(active_low.T, upstream, preferred_element_type=jnp.float32)
    d_active = jnp.dot(upstream, down_full.T, preferred_element_type=jnp.float32)
    d_hidden = gelu_back(d_active)[0].astype(jnp.bfloat16)
    grad_up = jnp.dot(normed_mlp_low.T, d_hidden, preferred_element_type=jnp.float32)
    d_normed_mlp = jnp.dot(d_hidden, up_full.T, preferred_element_type=jnp.float32)
    d_middle_part, grad_mlp_gain = mlp_norm_back(d_normed_mlp)
    d_middle = upstream.astype(jnp.float32) + d_middle_part
    d_branch = d_middle.astype(jnp.bfloat16)
    grad_out = jnp.dot(mixed_low.T, d_branch, preferred_element_type=jnp.float32)
    d_mixed = jnp.dot(d_branch, out_full.T, preferred_element_type=jnp.float32).astype(jnp.bfloat16)
    d_mixed = d_mixed.reshape(row_count, block_len, H, HD)
    correction = jnp.transpose(
        jnp.sum(d_mixed.astype(jnp.float32) * attn_heads, axis=-1), (0, 2, 1)
    )
    score_scale = 1.0 / math.sqrt(HD)
    grads_pair = jnp.zeros((row_count, block_len, 2 * features), jnp.float32)
    grads_column = jnp.zeros((row_count, block_len), jnp.float32)
    grad_query = jnp.zeros((row_count, block_len, H, HD), jnp.float32)
    for section in reversed(range(sections)):
        source = position - section
        key_value = kept_pairs[section]
        key_heads = key_value[:, :, :features].reshape(row_count, block_len, H, HD)
        value_heads = key_value[:, :, features:].reshape(row_count, block_len, H, HD)
        scores, logits, attend_mask, select_mask, unused = block_logits(
            queries, key_heads, kept_sums[section], segments, position, source, offset
        )
        attention = jnp.where(attend_mask[:, None], jnp.exp(logits - log_norm[..., None]), 0.0)
        attention_low = attention.astype(jnp.bfloat16)
        grad_values = jnp.einsum(
            "rhqk,rqhd->rkhd", attention_low, d_mixed, preferred_element_type=jnp.float32
        )
        grad_attention = jnp.einsum(
            "rqhd,rkhd->rhqk", d_mixed, value_heads, preferred_element_type=jnp.float32
        )
        grad_logits = attention * (grad_attention - correction[..., None])
        summed = jnp.sum(grad_logits, axis=1)
        column = jnp.sum(summed, axis=1)
        running = running_sums(summed)
        grad_chosen = jnp.where(
            select_mask, running - column[:, None, :] - grads_column[:, None, :], 0.0
        )
        grad_scores = grad_logits.at[:, 0].add(grad_chosen * jax.nn.sigmoid(scores[:, 0] - offset))
        grad_scores = grad_scores.astype(jnp.bfloat16)
        grad_query = (
            grad_query
            + jnp.einsum(
                "rhqk,rkhd->rqhd", grad_scores, key_heads, preferred_element_type=jnp.float32
            )
            * score_scale
        )
        grad_keys = (
            jnp.einsum("rhqk,rqhd->rkhd", grad_scores, queries, preferred_element_type=jnp.float32)
            * score_scale
        )
        grads_pair = grads_pair + jnp.concatenate(
            [
                grad_keys.reshape(row_count, block_len, features),
                grad_values.reshape(row_count, block_len, features),
            ],
            axis=-1,
        )
        grads_column = grads_column + column
        if section > 0:
            grads_pair, grads_column = (
                from_behind(grads_pair.astype(jnp.bfloat16), "seq", -1).astype(grads_pair.dtype),
                from_behind(grads_column.astype(jnp.bfloat16), "seq", -1).astype(
                    grads_column.dtype
                ),
            )
    d_packed = jnp.concatenate(
        [grad_query.reshape(token_count, features), grads_pair.reshape(token_count, 2 * features)],
        axis=-1,
    )
    d_packed = d_packed.astype(jnp.bfloat16)
    grad_qkv = jnp.dot(normed_low.T, d_packed, preferred_element_type=jnp.float32)
    d_normed = jnp.dot(d_packed, qkv_full.T, preferred_element_type=jnp.float32)
    d_inputs_part, grad_attn_gain = attn_norm_back(d_normed)
    d_tokens = (d_middle + d_inputs_part).reshape(row_count, block_len, features)
    gradients = (grad_qkv, grad_out, grad_up, grad_down, grad_attn_gain, grad_mlp_gain)
    reduced = (
        lax.psum_scatter(gradients[0], ("row", "seq"), scatter_dimension=0, tiled=True),
        lax.psum_scatter(gradients[1], ("row", "seq"), scatter_dimension=0, tiled=True),
        lax.psum_scatter(gradients[2], ("row", "seq"), scatter_dimension=0, tiled=True),
        lax.psum_scatter(gradients[3], ("row", "seq"), scatter_dimension=0, tiled=True),
        lax.psum_scatter(gradients[4], ("row", "seq"), scatter_dimension=0, tiled=True),
        lax.psum_scatter(gradients[5], ("row", "seq"), scatter_dimension=0, tiled=True),
    )
    return (
        output,
        d_tokens,
        reduced[0],
        reduced[1],
        reduced[2],
        reduced[3],
        reduced[4],
        reduced[5],
    )


def body(tokens, *rest):
    rows = lax.axis_size("row")
    if lax.axis_size("seq") == 2 and tokens.shape[0] == 2 and rows >= 4 and rows & (rows - 1) == 0:
        return row_body(tokens, *rest)
    return ring_body(tokens, *rest)


def solution(mesh):
    placed = (
        P("row", "seq", None),
        P("row", None),
        P(("row", "seq"), None),
        P(("row", "seq"), None),
        P(("row", "seq"), None),
        P(("row", "seq"), None),
        P(("row", "seq")),
        P(("row", "seq")),
        P("row", "seq", None),
    )
    return jax.shard_map(
        body,
        mesh=mesh,
        in_specs=placed,
        out_specs=(
            P("row", "seq", None),
            P("row", "seq", None),
            P(("row", "seq"), None),
            P(("row", "seq"), None),
            P(("row", "seq"), None),
            P(("row", "seq"), None),
            P(("row", "seq")),
            P(("row", "seq")),
        ),
        check_vma=False,
    )
```

```python
from functools import partial
import math

import jax
import jax.numpy as jnp
from jax import lax
from jax.experimental import pallas as pl
from jax.experimental.pallas import tpu as pltpu
from jax.sharding import PartitionSpec as P

H = 12
HD = 64
ROW_LEN = 2048
EPSILON = 1e-05
MASKED = -1e30
BIG = 1e30
LOG2E = 1.4426950408889634
OFFSET = math.log(ROW_LEN / 2.0) + 0.5
SAFE = 64.0
B = 256
BT = 512
MIB = 2**20
F32 = jnp.float32
BF = jnp.bfloat16


def dot(a, b):
    return jnp.dot(a, b, preferred_element_type=F32)


def dot_nt(a, b):
    return lax.dot_general(a, b, (((1,), (1,)), ((), ())), preferred_element_type=F32)


def dot_tn(a, b):
    return lax.dot_general(a, b, (((0,), (0,)), ((), ())), preferred_element_type=F32)


def iota(shape, dim):
    return lax.broadcasted_iota(jnp.int32, shape, dim)


def half_lanes(rows):
    return iota((rows, 128), 1) < HD


def pick_columns(c):
    return (iota((512, 128), 0) == 4 * iota((512, 128), 1) + c).astype(F32).astype(BF)


def pick_rows(piece, c):
    return (iota((piece, 4 * piece), 1) == 4 * iota((piece, 4 * piece), 0) + c).astype(F32).astype(BF)


def pack_kernel(qkv_ref, out_ref, up_ref, down_ref, gain_ref, a_ref, b_ref, l_ref):
    piece, features = out_ref.shape
    lane = iota((piece, 128), 1)
    a_ref[...] = qkv_ref[:, : 2 * features].astype(BF)
    b_ref[:, :features] = qkv_ref[:, 2 * features :].astype(BF)
    gains = jnp.where(lane == 0, gain_ref[:, 0:1], jnp.where(lane == 1, gain_ref[:, 1:2], 0.0))
    b_ref[:, features:] = gains.astype(BF)
    l_ref[:, :features] = out_ref[...].astype(BF)
    for c in range(4):
        pick = pick_columns(c)
        col = features * (1 + c)
        for tile in range(features // 128):
            part = up_ref[:, 512 * tile : 512 * tile + 512].astype(BF)
            l_ref[:, col + 128 * tile : col + 128 * tile + 128] = dot(part, pick).astype(BF)
        col = features * (5 + c)
        l_ref[:, col : col + features] = dot(pick_rows(piece, c), down_ref[...].astype(BF)).astype(BF)


def pack(w_qkv, w_out, w_up, w_down, gain_attn, gain_mlp):
    piece, features = w_out.shape
    return pl.pallas_call(
        pack_kernel,
        out_shape=[
            jax.ShapeDtypeStruct((piece, cols), BF) for cols in (2 * features, features + 128, 9 * features)
        ],
        name="pack_weights",
    )(w_qkv, w_out, w_up, w_down, jnp.stack([gain_attn, gain_mlp], axis=1))


def unpack_kernel(b_ref, out_ref, up_ref, down_ref):
    piece, features = out_ref.shape
    out_ref[...] = b_ref[:, :features].astype(F32)
    for tile in range(features // 128):
        total = None
        for c in range(4):
            col = features * (1 + c) + 128 * tile
            part = dot_nt(b_ref[:, col : col + 128], pick_columns(c))
            total = part if total is None else total + part
        up_ref[:, 512 * tile : 512 * tile + 512] = total
    total = None
    for c in range(4):
        col = features * (5 + c)
        part = dot_tn(pick_rows(piece, c), b_ref[:, col : col + features])
        total = part if total is None else total + part
    down_ref[...] = total


def unpack(buffer):
    piece = buffer.shape[0]
    features = (buffer.shape[1] - 128) // 9
    return pl.pallas_call(
        unpack_kernel,
        out_shape=(
            jax.ShapeDtypeStruct((piece, features), F32),
            jax.ShapeDtypeStruct((piece, 4 * features), F32),
            jax.ShapeDtypeStruct((4 * piece, features), F32),
        ),
        name="unpack_gradients",
    )(buffer)


def moments(values):
    mean_value = jnp.mean(values, axis=-1, keepdims=True)
    shifted = values - mean_value
    spread = jnp.mean(shifted * shifted, axis=-1, keepdims=True)
    return shifted, lax.rsqrt(spread + EPSILON)


def pick_half(own_ref, other_ref, step, steps):
    return jnp.where(step < steps // 2, own_ref[...], other_ref[...])


def halves(cols, steps):
    return (
        pl.BlockSpec((BT, cols), lambda t: (jnp.minimum(t, steps // 2 - 1), 0)),
        pl.BlockSpec((BT, cols), lambda t: (jnp.maximum(t - steps // 2, 0), 0)),
    )


def qkv_kernel(x_ref, other_ref, w_ref, v_w_ref, q_ref, k_ref, v_ref, rows_ref, size_ref):
    features = x_ref.shape[1]

    @pl.when(pl.program_id(0) == 0)
    def _():
        rows_ref[...] = v_w_ref[:, features:].astype(F32).T[:8]
        size_ref[...] = jnp.zeros_like(size_ref)

    shifted, scale = moments(pick_half(x_ref, other_ref, pl.program_id(0), pl.num_programs(0)).astype(F32))
    normed = (shifted * scale * rows_ref[0:1, :]).astype(BF)
    low = half_lanes(x_ref.shape[0])
    heads = (iota((features, 128), 0) // HD == iota((features, 128), 1)).astype(F32).astype(BF)

    def spread(ref, packed, other):
        for p in range(H // 2):
            pair = packed[:, 128 * p : 128 * p + 128]
            ref[:, 256 * p : 256 * p + 128] = jnp.where(low, pair, other).astype(BF)
            ref[:, 256 * p + 128 : 256 * p + 256] = jnp.where(low, other, pair).astype(BF)

    def measure(row, value):
        most = jnp.max(dot((value * value).astype(BF), heads), axis=0, keepdims=True)
        size_ref[row : row + 1] = jnp.maximum(size_ref[row : row + 1], most)

    q = dot(normed, w_ref[:, :features]) * (LOG2E / math.sqrt(HD))
    spread(q_ref, q, 0.0)
    measure(0, q)
    k = dot(normed, w_ref[:, features:])
    spread(k_ref, k, 1.0)
    measure(1, k)
    spread(v_ref, dot(normed, v_w_ref[:, :features]), 1.0)


def project_qkv(own, other, w_qk, w_v):
    tokens, features = 2 * own.shape[0], own.shape[1]
    steps = tokens // BT

    def tall(cols):
        return pl.BlockSpec((BT, cols), lambda t: (t, 0))

    def whole(array):
        return pl.BlockSpec(array.shape, lambda t: (0, 0))

    return pl.pallas_call(
        qkv_kernel,
        grid=(steps,),
        in_specs=[*halves(features, steps), whole(w_qk), whole(w_v)],
        out_specs=[
            tall(2 * features),
            tall(2 * features),
            tall(2 * features),
            pl.BlockSpec((8, features), lambda t: (0, 0)),
            pl.BlockSpec((8, 128), lambda t: (0, 0)),
        ],
        out_shape=[
            jax.ShapeDtypeStruct((tokens, 2 * features), BF),
            jax.ShapeDtypeStruct((tokens, 2 * features), BF),
            jax.ShapeDtypeStruct((tokens, 2 * features), BF),
            jax.ShapeDtypeStruct((8, features), F32),
            jax.ShapeDtypeStruct((8, 128), F32),
        ],
        compiler_params=pltpu.CompilerParams(vmem_limit_bytes=48 * MIB),
        name="project_qkv",
    )(own, other, w_qk, w_v)


def pick(h):
    return slice(128 * h, 128 * h + 128)


def block_rows(index):
    return pl.ds(pl.multiple_of(index * B, B), B)


def two_part(tri, values):
    high = values.astype(BF)
    rest = (values - high.astype(F32)).astype(BF)
    return dot(tri, high) + dot(tri, rest)


def selection(scores, segq, segk, rows, cols):
    earlier = (segq == segk) & (cols < rows)
    x = scores - OFFSET * LOG2E
    grown = jnp.exp2(jnp.minimum(x, 100.0))
    more = 1.0 + grown
    return jnp.where(earlier, jnp.maximum(x, jnp.log2(more)), 0.0), jnp.where(earlier, grown / more, 0.0)


def mixed(first, second):
    done = 0
    for n, step in enumerate(first):
        step()
        upto = (n + 1) * len(second) // len(first)
        for other in second[done:upto]:
            other()
        done = upto


STRIP = 64
LEAD = 2


def key_copies(block, stored, k_any, v_any, kx, vx, sem):
    rows = block_rows(stored)
    return (
        pltpu.make_async_copy(k_any.at[rows, :], kx.at[block], sem.at[0, block]),
        pltpu.make_async_copy(v_any.at[rows, :], vx.at[block], sem.at[1, block]),
    )


def forward_kernel(tab, slow, q_ref, q0_ref, k0_ref, segq_ref, segk_ref, k_any, v_any, o_ref, li_ref, e_ref,
                   acc, carry, tri, qx, penalty, gate, work, high, kx, vx, sem):
    t = pl.program_id(0)
    ib, jb = tab[2, t], tab[3, t]

    @pl.when(t == 0)
    def _():
        for block in range(kx.shape[0]):
            for copy in key_copies(block, tab[1, block * (block + 3) // 2], k_any, v_any, kx, vx, sem):
                copy.start()

    def prepare(step, slot):
        keys = block_rows(tab[1, step])
        at = tab[3, step]
        ahead = (tab[2, step] - at) * B
        segk = segk_ref[tab[1, step], 0:1, :]
        sums = []

        def scores():
            work[...] = dot_nt(q0_ref[block_rows(tab[0, step]), :], k0_ref[keys, :])

        def strip(n):
            part = slice(STRIP * n, STRIP * n + STRIP)
            segq = segq_ref[pl.ds(pl.multiple_of(tab[0, step] * B + STRIP * n, STRIP), STRIP), :]
            return part, segq, iota((STRIP, B), 0) + (ahead + STRIP * n), iota((STRIP, B), 1)

        def choose(n):
            part, segq, rows, cols = strip(n)
            chosen, opened = selection(work[part, :], segq, segk, rows, cols)
            gate[slot, part, :] = opened.astype(BF)
            high[part, :] = chosen.astype(BF)
            sums.append(jnp.sum(chosen, axis=0, keepdims=True))

        def add():
            before = carry[at, 0:1, :]
            work[...] = dot(tri[...], high[...]) + before
            carry[at, 0:1, :] = before + sum(sums[1:], sums[0])

        def close(n):
            part, segq, rows, cols = strip(n)
            penalty[slot, part, :] = jnp.where((segq == segk) & (cols <= rows), work[part, :], BIG)

        count = range(B // STRIP)
        return [scores] + [partial(choose, n) for n in count] + [add] + [partial(close, n) for n in count]

    @pl.when(t == 0)
    def _():
        carry[...] = jnp.zeros_like(carry)
        tri[...] = (iota((B, B), 1) < iota((B, B), 0)).astype(F32).astype(BF)
        for step in prepare(0, 0):
            step()

    @pl.when(jb == 0)
    def _():
        acc[...] = jnp.zeros_like(acc)
        qx[...] = q_ref[...]
        for copy in key_copies(ib, tab[0, t], k_any, v_any, kx, vx, sem):
            copy.wait()

        @pl.when(slow[0] != 0)
        def _():
            lane = iota((B, 128), 1)
            segq = segq_ref[block_rows(tab[0, t]), :]
            cols = iota((B, B), 1)

            def chosen(other):
                rows = iota((B, B), 0) + (ib - other) * B
                base = tab[1, t + other]
                first = dot_nt(q_ref[:, 0:128], k0_ref[block_rows(base), :])
                return selection(first, segq, segk_ref[base, 0:1, :], rows, cols)[0]

            own = jnp.sum(chosen(0), axis=0, keepdims=True)

            def step(other, top):
                base = tab[1, t + other]
                before = carry[other, 0:1, :] - jnp.where(other == 0, own, 0.0)
                kept = (segq == segk_ref[base, 0:1, :]) & (cols <= iota((B, B), 0) + (ib - other) * B)
                z_penalty = jnp.where(kept, dot(tri[...], chosen(other).astype(BF)) + before, BIG)
                for h in range(H):
                    z = dot_nt(q_ref[:, pick(h)], kx[other, :, pick(h)]) - z_penalty
                    top = jnp.where(lane == h, jnp.maximum(top, jnp.max(z, axis=1, keepdims=True)), top)
                return top

            top = lax.fori_loop(0, ib + 1, step, jnp.full((B, 128), -BIG, F32))
            for h in range(H):
                shift = -jnp.sum(jnp.where(lane == h, top, 0.0), axis=1, keepdims=True)
                one = shift.astype(BF).astype(F32)
                two = (shift - one).astype(BF).astype(F32)
                three = shift - one - two
                at = lane - (HD if h % 2 == 0 else 0)
                extra = jnp.where(at == 0, one, jnp.where(at == 1, two, jnp.where(at == 2, three, 0.0)))
                keep = (lane < HD) if h % 2 == 0 else (lane >= HD)
                qx[:, pick(h)] = jnp.where(keep, q_ref[:, pick(h)].astype(F32), extra).astype(BF)

    slot = t % 2

    def head(h):
        e = jnp.exp2(dot_nt(qx[:, pick(h)], kx[jb, :, pick(h)]) - penalty[slot]).astype(BF)
        e_ref[0, h] = e

    def value(h):
        acc[:, pick(h)] += dot(e_ref[0, h], vx[jb, :, pick(h)])

    e_ref[0, H] = gate[slot]
    steps = [partial(head, h) for h in range(LEAD)]
    for h in range(H):
        if h + LEAD < H:
            steps.append(partial(head, h + LEAD))
        steps.append(partial(value, h))
    mixed(steps, prepare(t + 1, 1 - slot))

    @pl.when(jb == ib)
    def _():
        low = half_lanes(B)
        for p in range(H // 2):
            one = acc[:, pick(2 * p)]
            two = acc[:, pick(2 * p + 1)]
            inverse = 1.0 / pltpu.roll(jnp.where(low, two, one), HD, 1)
            o_ref[:, pick(p)] = (jnp.where(low, one, two) * inverse).astype(BF)
            li_ref[:, pick(p)] = inverse


def attention_forward(table, slow, q, k, v, seg_col, seg_row):
    tokens = q.shape[0]
    blocks = tokens // B
    tiles = table.shape[1] - 1
    wide = 128 * H
    narrow = HD * H
    once = pl.Buffered(1)
    return pl.pallas_call(
        forward_kernel,
        grid_spec=pltpu.PrefetchScalarGridSpec(
            num_scalar_prefetch=2,
            grid=(tiles,),
            in_specs=[
                pl.BlockSpec((B, wide), lambda t, tab, slow: (tab[0, t], 0)),
                pl.BlockSpec((tokens, 128), lambda t, tab, slow: (0, 0), pipeline_mode=once),
                pl.BlockSpec((tokens, 128), lambda t, tab, slow: (0, 0), pipeline_mode=once),
                pl.BlockSpec((tokens, 1), lambda t, tab, slow: (0, 0), pipeline_mode=once),
                pl.BlockSpec((blocks, 8, B), lambda t, tab, slow: (0, 0, 0), pipeline_mode=once),
                pl.BlockSpec(memory_space=pl.ANY),
                pl.BlockSpec(memory_space=pl.ANY),
            ],
            out_specs=[
                pl.BlockSpec((B, narrow), lambda t, tab, slow: (tab[0, t], 0)),
                pl.BlockSpec((B, narrow), lambda t, tab, slow: (tab[0, t], 0)),
                pl.BlockSpec((1, H + 1, B, B), lambda t, tab, slow: (tab[4, t], 0, 0, 0)),
            ],
            scratch_shapes=[
                pltpu.VMEM((B, wide), F32),
                pltpu.VMEM((blocks, 8, B), F32),
                pltpu.VMEM((B, B), BF),
                pltpu.VMEM((B, wide), BF),
                pltpu.VMEM((2, B, B), F32),
                pltpu.VMEM((2, B, B), BF),
                pltpu.VMEM((B, B), F32),
                pltpu.VMEM((B, B), BF),
                pltpu.VMEM((blocks, B, wide), BF),
                pltpu.VMEM((blocks, B, wide), BF),
                pltpu.SemaphoreType.DMA((2, blocks)),
            ],
        ),
        out_shape=[
            jax.ShapeDtypeStruct((tokens, narrow), BF),
            jax.ShapeDtypeStruct((tokens, narrow), F32),
            jax.ShapeDtypeStruct((tiles, H + 1, B, B), BF),
        ],
        compiler_params=pltpu.CompilerParams(vmem_limit_bytes=48 * MIB),
        name="attention_forward",
    )(table, slow, q, q, k, seg_col, seg_row, k, v)


def backward_kernel(tab, e_ref, q_ref, d_ref, q0_ref, k0_ref, k_any, v_any, o_ref,
                    dq, dkt, dvt, carry, tri, sums, first, gate, work, kx, vx, sem):
    t = pl.program_id(0)
    last = pl.num_programs(0) - 1
    before = jnp.maximum(t - 1, 0)
    narrow = HD * H
    low = half_lanes(B)
    slot = t % 2

    @pl.when(t == 0)
    def _():
        for block in range(kx.shape[0]):
            for copy in key_copies(block, tab[1, block], k_any, v_any, kx, vx, sem):
                copy.start()
        carry[...] = jnp.zeros_like(carry)
        tri[...] = (iota((B, B), 1) > iota((B, B), 0)).astype(F32).astype(BF)
        dkt[...] = jnp.zeros_like(dkt)
        dvt[...] = jnp.zeros_like(dvt)
        dq[...] = jnp.zeros_like(dq)
        sums[...] = jnp.zeros_like(sums)
        first[...] = jnp.zeros_like(first)
        gate[...] = jnp.zeros_like(gate)

    @pl.when((tab[3, t] == 0) & (t < last))
    def _():
        dq[tab[2, t] % 2] = jnp.zeros(dq.shape[1:], F32)

    @pl.when(t < kx.shape[0])
    def _():
        for copy in key_copies(t, tab[1, t], k_any, v_any, kx, vx, sem):
            copy.wait()

    def finish():
        at = tab[3, before]

        def add():
            total = sums[1 - slot]
            later = carry[at, 0:1, :] + two_part(tri[...], total)
            carry[at, 0:1, :] = carry[at, 0:1, :] + jnp.sum(total, axis=0, keepdims=True)
            work[...] = (first[1 - slot] - later * gate[1 - slot].astype(F32)).astype(BF)

        def keys():
            dkt[:HD, block_rows(at)] += dot_tn(q0_ref[block_rows(tab[0, before]), :], work[...])[:HD]

        def queries():
            more = dot(work[...], k0_ref[block_rows(tab[1, before]), :])
            dq[tab[2, before] % 2, :, :128] += jnp.where(low, more, 0.0)

        return [add, keys, queries]

    @pl.when(t == last)
    def _():
        for step in finish():
            step()

    @pl.when(t < last)
    def _():
        cols = block_rows(tab[3, t])
        turn = tab[2, t] % 2
        kept = {}
        parts = {}

        def score(h):
            e = e_ref[0, h]
            dz = e.astype(F32) * dot_nt(d_ref[:, pick(h)], vx[tab[3, t], :, pick(h)])
            if h == 0:
                first[slot] = dz
                sums[slot] = dz
            else:
                sums[slot] += dz
                kept[h] = dz.astype(BF)

        def products(h):
            own = slice(HD * h, HD * h + HD)
            data = slice(HD * (h % 2), HD * (h % 2) + HD)
            dvt[own, cols] += dot_tn(d_ref[:, pick(h)], e_ref[0, h])[data]
            if h == 0:
                parts[0] = 0.0
                return
            ds = kept.pop(h)
            dkt[own, cols] += dot_tn(q_ref[:, pick(h)], ds)[data]
            parts[h] = dot(ds, kx[tab[3, t], :, pick(h)])
            if h % 2:
                dq[turn, :, pick(h // 2)] += jnp.where(low, parts.pop(h - 1), parts.pop(h))

        gate[slot] = e_ref[0, H]
        steps = [partial(score, h) for h in range(LEAD)]
        for h in range(H):
            if h + LEAD < H:
                steps.append(partial(score, h + LEAD))
            steps.append(partial(products, h))
        mixed(steps, finish())

    @pl.when((t > 0) & (tab[3, before] == tab[2, before]))
    def _():
        cols = block_rows(tab[2, before])
        o_ref[:, :narrow] = (dq[tab[2, before] % 2] * (1.0 / math.sqrt(HD))).astype(BF)
        o_ref[:, narrow : 2 * narrow] = (dkt[:, cols] * (1.0 / LOG2E)).astype(BF).T
        o_ref[:, 2 * narrow :] = dvt[:, cols].astype(BF).T


def attention_backward(table, e, q, k, v, d):
    tokens = q.shape[0]
    blocks = tokens // B
    tiles = table.shape[1] - 1
    wide = 128 * H
    narrow = HD * H
    once = pl.Buffered(1)
    return pl.pallas_call(
        backward_kernel,
        grid_spec=pltpu.PrefetchScalarGridSpec(
            num_scalar_prefetch=1,
            grid=(tiles + 1,),
            in_specs=[
                pl.BlockSpec((1, H + 1, B, B), lambda t, tab: (tab[4, t], 0, 0, 0)),
                pl.BlockSpec((B, wide), lambda t, tab: (tab[0, t], 0)),
                pl.BlockSpec((B, wide), lambda t, tab: (tab[0, t], 0)),
                pl.BlockSpec((tokens, 128), lambda t, tab: (0, 0), pipeline_mode=once),
                pl.BlockSpec((tokens, 128), lambda t, tab: (0, 0), pipeline_mode=once),
                pl.BlockSpec(memory_space=pl.ANY),
                pl.BlockSpec(memory_space=pl.ANY),
            ],
            out_specs=pl.BlockSpec((B, 3 * narrow), lambda t, tab: (tab[0, jnp.maximum(t - 1, 0)], 0)),
            scratch_shapes=[
                pltpu.VMEM((2, B, narrow), F32),
                pltpu.VMEM((narrow, tokens), F32),
                pltpu.VMEM((narrow, tokens), F32),
                pltpu.VMEM((blocks, 8, B), F32),
                pltpu.VMEM((B, B), BF),
                pltpu.VMEM((2, B, B), F32),
                pltpu.VMEM((2, B, B), F32),
                pltpu.VMEM((2, B, B), BF),
                pltpu.VMEM((B, B), BF),
                pltpu.VMEM((blocks, B, wide), BF),
                pltpu.VMEM((blocks, B, wide), BF),
                pltpu.SemaphoreType.DMA((2, blocks)),
            ],
        ),
        out_shape=jax.ShapeDtypeStruct((tokens, 3 * narrow), BF),
        compiler_params=pltpu.CompilerParams(vmem_limit_bytes=56 * MIB),
        cost_estimate=pl.CostEstimate(flops=tiles * H * B * B * 1024, bytes_accessed=tiles * B * B, transcendentals=0),
        name="attention_backward",
    )(table, e, q, d, q, k, k, v)


def tile_tables(blocks, position):
    pairs = [(i, j) for i in range(blocks) for j in range(i + 1)]
    back = [(i, j) for i in reversed(range(blocks)) for j in range(i + 1)]
    shift = position * (blocks // 2)

    def table(order):
        order = order + order[-1:]
        rows = jnp.array([i for i, _ in order], jnp.int32)
        keys = jnp.array([j for _, j in order], jnp.int32)
        return jnp.stack(
            [(rows + shift) % blocks, (keys + shift) % blocks, rows, keys, rows * (rows + 1) // 2 + keys]
        )

    return table(pairs), table(back)


PART = 256
ROWS = 64


def mlp_kernel(x_ref, x2_ref, ob_ref, dy1_ref, dy2_ref, li_ref, gain_ref, wo_ref, wu_ref, wd_ref, out_ref, dx_ref, d_ref, g_any,
               xh, scales, y, dn, n2, gup, gdown, gout, gsum, stage, gcol, us, das, actives, dus, sem):
    c, t = pl.program_id(0), pl.program_id(1)
    chunks, steps = pl.num_programs(0), pl.num_programs(1)
    rows = pl.ds(pl.multiple_of(t * BT, BT), BT)
    features = x_ref.shape[1]

    def send(slot, column):
        start = pl.multiple_of(column, 128)
        return pltpu.make_async_copy(stage.at[slot], g_any.at[:, pl.ds(start, features)], sem.at[slot])

    @pl.when(c == 0)
    def _():
        middle = pick_half(x_ref, x2_ref, t, steps).astype(F32) + dot(ob_ref[...], wo_ref[...])
        shifted, scale = moments(middle)
        xh[rows, :] = (shifted * scale).astype(BF)
        scales[rows, :] = jnp.broadcast_to(scale, (BT, 128))
        y[rows, :] = middle
        dn[rows, :] = jnp.zeros_like(middle)
        n2[rows, :] = (shifted * scale * gain_ref[1:2, :]).astype(BF)

    @pl.when(t == 0)
    def _():
        gup[...] = jnp.zeros_like(gup)
        gdown[...] = jnp.zeros_like(gdown)

    @pl.when((c == 0) & (t == 0))
    def _():
        gout[...] = jnp.zeros_like(gout)
        gsum[...] = jnp.zeros_like(gsum)

    n2_low = n2[rows, :]
    dy_low = pick_half(dy1_ref, dy2_ref, t, steps)

    def enter(p):
        units = slice(PART * p, PART * p + PART)

        def up():
            us[p % 2] = dot(n2_low, wu_ref[:, units])

        def down():
            das[p % 2] = dot_nt(dy_low, wd_ref[units, :])

        return [up, down]

    def bend(p, n):
        part = slice(ROWS * n, ROWS * n + ROWS)
        u = us[p % 2, part, :]
        cdf = 0.5 * (1.0 + lax.erf(u * math.sqrt(0.5)))
        density = jnp.exp(-0.5 * u * u) * (1.0 / math.sqrt(2.0 * math.pi))
        units = slice(PART * p, PART * p + PART)
        actives[part, units] = (u * cdf).astype(BF)
        dus[part, units] = ((cdf + u * density) * das[p % 2, part, :]).astype(BF)

    def leave(p):
        units = slice(PART * p, PART * p + PART)

        def down():
            y[rows, :] += dot(actives[:, units], wd_ref[units, :])

        def up():
            dn[rows, :] += dot_nt(dus[:, units], wu_ref[:, units])

        return [down, up]

    parts = features // PART
    for step in enter(0):
        step()
    for p in range(parts):
        products = (leave(p - 1) if p else []) + (enter(p + 1) if p + 1 < parts else [])
        mixed(products, [partial(bend, p, n) for n in range(BT // ROWS)])
    for step in leave(parts - 1):
        step()
    gdown[...] += dot_tn(actives[...], dy_low)
    gup[...] += dot_tn(n2_low, dus[...])

    @pl.when(t == steps - 1)
    def _():
        @pl.when(c > 0)
        def _():
            send(0, c * features).wait()
            send(1, (c + chunks) * features).wait()

        stage[0] = gup[...].astype(BF)
        stage[1] = gdown[...].astype(BF)
        send(0, (1 + c) * features).start()
        send(1, (1 + c + chunks) * features).start()

    @pl.when(c == chunks - 1)
    def _():
        out_ref[...] = y[rows, :].astype(BF)
        d_normed = dn[rows, :]
        scale = scales[rows, 0:1]
        unit = xh[rows, :].astype(F32)
        product = d_normed * unit
        gsum[...] += jnp.sum(product.reshape(BT // 8, 8, features), axis=0)
        inner = d_normed * gain_ref[1:2, :]
        dx = dy_low.astype(F32) + scale * (
            inner - jnp.mean(inner, axis=-1, keepdims=True) - unit * jnp.mean(inner * unit, axis=-1, keepdims=True)
        )
        dx_ref[...] = dx.astype(BF)
        db = dx.astype(BF)
        gout[...] += dot_tn(ob_ref[...], db)
        scaled = dot_nt(db, wo_ref[...]) * li_ref[...]
        low = half_lanes(BT)
        lane = iota((BT, 128), 1)
        swap_row, swap_col = iota((128, 128), 0), iota((128, 128), 1)
        swap = ((swap_row // HD != swap_col // HD) & (swap_col % HD < 2)).astype(F32).astype(BF)
        for p in range(H // 2):
            w = slice(128 * p, 128 * p + 128)
            pair = scaled[:, w]
            both = pair * ob_ref[:, w].astype(F32)
            high = both.astype(BF)
            delta = dot(high, swap) + dot((both - high.astype(F32)).astype(BF), swap)
            top = delta.astype(BF).astype(F32)
            extra = jnp.where((lane == 0) | (lane == HD), -top, top - delta)
            d_ref[:, 256 * p : 256 * p + 128] = jnp.where(low, pair, extra).astype(BF)
            d_ref[:, 256 * p + 128 : 256 * p + 256] = jnp.where(low, extra, pair).astype(BF)

    @pl.when((c == chunks - 1) & (t == steps - 1))
    def _():
        stage[2] = gout[...].astype(BF)
        column = jnp.broadcast_to(jnp.sum(gsum[...], axis=0, keepdims=True), (128, features))
        gcol[...] = column.T.astype(BF)
        last = pltpu.make_async_copy(
            gcol, g_any.at[:, pl.ds((1 + 2 * 4) * features, 128)], sem.at[3]
        )
        send(2, 0).start()
        last.start()
        send(0, chunks * features).wait()
        send(1, 2 * chunks * features).wait()
        send(2, 0).wait()
        last.wait()


def feed_forward(x, x_other, ob, dy, dy_other, li, gains, weights):
    tokens, features = ob.shape
    steps = tokens // BT
    chunks = 4

    def ends(c, t):
        return (jnp.where((c == 0) | (c == chunks - 1), t, steps - 1), 0)

    def own(t):
        return jnp.minimum(t, steps // 2 - 1)

    def other(t):
        return jnp.maximum(t - steps // 2, 0)

    def at_last(c, t):
        return (jnp.where(c == chunks - 1, t, 0), 0)

    block = (BT, features)
    once = pl.Buffered(1)
    return pl.pallas_call(
        mlp_kernel,
        grid=(chunks, steps),
        in_specs=[
            pl.BlockSpec(block, lambda c, t: (own(jnp.where(c == 0, t, steps - 1)), 0), pipeline_mode=once),
            pl.BlockSpec(block, lambda c, t: (other(jnp.where(c == 0, t, steps - 1)), 0), pipeline_mode=once),
            pl.BlockSpec(block, ends),
            pl.BlockSpec(block, lambda c, t: (own(t), 0)),
            pl.BlockSpec(block, lambda c, t: (other(t), 0)),
            pl.BlockSpec(block, at_last),
            pl.BlockSpec((8, features), lambda c, t: (0, 0)),
            pl.BlockSpec((features, features), lambda c, t: (0, 0), pipeline_mode=once),
            pl.BlockSpec((features, features), lambda c, t: (0, 1 + c)),
            pl.BlockSpec((features, features), lambda c, t: (0, 1 + chunks + c)),
        ],
        out_specs=[
            pl.BlockSpec(block, at_last),
            pl.BlockSpec(block, at_last),
            pl.BlockSpec((BT, 2 * features), at_last),
            pl.BlockSpec(memory_space=pl.ANY),
        ],
        out_shape=[
            jax.ShapeDtypeStruct((tokens, features), BF),
            jax.ShapeDtypeStruct((tokens, features), BF),
            jax.ShapeDtypeStruct((tokens, 2 * features), BF),
            jax.ShapeDtypeStruct((features, 9 * features + 128), BF),
        ],
        scratch_shapes=[
            pltpu.VMEM((tokens, features), BF),
            pltpu.VMEM((tokens, 128), F32),
            pltpu.VMEM((tokens, features), F32),
            pltpu.VMEM((tokens, features), F32),
            pltpu.VMEM((tokens, features), BF),
            pltpu.VMEM((features, features), F32),
            pltpu.VMEM((features, features), F32),
            pltpu.VMEM((features, features), F32),
            pltpu.VMEM((8, features), F32),
            pltpu.VMEM((3, features, features), BF),
            pltpu.VMEM((features, 128), BF),
            pltpu.VMEM((2, BT, PART), F32),
            pltpu.VMEM((2, BT, PART), F32),
            pltpu.VMEM((BT, features), BF),
            pltpu.VMEM((BT, features), BF),
            pltpu.SemaphoreType.DMA((4,)),
        ],
        compiler_params=pltpu.CompilerParams(vmem_limit_bytes=63 * MIB),
        name="feed_forward",
    )(x, x_other, ob, dy, dy_other, li, gains, weights, weights, weights)


def weight_order(bits, dims):
    return [
        sum(((place >> (bits - 1 - n)) & 1) << dim for n, dim in enumerate(dims)) for place in range(2**bits)
    ]


def weight_kernel(x_ref, other_ref, dqkv_ref, gain_ref, a_ref, b_ref, acc, *, orders):
    t = pl.program_id(0)

    @pl.when(t == 0)
    def _():
        acc[...] = jnp.zeros_like(acc)

    shifted, scale = moments(pick_half(x_ref, other_ref, t, pl.num_programs(0)).astype(F32))
    normed = (shifted * scale * gain_ref[0:1, :]).astype(BF)
    acc[...] += dot_tn(normed, dqkv_ref[...])

    @pl.when(t == pl.num_programs(0) - 1)
    def _():
        _, piece, split = a_ref.shape
        for place, block in enumerate(orders[0]):
            a_ref[place] = acc[piece * block : piece * block + piece, :split].astype(BF)
        for place, block in enumerate(orders[1]):
            b_ref[place] = acc[piece * block : piece * block + piece, split:].astype(BF)


def first_weight_gradient(x, x_other, dqkv, gains, orders):
    tokens, features = dqkv.shape[0], x.shape[1]
    steps = tokens // BT
    blocks = len(orders[0])
    shapes = [(blocks, features // blocks, cols) for cols in (2 * features, features)]
    return pl.pallas_call(
        partial(weight_kernel, orders=orders),
        grid=(steps,),
        in_specs=[
            *halves(features, steps),
            pl.BlockSpec((BT, 3 * features), lambda t: (t, 0)),
            pl.BlockSpec(gains.shape, lambda t: (0, 0)),
        ],
        out_specs=[pl.BlockSpec(shape, lambda t: (0, 0, 0)) for shape in shapes],
        out_shape=[jax.ShapeDtypeStruct(shape, BF) for shape in shapes],
        scratch_shapes=[pltpu.VMEM((features, 3 * features), F32)],
        compiler_params=pltpu.CompilerParams(vmem_limit_bytes=48 * MIB),
        cost_estimate=pl.CostEstimate(
            flops=12 * tokens * features * features, bytes_accessed=16 * tokens * features, transcendentals=0
        ),
        name="first_weight_gradient",
    )(x, x_other, dqkv, gains)


def tokens_kernel(x_ref, dqkv_ref, dx_ref, gain_ref, w_ref, v_w_ref, out_ref, gsum_ref):
    features = x_ref.shape[1]

    @pl.when(pl.program_id(0) == 0)
    def _():
        gsum_ref[...] = jnp.zeros_like(gsum_ref)

    shifted, scale = moments(x_ref[...].astype(F32))
    xh = shifted * scale
    d_normed = dot_nt(dqkv_ref[:, : 2 * features], w_ref[...])
    d_normed += dot_nt(dqkv_ref[:, 2 * features :], v_w_ref[:, :features])
    gsum_ref[...] += jnp.sum((d_normed * xh).reshape(BT // 8, 8, features), axis=0)
    inner = d_normed * gain_ref[0:1, :]
    dx = dx_ref[...].astype(F32) + scale * (
        inner - jnp.mean(inner, axis=-1, keepdims=True) - xh * jnp.mean(inner * xh, axis=-1, keepdims=True)
    )
    out_ref[...] = dx.astype(out_ref.dtype)


def first_token_gradient(x, dqkv, dx, gains, w_qk, w_v, half, dtype):
    tokens, features = x.shape
    steps = tokens // BT

    def tall(cols):
        return pl.BlockSpec((BT, cols), lambda t: (t + half * steps, 0))

    def whole(array):
        return pl.BlockSpec(array.shape, lambda t: (0, 0))

    own = pl.BlockSpec((BT, features), lambda t: (t, 0))
    return pl.pallas_call(
        tokens_kernel,
        grid=(steps,),
        in_specs=[own, tall(3 * features), tall(features), whole(gains), whole(w_qk), whole(w_v)],
        out_specs=[own, pl.BlockSpec((8, features), lambda t: (0, 0))],
        out_shape=[jax.ShapeDtypeStruct((tokens, features), dtype), jax.ShapeDtypeStruct((8, features), F32)],
        compiler_params=pltpu.CompilerParams(vmem_limit_bytes=48 * MIB),
        cost_estimate=pl.CostEstimate(
            flops=12 * tokens * features * features, bytes_accessed=16 * tokens * features, transcendentals=0
        ),
        name="first_token_gradient",
    )(x, dqkv, dx, gains, w_qk, w_v)


def swap(value):
    return lax.ppermute(value, "seq", [(0, 1), (1, 0)])


def own_and_other(pair, position):
    return (
        lax.dynamic_index_in_dim(pair, position, 0, keepdims=False),
        lax.dynamic_index_in_dim(pair, 1 - position, 0, keepdims=False),
    )


def in_order(own, other, position):
    return jnp.where(position == 0, jnp.stack([own, other]), jnp.stack([other, own]))


def exchange(value, dim):
    axis = "seq" if dim == 0 else "row"
    step = 1 if dim == 0 else 1 << (dim - 1)
    return lax.ppermute(value, axis, [(i, i ^ step) for i in range(lax.axis_size(axis))])


def bit(dim):
    return lax.axis_index("seq") if dim == 0 else (lax.axis_index("row") >> (dim - 1)) & 1


def doubled(array, shape, held, dim):
    other = exchange(array, dim)
    outer = sum(1 for d in held if d > dim)
    own = array.reshape(2**outer, -1, *shape)
    other = other.reshape(own.shape)
    both = jnp.where(bit(dim) == 0, jnp.stack([own, other], 1), jnp.stack([other, own], 1))
    return both.reshape(-1, *shape)


def halved(value, dim):
    half = value.shape[0] // 2
    mine = bit(dim)
    keep = lax.dynamic_slice_in_dim(value, mine * half, half, 0)
    send = lax.dynamic_slice_in_dim(value, (1 - mine) * half, half, 0)
    return keep + exchange(send, dim)


def cut(value, shares):
    rows = value.shape[0] // sum(shares)
    ends = [rows * sum(shares[: n + 1]) for n in range(len(shares))]
    return [value[end - rows * share : end] for share, end in zip(shares, ends) if share]


def after(value, *others):
    return lax.optimization_barrier((value, *others))[0]


def row_body(tokens, segments, w_qkv, w_out, w_up, w_down, gain_attn, gain_mlp, cotangent):
    both = ("row", "seq")
    position = lax.axis_index("seq")
    devices = 2 * lax.axis_size("row")
    bits = devices.bit_length() - 1
    far = tuple(range(3, bits))
    _, half, features = tokens.shape
    *pieces, later_piece = pack(w_qkv, w_out, w_up, w_down, gain_attn, gain_mlp)
    x, other = own_and_other(tokens, position)
    paths = ((0, *reversed(far), 2, 1), (0, 2, *reversed(far), 1))
    gathered = [piece[None] for piece in pieces]
    parts = cut(other, [0] * (bits - 4) + [2, 2, 3, 1])
    x_parts = []
    for stage in range(bits):
        if stage:
            *gathered, x_parts, parts = lax.optimization_barrier((*gathered, x_parts, parts))
        if stage == bits - 2:
            later_piece = after(later_piece, *gathered)
        for n, path in enumerate(paths):
            gathered[n] = doubled(gathered[n], pieces[n].shape, path[:stage], path[stage])
        if stage and parts:
            x_parts = x_parts + [swap(parts[0])]
            parts = parts[1:]
    x_other = jnp.concatenate(x_parts)
    w_qk, w_v = [array.reshape(-1, array.shape[-1]) for array in gathered]
    w_later = lax.all_gather(later_piece, both, axis=0, tiled=True)
    dy, other = own_and_other(cotangent, position)
    dy_other = swap(after(other, w_qk, x_other))
    row_segments = lax.dynamic_index_in_dim(segments, position, 0, keepdims=False)
    stored = jnp.roll(row_segments, position * half)
    seg_col = stored[:, None]
    seg_row = jnp.broadcast_to(stored.reshape(-1, 1, B), (stored.shape[0] // B, 8, B))
    q, k, v, gains, sizes = project_qkv(x, x_other, w_qk, w_v)
    slow = jnp.any(sizes[0] * sizes[1] * 1.05 > SAFE * SAFE).astype(jnp.int32)[None]
    table, back_table = tile_tables(2 * half // B, position)
    ob, li, e = attention_forward(table, slow, q, k, v, seg_col, seg_row)
    output, dx, d, g_later = feed_forward(x, x_other, ob, dy, dy_other, li, gains, w_later)
    r_later = lax.psum_scatter(g_later, both, scatter_dimension=0, tiled=True)
    output_other = swap(output[half:])
    dqkv = attention_backward(back_table, e, q, k, v, d)
    dqkv, output_other = lax.optimization_barrier((dqkv, output_other))
    paths = ((1, 2, *far, 0), (1, *far, 2, 0))
    orders = [weight_order(bits, path) for path in paths]
    summed = list(first_weight_gradient(x, x_other, dqkv, gains, orders))
    d_other, sum_other = first_token_gradient(x_other, after(dqkv, *summed), dx, gains, w_qk, w_v, 1, BF)
    d_own, sum_own = first_token_gradient(x, after(dqkv, d_other), dx, gains, w_qk, w_v, 0, F32)
    sums = jnp.sum(sum_other + sum_own, axis=0)
    g_gain = jnp.transpose(sums.reshape(*[2] * bits, -1), [bits - 1 - dim for dim in paths[0]] + [bits])
    g_gain = g_gain.reshape(devices, 1, -1)
    parts = cut(d_other, [0] * (bits - 5) + [1, 1, 1, 1])
    d_parts = []
    for stage in range(bits):
        if stage == bits - 2:
            summed[0], r_later = lax.optimization_barrier((summed[0], r_later))
        if stage:
            *summed, d_parts, parts = lax.optimization_barrier((*summed, d_parts, parts))
        else:
            summed = list(lax.optimization_barrier(tuple(summed)))
        if stage > 1:
            summed[0], g_gain = lax.optimization_barrier((summed[0], g_gain))
        for n, path in enumerate(paths):
            summed[n] = halved(summed[n], path[stage])
        if stage and parts:
            d_parts = d_parts + [swap(parts[0])]
            parts = parts[1:]
        g_gain = halved(g_gain, paths[0][stage])
    output = in_order(output[:half], output_other, position)
    d_tokens = in_order(d_own, jnp.concatenate(d_parts).astype(F32), position)
    g_out, g_up, g_down = unpack(r_later)
    return (
        output,
        d_tokens,
        jnp.concatenate([summed[0][0], summed[1][0]], axis=1).astype(F32),
        g_out,
        g_up,
        g_down,
        g_gain[0, 0],
        r_later[:, 9 * features].astype(F32),
    )


def from_behind(value, axis, steps):
    count = lax.axis_size(axis)
    first, last = (max(0, -steps), min(count, count - steps))
    return lax.ppermute(value, axis, [(source, source + steps) for source in range(first, last)])


def layer_norm(values, scaling):
    mean_value = jnp.mean(values, axis=-1, keepdims=True)
    shifted = values - mean_value
    spread = jnp.mean(shifted * shifted, axis=-1, keepdims=True)
    return shifted * lax.rsqrt(spread + EPSILON) * scaling


def running_sums(values):
    places = jnp.arange(values.shape[1], dtype=jnp.int32)
    upto = (places[None, :] <= places[:, None]).astype(jnp.float32)
    return jnp.einsum("im,rmj->rij", upto, values, precision=lax.Precision.HIGHEST)


def block_masks(segments, position, source, block_len):
    offsets = jnp.arange(block_len, dtype=jnp.int32)
    query_pos = position * block_len + offsets
    key_pos = source * block_len + offsets
    query_start = position * block_len
    key_start = jnp.maximum(source, 0) * block_len
    query_seg = lax.dynamic_slice_in_dim(segments, query_start, block_len, 1)
    key_seg = lax.dynamic_slice_in_dim(segments, key_start, block_len, 1)
    same_doc = (query_seg[:, :, None] == key_seg[:, None, :]) & (source >= 0)
    earlier = key_pos[None, :] < query_pos[:, None]
    reached = key_pos[None, :] <= query_pos[:, None]
    return (same_doc & reached[None], same_doc & earlier[None])


def block_logits(queries, key_heads, carried, segments, position, source, offset):
    block_len = queries.shape[1]
    scores = jnp.einsum(
        "rqhd,rkhd->rhqk", queries, key_heads, preferred_element_type=jnp.float32
    ) * (1.0 / math.sqrt(HD))
    attend_mask, select_mask = block_masks(segments, position, source, block_len)
    chosen = jnp.where(select_mask, jax.nn.softplus(scores[:, 0] - offset), 0.0)
    running = running_sums(chosen)
    penalty = carried[:, None, :] + running - chosen
    logits = jnp.where(attend_mask[:, None], scores - penalty[:, None], MASKED)
    return (scores, logits, attend_mask, select_mask, carried + running[:, -1])


def ring_body(tokens, segments, w_qkv, w_out, w_up, w_down, gain_attn, gain_mlp, cotangent):
    low_pieces = (
        w_qkv.astype(jnp.bfloat16),
        w_out.astype(jnp.bfloat16),
        w_up.astype(jnp.bfloat16),
        w_down.astype(jnp.bfloat16),
        gain_attn.astype(jnp.bfloat16),
        gain_mlp.astype(jnp.bfloat16),
    )
    gathered = (
        lax.all_gather(low_pieces[0], ("row", "seq"), axis=0, tiled=True),
        lax.all_gather(low_pieces[1], ("row", "seq"), axis=0, tiled=True),
        lax.all_gather(low_pieces[2], ("row", "seq"), axis=0, tiled=True),
        lax.all_gather(low_pieces[3], ("row", "seq"), axis=0, tiled=True),
        lax.all_gather(low_pieces[4], ("row", "seq"), axis=0, tiled=True),
        lax.all_gather(low_pieces[5], ("row", "seq"), axis=0, tiled=True),
    )
    qkv_full, out_full, up_full, down_full, attn_scale, mlp_scale = gathered
    row_count, block_len, features = tokens.shape
    token_count = row_count * block_len
    position = lax.axis_index("seq")
    sections = lax.axis_size("seq")
    offset = math.log(ROW_LEN / 2.0) + 0.5
    inputs = tokens.astype(jnp.float32).reshape(token_count, features)
    normed, attn_norm_back = jax.vjp(layer_norm, inputs, attn_scale.astype(jnp.float32))
    normed_low = normed.astype(jnp.bfloat16)
    packed = jnp.dot(normed_low, qkv_full, preferred_element_type=jnp.float32).astype(jnp.bfloat16)
    packed = packed.reshape(row_count, block_len, 3 * features)
    queries = packed[:, :, :features].reshape(row_count, block_len, H, HD)
    key_value = packed[:, :, features:]
    carried = jnp.zeros((row_count, block_len), jnp.float32)
    running_max = jnp.full((row_count, H, block_len), MASKED, jnp.float32)
    running_sum = jnp.zeros((row_count, H, block_len), jnp.float32)
    accumulated = jnp.zeros((row_count, block_len, H, HD), jnp.float32)
    kept_pairs = []
    kept_sums = []
    for section in range(sections):
        source = position - section
        key_heads = key_value[:, :, :features].reshape(row_count, block_len, H, HD)
        value_heads = key_value[:, :, features:].reshape(row_count, block_len, H, HD)
        scores, logits, attend_mask, select_mask, passed = block_logits(
            queries, key_heads, carried, segments, position, source, offset
        )
        kept_pairs.append(key_value)
        kept_sums.append(carried)
        new_max = jnp.maximum(running_max, jnp.max(logits, axis=-1))
        rescale = jnp.exp(running_max - new_max)
        exp_scores = jnp.where(attend_mask[:, None], jnp.exp(logits - new_max[..., None]), 0.0)
        running_sum = running_sum * rescale + jnp.sum(exp_scores, axis=-1)
        accumulated = accumulated * jnp.transpose(rescale, (0, 2, 1))[..., None] + jnp.einsum(
            "rhqk,rkhd->rqhd",
            exp_scores.astype(jnp.bfloat16),
            value_heads,
            preferred_element_type=jnp.float32,
        )
        running_max = new_max
        if section + 1 < sections:
            key_value = from_behind(key_value, "seq", 1)
            carried = from_behind(passed, "seq", 1)
    log_norm = running_max + jnp.log(running_sum)
    attn_heads = accumulated / jnp.transpose(running_sum, (0, 2, 1))[..., None]
    mixed_low = attn_heads.reshape(token_count, features).astype(jnp.bfloat16)
    branch = jnp.dot(mixed_low, out_full, preferred_element_type=jnp.float32)
    middle = inputs + branch
    normed_mlp, mlp_norm_back = jax.vjp(layer_norm, middle, mlp_scale.astype(jnp.float32))
    normed_mlp_low = normed_mlp.astype(jnp.bfloat16)
    hidden = jnp.dot(normed_mlp_low, up_full, preferred_element_type=jnp.float32)
    active, gelu_back = jax.vjp(partial(jax.nn.gelu, approximate=False), hidden)
    active_low = active.astype(jnp.bfloat16)
    output = (middle + jnp.dot(active_low, down_full, preferred_element_type=jnp.float32)).astype(
        jnp.bfloat16
    )
    output = output.reshape(row_count, block_len, features)
    upstream = cotangent.reshape(token_count, features)
    grad_down = jnp.dot(active_low.T, upstream, preferred_element_type=jnp.float32)
    d_active = jnp.dot(upstream, down_full.T, preferred_element_type=jnp.float32)
    d_hidden = gelu_back(d_active)[0].astype(jnp.bfloat16)
    grad_up = jnp.dot(normed_mlp_low.T, d_hidden, preferred_element_type=jnp.float32)
    d_normed_mlp = jnp.dot(d_hidden, up_full.T, preferred_element_type=jnp.float32)
    d_middle_part, grad_mlp_gain = mlp_norm_back(d_normed_mlp)
    d_middle = upstream.astype(jnp.float32) + d_middle_part
    d_branch = d_middle.astype(jnp.bfloat16)
    grad_out = jnp.dot(mixed_low.T, d_branch, preferred_element_type=jnp.float32)
    d_mixed = jnp.dot(d_branch, out_full.T, preferred_element_type=jnp.float32).astype(jnp.bfloat16)
    d_mixed = d_mixed.reshape(row_count, block_len, H, HD)
    correction = jnp.transpose(
        jnp.sum(d_mixed.astype(jnp.float32) * attn_heads, axis=-1), (0, 2, 1)
    )
    score_scale = 1.0 / math.sqrt(HD)
    grads_pair = jnp.zeros((row_count, block_len, 2 * features), jnp.float32)
    grads_column = jnp.zeros((row_count, block_len), jnp.float32)
    grad_query = jnp.zeros((row_count, block_len, H, HD), jnp.float32)
    for section in reversed(range(sections)):
        source = position - section
        key_value = kept_pairs[section]
        key_heads = key_value[:, :, :features].reshape(row_count, block_len, H, HD)
        value_heads = key_value[:, :, features:].reshape(row_count, block_len, H, HD)
        scores, logits, attend_mask, select_mask, unused = block_logits(
            queries, key_heads, kept_sums[section], segments, position, source, offset
        )
        attention = jnp.where(attend_mask[:, None], jnp.exp(logits - log_norm[..., None]), 0.0)
        attention_low = attention.astype(jnp.bfloat16)
        grad_values = jnp.einsum(
            "rhqk,rqhd->rkhd", attention_low, d_mixed, preferred_element_type=jnp.float32
        )
        grad_attention = jnp.einsum(
            "rqhd,rkhd->rhqk", d_mixed, value_heads, preferred_element_type=jnp.float32
        )
        grad_logits = attention * (grad_attention - correction[..., None])
        summed = jnp.sum(grad_logits, axis=1)
        column = jnp.sum(summed, axis=1)
        running = running_sums(summed)
        grad_chosen = jnp.where(
            select_mask, running - column[:, None, :] - grads_column[:, None, :], 0.0
        )
        grad_scores = grad_logits.at[:, 0].add(grad_chosen * jax.nn.sigmoid(scores[:, 0] - offset))
        grad_scores = grad_scores.astype(jnp.bfloat16)
        grad_query = (
            grad_query
            + jnp.einsum(
                "rhqk,rkhd->rqhd", grad_scores, key_heads, preferred_element_type=jnp.float32
            )
            * score_scale
        )
        grad_keys = (
            jnp.einsum("rhqk,rqhd->rkhd", grad_scores, queries, preferred_element_type=jnp.float32)
            * score_scale
        )
        grads_pair = grads_pair + jnp.concatenate(
            [
                grad_keys.reshape(row_count, block_len, features),
                grad_values.reshape(row_count, block_len, features),
            ],
            axis=-1,
        )
        grads_column = grads_column + column
        if section > 0:
            grads_pair, grads_column = (
                from_behind(grads_pair.astype(jnp.bfloat16), "seq", -1).astype(grads_pair.dtype),
                from_behind(grads_column.astype(jnp.bfloat16), "seq", -1).astype(
                    grads_column.dtype
                ),
            )
    d_packed = jnp.concatenate(
        [grad_query.reshape(token_count, features), grads_pair.reshape(token_count, 2 * features)],
        axis=-1,
    )
    d_packed = d_packed.astype(jnp.bfloat16)
    grad_qkv = jnp.dot(normed_low.T, d_packed, preferred_element_type=jnp.float32)
    d_normed = jnp.dot(d_packed, qkv_full.T, preferred_element_type=jnp.float32)
    d_inputs_part, grad_attn_gain = attn_norm_back(d_normed)
    d_tokens = (d_middle + d_inputs_part).reshape(row_count, block_len, features)
    gradients = (grad_qkv, grad_out, grad_up, grad_down, grad_attn_gain, grad_mlp_gain)
    reduced = (
        lax.psum_scatter(gradients[0], ("row", "seq"), scatter_dimension=0, tiled=True),
        lax.psum_scatter(gradients[1], ("row", "seq"), scatter_dimension=0, tiled=True),
        lax.psum_scatter(gradients[2], ("row", "seq"), scatter_dimension=0, tiled=True),
        lax.psum_scatter(gradients[3], ("row", "seq"), scatter_dimension=0, tiled=True),
        lax.psum_scatter(gradients[4], ("row", "seq"), scatter_dimension=0, tiled=True),
        lax.psum_scatter(gradients[5], ("row", "seq"), scatter_dimension=0, tiled=True),
    )
    return (
        output,
        d_tokens,
        reduced[0],
        reduced[1],
        reduced[2],
        reduced[3],
        reduced[4],
        reduced[5],
    )


def body(tokens, *rest):
    rows = lax.axis_size("row")
    if lax.axis_size("seq") == 2 and tokens.shape[0] == 2 and rows >= 4 and rows & (rows - 1) == 0:
        return row_body(tokens, *rest)
    return ring_body(tokens, *rest)


def solution(mesh):
    placed = (
        P("row", "seq", None),
        P("row", None),
        P(("row", "seq"), None),
        P(("row", "seq"), None),
        P(("row", "seq"), None),
        P(("row", "seq"), None),
        P(("row", "seq")),
        P(("row", "seq")),
        P("row", "seq", None),
    )
    return jax.shard_map(
        body,
        mesh=mesh,
        in_specs=placed,
        out_specs=(
            P("row", "seq", None),
            P("row", "seq", None),
            P(("row", "seq"), None),
            P(("row", "seq"), None),
            P(("row", "seq"), None),
            P(("row", "seq"), None),
            P(("row", "seq")),
            P(("row", "seq")),
        ),
        check_vma=False,
    )
```

```python
from functools import partial
import math

import jax
import jax.numpy as jnp
from jax import lax
from jax.experimental import pallas as pl
from jax.experimental.pallas import tpu as pltpu
from jax.sharding import PartitionSpec as P

H = 12
HD = 64
ROW_LEN = 2048
EPSILON = 1e-05
MASKED = -1e30
BIG = 1e30
LOG2E = 1.4426950408889634
OFFSET = math.log(ROW_LEN / 2.0) + 0.5
SAFE = 64.0
B = 256
BT = 512
MIB = 2**20
F32 = jnp.float32
BF = jnp.bfloat16


def dot(a, b):
    return jnp.dot(a, b, preferred_element_type=F32)


def dot_nt(a, b):
    return lax.dot_general(a, b, (((1,), (1,)), ((), ())), preferred_element_type=F32)


def dot_tn(a, b):
    return lax.dot_general(a, b, (((0,), (0,)), ((), ())), preferred_element_type=F32)


def iota(shape, dim):
    return lax.broadcasted_iota(jnp.int32, shape, dim)


def half_lanes(rows):
    return iota((rows, 128), 1) < HD


def pick_columns(c):
    return (iota((512, 128), 0) == 4 * iota((512, 128), 1) + c).astype(F32).astype(BF)


def pick_rows(piece, c):
    return (iota((piece, 4 * piece), 1) == 4 * iota((piece, 4 * piece), 0) + c).astype(F32).astype(BF)


def pack_kernel(qkv_ref, out_ref, up_ref, down_ref, gain_ref, a_ref, b_ref, l_ref):
    piece, features = out_ref.shape
    lane = iota((piece, 128), 1)
    a_ref[...] = qkv_ref[:, : 2 * features].astype(BF)
    b_ref[:, :features] = qkv_ref[:, 2 * features :].astype(BF)
    gains = jnp.where(lane == 0, gain_ref[:, 0:1], jnp.where(lane == 1, gain_ref[:, 1:2], 0.0))
    b_ref[:, features:] = gains.astype(BF)
    l_ref[:, :features] = out_ref[...].astype(BF)
    for c in range(4):
        pick = pick_columns(c)
        col = features * (1 + c)
        for tile in range(features // 128):
            part = up_ref[:, 512 * tile : 512 * tile + 512].astype(BF)
            l_ref[:, col + 128 * tile : col + 128 * tile + 128] = dot(part, pick).astype(BF)
        col = features * (5 + c)
        l_ref[:, col : col + features] = dot(pick_rows(piece, c), down_ref[...].astype(BF)).astype(BF)


def pack(w_qkv, w_out, w_up, w_down, gain_attn, gain_mlp):
    piece, features = w_out.shape
    return pl.pallas_call(
        pack_kernel,
        out_shape=[
            jax.ShapeDtypeStruct((piece, cols), BF) for cols in (2 * features, features + 128, 9 * features)
        ],
        name="pack_weights",
    )(w_qkv, w_out, w_up, w_down, jnp.stack([gain_attn, gain_mlp], axis=1))


def unpack_kernel(b_ref, out_ref, up_ref, down_ref):
    piece, features = out_ref.shape
    out_ref[...] = b_ref[:, :features].astype(F32)
    for tile in range(features // 128):
        total = None
        for c in range(4):
            col = features * (1 + c) + 128 * tile
            part = dot_nt(b_ref[:, col : col + 128], pick_columns(c))
            total = part if total is None else total + part
        up_ref[:, 512 * tile : 512 * tile + 512] = total
    total = None
    for c in range(4):
        col = features * (5 + c)
        part = dot_tn(pick_rows(piece, c), b_ref[:, col : col + features])
        total = part if total is None else total + part
    down_ref[...] = total


def unpack(buffer):
    piece = buffer.shape[0]
    features = (buffer.shape[1] - 128) // 9
    return pl.pallas_call(
        unpack_kernel,
        out_shape=(
            jax.ShapeDtypeStruct((piece, features), F32),
            jax.ShapeDtypeStruct((piece, 4 * features), F32),
            jax.ShapeDtypeStruct((4 * piece, features), F32),
        ),
        name="unpack_gradients",
    )(buffer)


def moments(values):
    mean_value = jnp.mean(values, axis=-1, keepdims=True)
    shifted = values - mean_value
    spread = jnp.mean(shifted * shifted, axis=-1, keepdims=True)
    return shifted, lax.rsqrt(spread + EPSILON)


def pick_half(own_ref, other_ref, step, steps):
    return jnp.where(step < steps // 2, own_ref[...], other_ref[...])


def halves(cols, steps):
    return (
        pl.BlockSpec((BT, cols), lambda t: (jnp.minimum(t, steps // 2 - 1), 0)),
        pl.BlockSpec((BT, cols), lambda t: (jnp.maximum(t - steps // 2, 0), 0)),
    )


def qkv_kernel(x_ref, other_ref, w_ref, v_w_ref, q_ref, k_ref, v_ref, rows_ref, size_ref):
    features = x_ref.shape[1]

    @pl.when(pl.program_id(0) == 0)
    def _():
        rows_ref[...] = v_w_ref[:, features:].astype(F32).T[:8]
        size_ref[...] = jnp.zeros_like(size_ref)

    shifted, scale = moments(pick_half(x_ref, other_ref, pl.program_id(0), pl.num_programs(0)).astype(F32))
    normed = (shifted * scale * rows_ref[0:1, :]).astype(BF)
    low = half_lanes(x_ref.shape[0])
    heads = (iota((features, 128), 0) // HD == iota((features, 128), 1)).astype(F32).astype(BF)

    def spread(ref, packed, other):
        for p in range(H // 2):
            pair = packed[:, 128 * p : 128 * p + 128]
            ref[:, 256 * p : 256 * p + 128] = jnp.where(low, pair, other).astype(BF)
            ref[:, 256 * p + 128 : 256 * p + 256] = jnp.where(low, other, pair).astype(BF)

    def measure(row, value):
        most = jnp.max(dot((value * value).astype(BF), heads), axis=0, keepdims=True)
        size_ref[row : row + 1] = jnp.maximum(size_ref[row : row + 1], most)

    q = dot(normed, w_ref[:, :features]) * (LOG2E / math.sqrt(HD))
    spread(q_ref, q, 0.0)
    measure(0, q)
    k = dot(normed, w_ref[:, features:])
    spread(k_ref, k, 1.0)
    measure(1, k)
    spread(v_ref, dot(normed, v_w_ref[:, :features]), 1.0)


def project_qkv(own, other, w_qk, w_v):
    tokens, features = 2 * own.shape[0], own.shape[1]
    steps = tokens // BT

    def tall(cols):
        return pl.BlockSpec((BT, cols), lambda t: (t, 0))

    def whole(array):
        return pl.BlockSpec(array.shape, lambda t: (0, 0))

    return pl.pallas_call(
        qkv_kernel,
        grid=(steps,),
        in_specs=[*halves(features, steps), whole(w_qk), whole(w_v)],
        out_specs=[
            tall(2 * features),
            tall(2 * features),
            tall(2 * features),
            pl.BlockSpec((8, features), lambda t: (0, 0)),
            pl.BlockSpec((8, 128), lambda t: (0, 0)),
        ],
        out_shape=[
            jax.ShapeDtypeStruct((tokens, 2 * features), BF),
            jax.ShapeDtypeStruct((tokens, 2 * features), BF),
            jax.ShapeDtypeStruct((tokens, 2 * features), BF),
            jax.ShapeDtypeStruct((8, features), F32),
            jax.ShapeDtypeStruct((8, 128), F32),
        ],
        compiler_params=pltpu.CompilerParams(vmem_limit_bytes=48 * MIB),
        name="project_qkv",
    )(own, other, w_qk, w_v)


def pick(h):
    return slice(128 * h, 128 * h + 128)


def block_rows(index):
    return pl.ds(pl.multiple_of(index * B, B), B)


def two_part(tri, values):
    high = values.astype(BF)
    rest = (values - high.astype(F32)).astype(BF)
    return dot(tri, high) + dot(tri, rest)


def selection(scores, segq, segk, rows, cols):
    earlier = (segq == segk) & (cols < rows)
    x = scores - OFFSET * LOG2E
    grown = jnp.exp2(jnp.minimum(x, 100.0))
    more = 1.0 + grown
    return jnp.where(earlier, jnp.maximum(x, jnp.log2(more)), 0.0), jnp.where(earlier, grown / more, 0.0)


def mixed(first, second):
    done = 0
    for n, step in enumerate(first):
        step()
        upto = (n + 1) * len(second) // len(first)
        for other in second[done:upto]:
            other()
        done = upto


STRIP = 64
LEAD = 2


def key_copies(block, stored, k_any, v_any, kx, vx, sem):
    rows = block_rows(stored)
    return (
        pltpu.make_async_copy(k_any.at[rows, :], kx.at[block], sem.at[0, block]),
        pltpu.make_async_copy(v_any.at[rows, :], vx.at[block], sem.at[1, block]),
    )


def forward_kernel(tab, slow, q_ref, q0_ref, k0_ref, segq_ref, segk_ref, k_any, v_any, o_ref, li_ref, e_ref,
                   acc, carry, tri, qx, penalty, gate, work, high, kx, vx, sem):
    t = pl.program_id(0)
    ib, jb = tab[2, t], tab[3, t]

    @pl.when(t == 0)
    def _():
        for block in range(kx.shape[0]):
            for copy in key_copies(block, tab[1, block * (block + 3) // 2], k_any, v_any, kx, vx, sem):
                copy.start()

    def prepare(step, slot):
        keys = block_rows(tab[1, step])
        at = tab[3, step]
        ahead = (tab[2, step] - at) * B
        segk = segk_ref[tab[1, step], 0:1, :]
        sums = []

        def scores():
            work[...] = dot_nt(q0_ref[block_rows(tab[0, step]), :], k0_ref[keys, :])

        def strip(n):
            part = slice(STRIP * n, STRIP * n + STRIP)
            segq = segq_ref[pl.ds(pl.multiple_of(tab[0, step] * B + STRIP * n, STRIP), STRIP), :]
            return part, segq, iota((STRIP, B), 0) + (ahead + STRIP * n), iota((STRIP, B), 1)

        def choose(n):
            part, segq, rows, cols = strip(n)
            chosen, opened = selection(work[part, :], segq, segk, rows, cols)
            gate[slot, part, :] = opened.astype(BF)
            high[part, :] = chosen.astype(BF)
            sums.append(jnp.sum(chosen, axis=0, keepdims=True))

        def add():
            before = carry[at, 0:1, :]
            work[...] = dot(tri[...], high[...]) + before
            carry[at, 0:1, :] = before + sum(sums[1:], sums[0])

        def close(n):
            part, segq, rows, cols = strip(n)
            penalty[slot, part, :] = jnp.where((segq == segk) & (cols <= rows), work[part, :], BIG)

        count = range(B // STRIP)
        return [scores] + [partial(choose, n) for n in count] + [add] + [partial(close, n) for n in count]

    @pl.when(t == 0)
    def _():
        carry[...] = jnp.zeros_like(carry)
        tri[...] = (iota((B, B), 1) < iota((B, B), 0)).astype(F32).astype(BF)
        for step in prepare(0, 0):
            step()

    @pl.when(jb == 0)
    def _():
        acc[...] = jnp.zeros_like(acc)
        qx[...] = q_ref[...]
        for copy in key_copies(ib, tab[0, t], k_any, v_any, kx, vx, sem):
            copy.wait()

        @pl.when(slow[0] != 0)
        def _():
            lane = iota((B, 128), 1)
            segq = segq_ref[block_rows(tab[0, t]), :]
            cols = iota((B, B), 1)

            def chosen(other):
                rows = iota((B, B), 0) + (ib - other) * B
                base = tab[1, t + other]
                first = dot_nt(q_ref[:, 0:128], k0_ref[block_rows(base), :])
                return selection(first, segq, segk_ref[base, 0:1, :], rows, cols)[0]

            own = jnp.sum(chosen(0), axis=0, keepdims=True)

            def step(other, top):
                base = tab[1, t + other]
                before = carry[other, 0:1, :] - jnp.where(other == 0, own, 0.0)
                kept = (segq == segk_ref[base, 0:1, :]) & (cols <= iota((B, B), 0) + (ib - other) * B)
                z_penalty = jnp.where(kept, dot(tri[...], chosen(other).astype(BF)) + before, BIG)
                for h in range(H):
                    z = dot_nt(q_ref[:, pick(h)], kx[other, :, pick(h)]) - z_penalty
                    top = jnp.where(lane == h, jnp.maximum(top, jnp.max(z, axis=1, keepdims=True)), top)
                return top

            top = lax.fori_loop(0, ib + 1, step, jnp.full((B, 128), -BIG, F32))
            for h in range(H):
                shift = -jnp.sum(jnp.where(lane == h, top, 0.0), axis=1, keepdims=True)
                one = shift.astype(BF).astype(F32)
                two = (shift - one).astype(BF).astype(F32)
                three = shift - one - two
                at = lane - (HD if h % 2 == 0 else 0)
                extra = jnp.where(at == 0, one, jnp.where(at == 1, two, jnp.where(at == 2, three, 0.0)))
                keep = (lane < HD) if h % 2 == 0 else (lane >= HD)
                qx[:, pick(h)] = jnp.where(keep, q_ref[:, pick(h)].astype(F32), extra).astype(BF)

    slot = t % 2

    def head(h):
        e = jnp.exp2(dot_nt(qx[:, pick(h)], kx[jb, :, pick(h)]) - penalty[slot]).astype(BF)
        e_ref[0, h] = e

    def value(h):
        acc[:, pick(h)] += dot(e_ref[0, h], vx[jb, :, pick(h)])

    e_ref[0, H] = gate[slot]
    steps = [partial(head, h) for h in range(LEAD)]
    for h in range(H):
        if h + LEAD < H:
            steps.append(partial(head, h + LEAD))
        steps.append(partial(value, h))
    mixed(steps, prepare(t + 1, 1 - slot))

    @pl.when(jb == ib)
    def _():
        low = half_lanes(B)
        for p in range(H // 2):
            one = acc[:, pick(2 * p)]
            two = acc[:, pick(2 * p + 1)]
            inverse = 1.0 / pltpu.roll(jnp.where(low, two, one), HD, 1)
            o_ref[:, pick(p)] = (jnp.where(low, one, two) * inverse).astype(BF)
            li_ref[:, pick(p)] = inverse


def attention_forward(table, slow, q, k, v, seg_col, seg_row):
    tokens = q.shape[0]
    blocks = tokens // B
    tiles = table.shape[1] - 1
    wide = 128 * H
    narrow = HD * H
    once = pl.Buffered(1)
    return pl.pallas_call(
        forward_kernel,
        grid_spec=pltpu.PrefetchScalarGridSpec(
            num_scalar_prefetch=2,
            grid=(tiles,),
            in_specs=[
                pl.BlockSpec((B, wide), lambda t, tab, slow: (tab[0, t], 0)),
                pl.BlockSpec((tokens, 128), lambda t, tab, slow: (0, 0), pipeline_mode=once),
                pl.BlockSpec((tokens, 128), lambda t, tab, slow: (0, 0), pipeline_mode=once),
                pl.BlockSpec((tokens, 1), lambda t, tab, slow: (0, 0), pipeline_mode=once),
                pl.BlockSpec((blocks, 8, B), lambda t, tab, slow: (0, 0, 0), pipeline_mode=once),
                pl.BlockSpec(memory_space=pl.ANY),
                pl.BlockSpec(memory_space=pl.ANY),
            ],
            out_specs=[
                pl.BlockSpec((B, narrow), lambda t, tab, slow: (tab[0, t], 0)),
                pl.BlockSpec((B, narrow), lambda t, tab, slow: (tab[0, t], 0)),
                pl.BlockSpec((1, H + 1, B, B), lambda t, tab, slow: (tab[4, t], 0, 0, 0)),
            ],
            scratch_shapes=[
                pltpu.VMEM((B, wide), F32),
                pltpu.VMEM((blocks, 8, B), F32),
                pltpu.VMEM((B, B), BF),
                pltpu.VMEM((B, wide), BF),
                pltpu.VMEM((2, B, B), F32),
                pltpu.VMEM((2, B, B), BF),
                pltpu.VMEM((B, B), F32),
                pltpu.VMEM((B, B), BF),
                pltpu.VMEM((blocks, B, wide), BF),
                pltpu.VMEM((blocks, B, wide), BF),
                pltpu.SemaphoreType.DMA((2, blocks)),
            ],
        ),
        out_shape=[
            jax.ShapeDtypeStruct((tokens, narrow), BF),
            jax.ShapeDtypeStruct((tokens, narrow), F32),
            jax.ShapeDtypeStruct((tiles, H + 1, B, B), BF),
        ],
        compiler_params=pltpu.CompilerParams(vmem_limit_bytes=48 * MIB),
        name="attention_forward",
    )(table, slow, q, q, k, seg_col, seg_row, k, v)


def backward_kernel(tab, e_ref, q_ref, d_ref, q0_ref, k0_ref, k_any, v_any, o_ref,
                    dq, dkt, dvt, carry, tri, sums, first, gate, work, kx, vx, sem):
    t = pl.program_id(0)
    last = pl.num_programs(0) - 1
    before = jnp.maximum(t - 1, 0)
    narrow = HD * H
    low = half_lanes(B)
    slot = t % 2

    @pl.when(t == 0)
    def _():
        for block in range(kx.shape[0]):
            for copy in key_copies(block, tab[1, block], k_any, v_any, kx, vx, sem):
                copy.start()
        carry[...] = jnp.zeros_like(carry)
        tri[...] = (iota((B, B), 1) > iota((B, B), 0)).astype(F32).astype(BF)
        dkt[...] = jnp.zeros_like(dkt)
        dvt[...] = jnp.zeros_like(dvt)
        dq[...] = jnp.zeros_like(dq)
        sums[...] = jnp.zeros_like(sums)
        first[...] = jnp.zeros_like(first)
        gate[...] = jnp.zeros_like(gate)

    @pl.when((tab[3, t] == 0) & (t < last))
    def _():
        dq[tab[2, t] % 2] = jnp.zeros(dq.shape[1:], F32)

    @pl.when(t < kx.shape[0])
    def _():
        for copy in key_copies(t, tab[1, t], k_any, v_any, kx, vx, sem):
            copy.wait()

    def finish():
        at = tab[3, before]

        def add():
            total = sums[1 - slot]
            later = carry[at, 0:1, :] + two_part(tri[...], total)
            carry[at, 0:1, :] = carry[at, 0:1, :] + jnp.sum(total, axis=0, keepdims=True)
            work[...] = (first[1 - slot] - later * gate[1 - slot].astype(F32)).astype(BF)

        def keys():
            dkt[:HD, block_rows(at)] += dot_tn(q0_ref[block_rows(tab[0, before]), :], work[...])[:HD]

        def queries():
            more = dot(work[...], k0_ref[block_rows(tab[1, before]), :])
            dq[tab[2, before] % 2, :, :128] += jnp.where(low, more, 0.0)

        return [add, keys, queries]

    @pl.when(t == last)
    def _():
        for step in finish():
            step()

    @pl.when(t < last)
    def _():
        cols = block_rows(tab[3, t])
        turn = tab[2, t] % 2
        kept = {}
        parts = {}

        def score(h):
            e = e_ref[0, h]
            dz = e.astype(F32) * dot_nt(d_ref[:, pick(h)], vx[tab[3, t], :, pick(h)])
            if h == 0:
                first[slot] = dz
                sums[slot] = dz
            else:
                sums[slot] += dz
                kept[h] = dz.astype(BF)

        def products(h):
            own = slice(HD * h, HD * h + HD)
            data = slice(HD * (h % 2), HD * (h % 2) + HD)
            dvt[own, cols] += dot_tn(d_ref[:, pick(h)], e_ref[0, h])[data]
            if h == 0:
                parts[0] = 0.0
                return
            ds = kept.pop(h)
            dkt[own, cols] += dot_tn(q_ref[:, pick(h)], ds)[data]
            parts[h] = dot(ds, kx[tab[3, t], :, pick(h)])
            if h % 2:
                dq[turn, :, pick(h // 2)] += jnp.where(low, parts.pop(h - 1), parts.pop(h))

        gate[slot] = e_ref[0, H]
        steps = [partial(score, h) for h in range(LEAD)]
        for h in range(H):
            if h + LEAD < H:
                steps.append(partial(score, h + LEAD))
            steps.append(partial(products, h))
        mixed(steps, finish())

    @pl.when((t > 0) & (tab[3, before] == tab[2, before]))
    def _():
        cols = block_rows(tab[2, before])
        o_ref[:, :narrow] = (dq[tab[2, before] % 2] * (1.0 / math.sqrt(HD))).astype(BF)
        o_ref[:, narrow : 2 * narrow] = (dkt[:, cols] * (1.0 / LOG2E)).astype(BF).T
        o_ref[:, 2 * narrow :] = dvt[:, cols].astype(BF).T


def attention_backward(table, e, q, k, v, d):
    tokens = q.shape[0]
    blocks = tokens // B
    tiles = table.shape[1] - 1
    wide = 128 * H
    narrow = HD * H
    once = pl.Buffered(1)
    return pl.pallas_call(
        backward_kernel,
        grid_spec=pltpu.PrefetchScalarGridSpec(
            num_scalar_prefetch=1,
            grid=(tiles + 1,),
            in_specs=[
                pl.BlockSpec((1, H + 1, B, B), lambda t, tab: (tab[4, t], 0, 0, 0)),
                pl.BlockSpec((B, wide), lambda t, tab: (tab[0, t], 0)),
                pl.BlockSpec((B, wide), lambda t, tab: (tab[0, t], 0)),
                pl.BlockSpec((tokens, 128), lambda t, tab: (0, 0), pipeline_mode=once),
                pl.BlockSpec((tokens, 128), lambda t, tab: (0, 0), pipeline_mode=once),
                pl.BlockSpec(memory_space=pl.ANY),
                pl.BlockSpec(memory_space=pl.ANY),
            ],
            out_specs=pl.BlockSpec((B, 3 * narrow), lambda t, tab: (tab[0, jnp.maximum(t - 1, 0)], 0)),
            scratch_shapes=[
                pltpu.VMEM((2, B, narrow), F32),
                pltpu.VMEM((narrow, tokens), F32),
                pltpu.VMEM((narrow, tokens), F32),
                pltpu.VMEM((blocks, 8, B), F32),
                pltpu.VMEM((B, B), BF),
                pltpu.VMEM((2, B, B), F32),
                pltpu.VMEM((2, B, B), F32),
                pltpu.VMEM((2, B, B), BF),
                pltpu.VMEM((B, B), BF),
                pltpu.VMEM((blocks, B, wide), BF),
                pltpu.VMEM((blocks, B, wide), BF),
                pltpu.SemaphoreType.DMA((2, blocks)),
            ],
        ),
        out_shape=jax.ShapeDtypeStruct((tokens, 3 * narrow), BF),
        compiler_params=pltpu.CompilerParams(vmem_limit_bytes=56 * MIB),
        cost_estimate=pl.CostEstimate(flops=tiles * H * B * B * 1024, bytes_accessed=tiles * B * B, transcendentals=0),
        name="attention_backward",
    )(table, e, q, d, q, k, k, v)


def tile_tables(blocks, position):
    pairs = [(i, j) for i in range(blocks) for j in range(i + 1)]
    back = [(i, j) for i in reversed(range(blocks)) for j in range(i + 1)]
    shift = position * (blocks // 2)

    def table(order):
        order = order + order[-1:]
        rows = jnp.array([i for i, _ in order], jnp.int32)
        keys = jnp.array([j for _, j in order], jnp.int32)
        return jnp.stack(
            [(rows + shift) % blocks, (keys + shift) % blocks, rows, keys, rows * (rows + 1) // 2 + keys]
        )

    return table(pairs), table(back)


PART = 256
ROWS = 64


def mlp_kernel(x_ref, x2_ref, ob_ref, dy1_ref, dy2_ref, li_ref, gain_ref, wo_ref, wu_ref, wd_ref, out_ref, dx_ref, d_ref, g_any,
               xh, scales, y, dn, n2, gup, gdown, gout, gsum, stage, gcol, us, das, actives, dus, sem):
    c, t = pl.program_id(0), pl.program_id(1)
    chunks, steps = pl.num_programs(0), pl.num_programs(1)
    rows = pl.ds(pl.multiple_of(t * BT, BT), BT)
    features = x_ref.shape[1]

    def send(slot, column):
        start = pl.multiple_of(column, 128)
        return pltpu.make_async_copy(stage.at[slot], g_any.at[:, pl.ds(start, features)], sem.at[slot])

    @pl.when(c == 0)
    def _():
        middle = pick_half(x_ref, x2_ref, t, steps).astype(F32) + dot(ob_ref[...], wo_ref[...])
        shifted, scale = moments(middle)
        xh[rows, :] = (shifted * scale).astype(BF)
        scales[rows, :] = jnp.broadcast_to(scale, (BT, 128))
        y[rows, :] = middle
        dn[rows, :] = jnp.zeros_like(middle)
        n2[rows, :] = (shifted * scale * gain_ref[1:2, :]).astype(BF)

    @pl.when(t == 0)
    def _():
        gup[...] = jnp.zeros_like(gup)
        gdown[...] = jnp.zeros_like(gdown)

    @pl.when((c == 0) & (t == 0))
    def _():
        gout[...] = jnp.zeros_like(gout)
        gsum[...] = jnp.zeros_like(gsum)

    n2_low = n2[rows, :]
    dy_low = pick_half(dy1_ref, dy2_ref, t, steps)

    def enter(p):
        units = slice(PART * p, PART * p + PART)

        def up():
            us[p % 2] = dot(n2_low, wu_ref[:, units])

        def down():
            das[p % 2] = dot_nt(dy_low, wd_ref[units, :])

        return [up, down]

    def bend(p, n):
        part = slice(ROWS * n, ROWS * n + ROWS)
        u = us[p % 2, part, :]
        cdf = 0.5 * (1.0 + lax.erf(u * math.sqrt(0.5)))
        density = jnp.exp(-0.5 * u * u) * (1.0 / math.sqrt(2.0 * math.pi))
        units = slice(PART * p, PART * p + PART)
        actives[part, units] = (u * cdf).astype(BF)
        dus[part, units] = ((cdf + u * density) * das[p % 2, part, :]).astype(BF)

    def leave(p):
        units = slice(PART * p, PART * p + PART)

        def down():
            y[rows, :] += dot(actives[:, units], wd_ref[units, :])

        def up():
            dn[rows, :] += dot_nt(dus[:, units], wu_ref[:, units])

        return [down, up]

    parts = features // PART
    for step in enter(0):
        step()
    for p in range(parts):
        products = (leave(p - 1) if p else []) + (enter(p + 1) if p + 1 < parts else [])
        mixed(products, [partial(bend, p, n) for n in range(BT // ROWS)])
    for step in leave(parts - 1):
        step()
    gdown[...] += dot_tn(actives[...], dy_low)
    gup[...] += dot_tn(n2_low, dus[...])

    @pl.when(t == steps - 1)
    def _():
        @pl.when(c > 0)
        def _():
            send(0, c * features).wait()
            send(1, (c + chunks) * features).wait()

        stage[0] = gup[...].astype(BF)
        stage[1] = gdown[...].astype(BF)
        send(0, (1 + c) * features).start()
        send(1, (1 + c + chunks) * features).start()

    @pl.when(c == chunks - 1)
    def _():
        out_ref[...] = y[rows, :].astype(BF)
        d_normed = dn[rows, :]
        scale = scales[rows, 0:1]
        unit = xh[rows, :].astype(F32)
        product = d_normed * unit
        gsum[...] += jnp.sum(product.reshape(BT // 8, 8, features), axis=0)
        inner = d_normed * gain_ref[1:2, :]
        dx = dy_low.astype(F32) + scale * (
            inner - jnp.mean(inner, axis=-1, keepdims=True) - unit * jnp.mean(inner * unit, axis=-1, keepdims=True)
        )
        dx_ref[...] = dx.astype(BF)
        db = dx.astype(BF)
        gout[...] += dot_tn(ob_ref[...], db)
        scaled = dot_nt(db, wo_ref[...]) * li_ref[...]
        low = half_lanes(BT)
        lane = iota((BT, 128), 1)
        swap_row, swap_col = iota((128, 128), 0), iota((128, 128), 1)
        swap = ((swap_row // HD != swap_col // HD) & (swap_col % HD < 2)).astype(F32).astype(BF)
        for p in range(H // 2):
            w = slice(128 * p, 128 * p + 128)
            pair = scaled[:, w]
            both = pair * ob_ref[:, w].astype(F32)
            high = both.astype(BF)
            delta = dot(high, swap) + dot((both - high.astype(F32)).astype(BF), swap)
            top = delta.astype(BF).astype(F32)
            extra = jnp.where((lane == 0) | (lane == HD), -top, top - delta)
            d_ref[:, 256 * p : 256 * p + 128] = jnp.where(low, pair, extra).astype(BF)
            d_ref[:, 256 * p + 128 : 256 * p + 256] = jnp.where(low, extra, pair).astype(BF)

    @pl.when((c == chunks - 1) & (t == steps - 1))
    def _():
        stage[2] = gout[...].astype(BF)
        column = jnp.broadcast_to(jnp.sum(gsum[...], axis=0, keepdims=True), (128, features))
        gcol[...] = column.T.astype(BF)
        last = pltpu.make_async_copy(
            gcol, g_any.at[:, pl.ds((1 + 2 * 4) * features, 128)], sem.at[3]
        )
        send(2, 0).start()
        last.start()
        send(0, chunks * features).wait()
        send(1, 2 * chunks * features).wait()
        send(2, 0).wait()
        last.wait()


def feed_forward(x, x_other, ob, dy, dy_other, li, gains, weights):
    tokens, features = ob.shape
    steps = tokens // BT
    chunks = 4

    def ends(c, t):
        return (jnp.where((c == 0) | (c == chunks - 1), t, steps - 1), 0)

    def own(t):
        return jnp.minimum(t, steps // 2 - 1)

    def other(t):
        return jnp.maximum(t - steps // 2, 0)

    def at_last(c, t):
        return (jnp.where(c == chunks - 1, t, 0), 0)

    block = (BT, features)
    once = pl.Buffered(1)
    return pl.pallas_call(
        mlp_kernel,
        grid=(chunks, steps),
        in_specs=[
            pl.BlockSpec(block, lambda c, t: (own(jnp.where(c == 0, t, steps - 1)), 0), pipeline_mode=once),
            pl.BlockSpec(block, lambda c, t: (other(jnp.where(c == 0, t, steps - 1)), 0), pipeline_mode=once),
            pl.BlockSpec(block, ends),
            pl.BlockSpec(block, lambda c, t: (own(t), 0)),
            pl.BlockSpec(block, lambda c, t: (other(t), 0)),
            pl.BlockSpec(block, at_last),
            pl.BlockSpec((8, features), lambda c, t: (0, 0)),
            pl.BlockSpec((features, features), lambda c, t: (0, 0), pipeline_mode=once),
            pl.BlockSpec((features, features), lambda c, t: (0, 1 + c)),
            pl.BlockSpec((features, features), lambda c, t: (0, 1 + chunks + c)),
        ],
        out_specs=[
            pl.BlockSpec(block, at_last),
            pl.BlockSpec(block, at_last),
            pl.BlockSpec((BT, 2 * features), at_last),
            pl.BlockSpec(memory_space=pl.ANY),
        ],
        out_shape=[
            jax.ShapeDtypeStruct((tokens, features), BF),
            jax.ShapeDtypeStruct((tokens, features), BF),
            jax.ShapeDtypeStruct((tokens, 2 * features), BF),
            jax.ShapeDtypeStruct((features, 9 * features + 128), BF),
        ],
        scratch_shapes=[
            pltpu.VMEM((tokens, features), BF),
            pltpu.VMEM((tokens, 128), F32),
            pltpu.VMEM((tokens, features), F32),
            pltpu.VMEM((tokens, features), F32),
            pltpu.VMEM((tokens, features), BF),
            pltpu.VMEM((features, features), F32),
            pltpu.VMEM((features, features), F32),
            pltpu.VMEM((features, features), F32),
            pltpu.VMEM((8, features), F32),
            pltpu.VMEM((3, features, features), BF),
            pltpu.VMEM((features, 128), BF),
            pltpu.VMEM((2, BT, PART), F32),
            pltpu.VMEM((2, BT, PART), F32),
            pltpu.VMEM((BT, features), BF),
            pltpu.VMEM((BT, features), BF),
            pltpu.SemaphoreType.DMA((4,)),
        ],
        compiler_params=pltpu.CompilerParams(vmem_limit_bytes=63 * MIB),
        name="feed_forward",
    )(x, x_other, ob, dy, dy_other, li, gains, weights, weights, weights)


def weight_order(bits, dims):
    return [
        sum(((place >> (bits - 1 - n)) & 1) << dim for n, dim in enumerate(dims)) for place in range(2**bits)
    ]


def weight_kernel(x_ref, other_ref, dqkv_ref, gain_ref, a_ref, b_ref, acc, *, orders):
    t = pl.program_id(0)

    @pl.when(t == 0)
    def _():
        acc[...] = jnp.zeros_like(acc)

    shifted, scale = moments(pick_half(x_ref, other_ref, t, pl.num_programs(0)).astype(F32))
    normed = (shifted * scale * gain_ref[0:1, :]).astype(BF)
    acc[...] += dot_tn(normed, dqkv_ref[...])

    @pl.when(t == pl.num_programs(0) - 1)
    def _():
        _, piece, split = a_ref.shape
        for place, block in enumerate(orders[0]):
            a_ref[place] = acc[piece * block : piece * block + piece, :split].astype(BF)
        for place, block in enumerate(orders[1]):
            b_ref[place] = acc[piece * block : piece * block + piece, split:].astype(BF)


def first_weight_gradient(x, x_other, dqkv, gains, orders):
    tokens, features = dqkv.shape[0], x.shape[1]
    steps = tokens // BT
    blocks = len(orders[0])
    shapes = [(blocks, features // blocks, cols) for cols in (2 * features, features)]
    return pl.pallas_call(
        partial(weight_kernel, orders=orders),
        grid=(steps,),
        in_specs=[
            *halves(features, steps),
            pl.BlockSpec((BT, 3 * features), lambda t: (t, 0)),
            pl.BlockSpec(gains.shape, lambda t: (0, 0)),
        ],
        out_specs=[pl.BlockSpec(shape, lambda t: (0, 0, 0)) for shape in shapes],
        out_shape=[jax.ShapeDtypeStruct(shape, BF) for shape in shapes],
        scratch_shapes=[pltpu.VMEM((features, 3 * features), F32)],
        compiler_params=pltpu.CompilerParams(vmem_limit_bytes=48 * MIB),
        cost_estimate=pl.CostEstimate(
            flops=12 * tokens * features * features, bytes_accessed=16 * tokens * features, transcendentals=0
        ),
        name="first_weight_gradient",
    )(x, x_other, dqkv, gains)


def tokens_kernel(x_ref, dqkv_ref, dx_ref, gain_ref, w_ref, v_w_ref, first_ref, out_ref, gsum_ref):
    features = x_ref.shape[1]

    @pl.when(pl.program_id(0) == 0)
    def _():
        gsum_ref[...] = jnp.zeros_like(gsum_ref)

    shifted, scale = moments(x_ref[...].astype(F32))
    xh = shifted * scale
    d_normed = dot_nt(dqkv_ref[:, : 2 * features], w_ref[...])
    d_normed += dot_nt(dqkv_ref[:, 2 * features :], v_w_ref[:, :features])
    gsum_ref[...] += jnp.sum((d_normed * xh).reshape(BT // 8, 8, features), axis=0)
    inner = d_normed * gain_ref[0:1, :]
    dx = dx_ref[...].astype(F32) + scale * (
        inner - jnp.mean(inner, axis=-1, keepdims=True) - xh * jnp.mean(inner * xh, axis=-1, keepdims=True)
    )
    out_ref[...] = dx.astype(out_ref.dtype)


def first_token_gradient(x, dqkv, dx, gains, w_qk, w_v, first, half, dtype):
    tokens, features = x.shape
    steps = tokens // BT

    def tall(cols):
        return pl.BlockSpec((BT, cols), lambda t: (t + half * steps, 0))

    def whole(array):
        return pl.BlockSpec(array.shape, lambda t: (0, 0))

    own = pl.BlockSpec((BT, features), lambda t: (t, 0))
    return pl.pallas_call(
        tokens_kernel,
        grid=(steps,),
        in_specs=[own, tall(3 * features), tall(features), whole(gains), whole(w_qk), whole(w_v), pl.BlockSpec(memory_space=pl.ANY)],
        out_specs=[own, pl.BlockSpec((8, features), lambda t: (0, 0))],
        out_shape=[jax.ShapeDtypeStruct((tokens, features), dtype), jax.ShapeDtypeStruct((8, features), F32)],
        compiler_params=pltpu.CompilerParams(vmem_limit_bytes=48 * MIB),
        cost_estimate=pl.CostEstimate(
            flops=12 * tokens * features * features, bytes_accessed=16 * tokens * features, transcendentals=0
        ),
        name="first_token_gradient",
    )(x, dqkv, dx, gains, w_qk, w_v, first)


def swap(value):
    return lax.ppermute(value, "seq", [(0, 1), (1, 0)])


def own_and_other(pair, position):
    return (
        lax.dynamic_index_in_dim(pair, position, 0, keepdims=False),
        lax.dynamic_index_in_dim(pair, 1 - position, 0, keepdims=False),
    )


def in_order(own, other, position):
    return jnp.where(position == 0, jnp.stack([own, other]), jnp.stack([other, own]))


def exchange(value, dim):
    axis = "seq" if dim == 0 else "row"
    step = 1 if dim == 0 else 1 << (dim - 1)
    return lax.ppermute(value, axis, [(i, i ^ step) for i in range(lax.axis_size(axis))])


def bit(dim):
    return lax.axis_index("seq") if dim == 0 else (lax.axis_index("row") >> (dim - 1)) & 1


def doubled(array, shape, held, dim):
    other = exchange(array, dim)
    outer = sum(1 for d in held if d > dim)
    own = array.reshape(2**outer, -1, *shape)
    other = other.reshape(own.shape)
    both = jnp.where(bit(dim) == 0, jnp.stack([own, other], 1), jnp.stack([other, own], 1))
    return both.reshape(-1, *shape)


def halved(value, dim):
    half = value.shape[0] // 2
    mine = bit(dim)
    keep = lax.dynamic_slice_in_dim(value, mine * half, half, 0)
    send = lax.dynamic_slice_in_dim(value, (1 - mine) * half, half, 0)
    return keep + exchange(send, dim)


def cut(value, shares):
    rows = value.shape[0] // sum(shares)
    ends = [rows * sum(shares[: n + 1]) for n in range(len(shares))]
    return [value[end - rows * share : end] for share, end in zip(shares, ends) if share]


def after(value, *others):
    return lax.optimization_barrier((value, *others))[0]


def row_body(tokens, segments, w_qkv, w_out, w_up, w_down, gain_attn, gain_mlp, cotangent):
    both = ("row", "seq")
    position = lax.axis_index("seq")
    devices = 2 * lax.axis_size("row")
    bits = devices.bit_length() - 1
    far = tuple(range(3, bits))
    _, half, features = tokens.shape
    *pieces, later_piece = pack(w_qkv, w_out, w_up, w_down, gain_attn, gain_mlp)
    x, other = own_and_other(tokens, position)
    paths = ((0, *reversed(far), 2, 1), (0, 2, *reversed(far), 1))
    gathered = [piece[None] for piece in pieces]
    parts = cut(other, [0] * (bits - 4) + [2, 2, 3, 1])
    x_parts = []
    for stage in range(bits):
        if stage:
            *gathered, x_parts, parts = lax.optimization_barrier((*gathered, x_parts, parts))
        if stage == bits - 2:
            later_piece = after(later_piece, *gathered)
        for n, path in enumerate(paths):
            gathered[n] = doubled(gathered[n], pieces[n].shape, path[:stage], path[stage])
        if stage and parts:
            x_parts = x_parts + [swap(parts[0])]
            parts = parts[1:]
    x_other = jnp.concatenate(x_parts)
    w_qk, w_v = [array.reshape(-1, array.shape[-1]) for array in gathered]
    w_later = lax.all_gather(later_piece, both, axis=0, tiled=True)
    dy, other = own_and_other(cotangent, position)
    dy_other = swap(after(other, w_qk, x_other))
    row_segments = lax.dynamic_index_in_dim(segments, position, 0, keepdims=False)
    stored = jnp.roll(row_segments, position * half)
    seg_col = stored[:, None]
    seg_row = jnp.broadcast_to(stored.reshape(-1, 1, B), (stored.shape[0] // B, 8, B))
    q, k, v, gains, sizes = project_qkv(x, x_other, w_qk, w_v)
    slow = jnp.any(sizes[0] * sizes[1] * 1.05 > SAFE * SAFE).astype(jnp.int32)[None]
    table, back_table = tile_tables(2 * half // B, position)
    ob, li, e = attention_forward(table, slow, q, k, v, seg_col, seg_row)
    output, dx, d, g_later = feed_forward(x, x_other, ob, dy, dy_other, li, gains, w_later)
    r_later = lax.psum_scatter(g_later, both, scatter_dimension=0, tiled=True)
    output_other = swap(output[half:])
    dqkv = attention_backward(back_table, e, q, k, v, d)
    dqkv, output_other = lax.optimization_barrier((dqkv, output_other))
    paths = ((1, 2, *far, 0), (1, *far, 2, 0))
    orders = [weight_order(bits, path) for path in paths]
    summed = list(first_weight_gradient(x, x_other, dqkv, gains, orders))
    d_other, sum_other = first_token_gradient(x_other, dqkv, dx, gains, w_qk, w_v, summed[0], 1, BF)
    parts = cut(d_other, [0] * (bits - 5) + [1, 1, 1, 1])
    d_parts = []
    for stage in range(bits):
        if stage == bits - 2:
            summed[0], r_later = lax.optimization_barrier((summed[0], r_later))
        if stage:
            *summed, d_parts, parts = lax.optimization_barrier((*summed, d_parts, parts))
        else:
            summed = list(lax.optimization_barrier(tuple(summed)))
        if stage > 1:
            summed[0], g_gain = lax.optimization_barrier((summed[0], g_gain))
        for n, path in enumerate(paths):
            summed[n] = halved(summed[n], path[stage])
        if stage and parts:
            d_parts = d_parts + [swap(parts[0])]
            parts = parts[1:]
        if stage:
            g_gain = halved(g_gain, paths[0][stage - 1])
        else:
            d_own, sum_own = first_token_gradient(x, dqkv, dx, gains, w_qk, w_v, summed[0], 0, F32)
            sums = jnp.sum(sum_other + sum_own, axis=0)
            g_gain = jnp.transpose(sums.reshape(*[2] * bits, -1), [bits - 1 - dim for dim in paths[0]] + [bits])
            g_gain = g_gain.reshape(devices, 1, -1)
    g_gain = halved(g_gain, paths[0][-1])
    output = in_order(output[:half], output_other, position)
    d_tokens = in_order(d_own, jnp.concatenate(d_parts).astype(F32), position)
    g_out, g_up, g_down = unpack(r_later)
    return (
        output,
        d_tokens,
        jnp.concatenate([summed[0][0], summed[1][0]], axis=1).astype(F32),
        g_out,
        g_up,
        g_down,
        g_gain[0, 0],
        r_later[:, 9 * features].astype(F32),
    )


def from_behind(value, axis, steps):
    count = lax.axis_size(axis)
    first, last = (max(0, -steps), min(count, count - steps))
    return lax.ppermute(value, axis, [(source, source + steps) for source in range(first, last)])


def layer_norm(values, scaling):
    mean_value = jnp.mean(values, axis=-1, keepdims=True)
    shifted = values - mean_value
    spread = jnp.mean(shifted * shifted, axis=-1, keepdims=True)
    return shifted * lax.rsqrt(spread + EPSILON) * scaling


def running_sums(values):
    places = jnp.arange(values.shape[1], dtype=jnp.int32)
    upto = (places[None, :] <= places[:, None]).astype(jnp.float32)
    return jnp.einsum("im,rmj->rij", upto, values, precision=lax.Precision.HIGHEST)


def block_masks(segments, position, source, block_len):
    offsets = jnp.arange(block_len, dtype=jnp.int32)
    query_pos = position * block_len + offsets
    key_pos = source * block_len + offsets
    query_start = position * block_len
    key_start = jnp.maximum(source, 0) * block_len
    query_seg = lax.dynamic_slice_in_dim(segments, query_start, block_len, 1)
    key_seg = lax.dynamic_slice_in_dim(segments, key_start, block_len, 1)
    same_doc = (query_seg[:, :, None] == key_seg[:, None, :]) & (source >= 0)
    earlier = key_pos[None, :] < query_pos[:, None]
    reached = key_pos[None, :] <= query_pos[:, None]
    return (same_doc & reached[None], same_doc & earlier[None])


def block_logits(queries, key_heads, carried, segments, position, source, offset):
    block_len = queries.shape[1]
    scores = jnp.einsum(
        "rqhd,rkhd->rhqk", queries, key_heads, preferred_element_type=jnp.float32
    ) * (1.0 / math.sqrt(HD))
    attend_mask, select_mask = block_masks(segments, position, source, block_len)
    chosen = jnp.where(select_mask, jax.nn.softplus(scores[:, 0] - offset), 0.0)
    running = running_sums(chosen)
    penalty = carried[:, None, :] + running - chosen
    logits = jnp.where(attend_mask[:, None], scores - penalty[:, None], MASKED)
    return (scores, logits, attend_mask, select_mask, carried + running[:, -1])


def ring_body(tokens, segments, w_qkv, w_out, w_up, w_down, gain_attn, gain_mlp, cotangent):
    low_pieces = (
        w_qkv.astype(jnp.bfloat16),
        w_out.astype(jnp.bfloat16),
        w_up.astype(jnp.bfloat16),
        w_down.astype(jnp.bfloat16),
        gain_attn.astype(jnp.bfloat16),
        gain_mlp.astype(jnp.bfloat16),
    )
    gathered = (
        lax.all_gather(low_pieces[0], ("row", "seq"), axis=0, tiled=True),
        lax.all_gather(low_pieces[1], ("row", "seq"), axis=0, tiled=True),
        lax.all_gather(low_pieces[2], ("row", "seq"), axis=0, tiled=True),
        lax.all_gather(low_pieces[3], ("row", "seq"), axis=0, tiled=True),
        lax.all_gather(low_pieces[4], ("row", "seq"), axis=0, tiled=True),
        lax.all_gather(low_pieces[5], ("row", "seq"), axis=0, tiled=True),
    )
    qkv_full, out_full, up_full, down_full, attn_scale, mlp_scale = gathered
    row_count, block_len, features = tokens.shape
    token_count = row_count * block_len
    position = lax.axis_index("seq")
    sections = lax.axis_size("seq")
    offset = math.log(ROW_LEN / 2.0) + 0.5
    inputs = tokens.astype(jnp.float32).reshape(token_count, features)
    normed, attn_norm_back = jax.vjp(layer_norm, inputs, attn_scale.astype(jnp.float32))
    normed_low = normed.astype(jnp.bfloat16)
    packed = jnp.dot(normed_low, qkv_full, preferred_element_type=jnp.float32).astype(jnp.bfloat16)
    packed = packed.reshape(row_count, block_len, 3 * features)
    queries = packed[:, :, :features].reshape(row_count, block_len, H, HD)
    key_value = packed[:, :, features:]
    carried = jnp.zeros((row_count, block_len), jnp.float32)
    running_max = jnp.full((row_count, H, block_len), MASKED, jnp.float32)
    running_sum = jnp.zeros((row_count, H, block_len), jnp.float32)
    accumulated = jnp.zeros((row_count, block_len, H, HD), jnp.float32)
    kept_pairs = []
    kept_sums = []
    for section in range(sections):
        source = position - section
        key_heads = key_value[:, :, :features].reshape(row_count, block_len, H, HD)
        value_heads = key_value[:, :, features:].reshape(row_count, block_len, H, HD)
        scores, logits, attend_mask, select_mask, passed = block_logits(
            queries, key_heads, carried, segments, position, source, offset
        )
        kept_pairs.append(key_value)
        kept_sums.append(carried)
        new_max = jnp.maximum(running_max, jnp.max(logits, axis=-1))
        rescale = jnp.exp(running_max - new_max)
        exp_scores = jnp.where(attend_mask[:, None], jnp.exp(logits - new_max[..., None]), 0.0)
        running_sum = running_sum * rescale + jnp.sum(exp_scores, axis=-1)
        accumulated = accumulated * jnp.transpose(rescale, (0, 2, 1))[..., None] + jnp.einsum(
            "rhqk,rkhd->rqhd",
            exp_scores.astype(jnp.bfloat16),
            value_heads,
            preferred_element_type=jnp.float32,
        )
        running_max = new_max
        if section + 1 < sections:
            key_value = from_behind(key_value, "seq", 1)
            carried = from_behind(passed, "seq", 1)
    log_norm = running_max + jnp.log(running_sum)
    attn_heads = accumulated / jnp.transpose(running_sum, (0, 2, 1))[..., None]
    mixed_low = attn_heads.reshape(token_count, features).astype(jnp.bfloat16)
    branch = jnp.dot(mixed_low, out_full, preferred_element_type=jnp.float32)
    middle = inputs + branch
    normed_mlp, mlp_norm_back = jax.vjp(layer_norm, middle, mlp_scale.astype(jnp.float32))
    normed_mlp_low = normed_mlp.astype(jnp.bfloat16)
    hidden = jnp.dot(normed_mlp_low, up_full, preferred_element_type=jnp.float32)
    active, gelu_back = jax.vjp(partial(jax.nn.gelu, approximate=False), hidden)
    active_low = active.astype(jnp.bfloat16)
    output = (middle + jnp.dot(active_low, down_full, preferred_element_type=jnp.float32)).astype(
        jnp.bfloat16
    )
    output = output.reshape(row_count, block_len, features)
    upstream = cotangent.reshape(token_count, features)
    grad_down = jnp.dot(active_low.T, upstream, preferred_element_type=jnp.float32)
    d_active = jnp.dot(upstream, down_full.T, preferred_element_type=jnp.float32)
    d_hidden = gelu_back(d_active)[0].astype(jnp.bfloat16)
    grad_up = jnp.dot(normed_mlp_low.T, d_hidden, preferred_element_type=jnp.float32)
    d_normed_mlp = jnp.dot(d_hidden, up_full.T, preferred_element_type=jnp.float32)
    d_middle_part, grad_mlp_gain = mlp_norm_back(d_normed_mlp)
    d_middle = upstream.astype(jnp.float32) + d_middle_part
    d_branch = d_middle.astype(jnp.bfloat16)
    grad_out = jnp.dot(mixed_low.T, d_branch, preferred_element_type=jnp.float32)
    d_mixed = jnp.dot(d_branch, out_full.T, preferred_element_type=jnp.float32).astype(jnp.bfloat16)
    d_mixed = d_mixed.reshape(row_count, block_len, H, HD)
    correction = jnp.transpose(
        jnp.sum(d_mixed.astype(jnp.float32) * attn_heads, axis=-1), (0, 2, 1)
    )
    score_scale = 1.0 / math.sqrt(HD)
    grads_pair = jnp.zeros((row_count, block_len, 2 * features), jnp.float32)
    grads_column = jnp.zeros((row_count, block_len), jnp.float32)
    grad_query = jnp.zeros((row_count, block_len, H, HD), jnp.float32)
    for section in reversed(range(sections)):
        source = position - section
        key_value = kept_pairs[section]
        key_heads = key_value[:, :, :features].reshape(row_count, block_len, H, HD)
        value_heads = key_value[:, :, features:].reshape(row_count, block_len, H, HD)
        scores, logits, attend_mask, select_mask, unused = block_logits(
            queries, key_heads, kept_sums[section], segments, position, source, offset
        )
        attention = jnp.where(attend_mask[:, None], jnp.exp(logits - log_norm[..., None]), 0.0)
        attention_low = attention.astype(jnp.bfloat16)
        grad_values = jnp.einsum(
            "rhqk,rqhd->rkhd", attention_low, d_mixed, preferred_element_type=jnp.float32
        )
        grad_attention = jnp.einsum(
            "rqhd,rkhd->rhqk", d_mixed, value_heads, preferred_element_type=jnp.float32
        )
        grad_logits = attention * (grad_attention - correction[..., None])
        summed = jnp.sum(grad_logits, axis=1)
        column = jnp.sum(summed, axis=1)
        running = running_sums(summed)
        grad_chosen = jnp.where(
            select_mask, running - column[:, None, :] - grads_column[:, None, :], 0.0
        )
        grad_scores = grad_logits.at[:, 0].add(grad_chosen * jax.nn.sigmoid(scores[:, 0] - offset))
        grad_scores = grad_scores.astype(jnp.bfloat16)
        grad_query = (
            grad_query
            + jnp.einsum(
                "rhqk,rkhd->rqhd", grad_scores, key_heads, preferred_element_type=jnp.float32
            )
            * score_scale
        )
        grad_keys = (
            jnp.einsum("rhqk,rqhd->rkhd", grad_scores, queries, preferred_element_type=jnp.float32)
            * score_scale
        )
        grads_pair = grads_pair + jnp.concatenate(
            [
                grad_keys.reshape(row_count, block_len, features),
                grad_values.reshape(row_count, block_len, features),
            ],
            axis=-1,
        )
        grads_column = grads_column + column
        if section > 0:
            grads_pair, grads_column = (
                from_behind(grads_pair.astype(jnp.bfloat16), "seq", -1).astype(grads_pair.dtype),
                from_behind(grads_column.astype(jnp.bfloat16), "seq", -1).astype(
                    grads_column.dtype
                ),
            )
    d_packed = jnp.concatenate(
        [grad_query.reshape(token_count, features), grads_pair.reshape(token_count, 2 * features)],
        axis=-1,
    )
    d_packed = d_packed.astype(jnp.bfloat16)
    grad_qkv = jnp.dot(normed_low.T, d_packed, preferred_element_type=jnp.float32)
    d_normed = jnp.dot(d_packed, qkv_full.T, preferred_element_type=jnp.float32)
    d_inputs_part, grad_attn_gain = attn_norm_back(d_normed)
    d_tokens = (d_middle + d_inputs_part).reshape(row_count, block_len, features)
    gradients = (grad_qkv, grad_out, grad_up, grad_down, grad_attn_gain, grad_mlp_gain)
    reduced = (
        lax.psum_scatter(gradients[0], ("row", "seq"), scatter_dimension=0, tiled=True),
        lax.psum_scatter(gradients[1], ("row", "seq"), scatter_dimension=0, tiled=True),
        lax.psum_scatter(gradients[2], ("row", "seq"), scatter_dimension=0, tiled=True),
        lax.psum_scatter(gradients[3], ("row", "seq"), scatter_dimension=0, tiled=True),
        lax.psum_scatter(gradients[4], ("row", "seq"), scatter_dimension=0, tiled=True),
        lax.psum_scatter(gradients[5], ("row", "seq"), scatter_dimension=0, tiled=True),
    )
    return (
        output,
        d_tokens,
        reduced[0],
        reduced[1],
        reduced[2],
        reduced[3],
        reduced[4],
        reduced[5],
    )


def body(tokens, *rest):
    rows = lax.axis_size("row")
    if lax.axis_size("seq") == 2 and tokens.shape[0] == 2 and rows >= 4 and rows & (rows - 1) == 0:
        return row_body(tokens, *rest)
    return ring_body(tokens, *rest)


def solution(mesh):
    placed = (
        P("row", "seq", None),
        P("row", None),
        P(("row", "seq"), None),
        P(("row", "seq"), None),
        P(("row", "seq"), None),
        P(("row", "seq"), None),
        P(("row", "seq")),
        P(("row", "seq")),
        P("row", "seq", None),
    )
    return jax.shard_map(
        body,
        mesh=mesh,
        in_specs=placed,
        out_specs=(
            P("row", "seq", None),
            P("row", "seq", None),
            P(("row", "seq"), None),
            P(("row", "seq"), None),
            P(("row", "seq"), None),
            P(("row", "seq"), None),
            P(("row", "seq")),
            P(("row", "seq")),
        ),
        check_vma=False,
    )
```
